32 devices in a mesh: tower: 2 (over x), dp: 16 (over z, y, core).
Axes of the slice: x: 2, y: 2, z: 4, core: 2. Of those that a mesh axis runs over, the one named last changes fastest.
Arguments:
- tokens: bfloat16 [2, 32, 512, 768], P('tower', 'dp'), may hold values from -6 to 6
- group_id: int32 [32], P('dp'), may hold values from 0 to 1
- caption_len: int32 [32], P('dp'), may hold values from 128 to 512
- cls_row: bfloat16 [768], replicated, may hold values from -6 to 6
- norm_gains: bfloat16 [2, 2, 768], P('tower'), may hold values from 0.099609375 to 1.8984375
- shifts: bfloat16 [2, 2, 768], P('tower'), may hold values from -3 to 3
- bias_model: bfloat16 [2, 5, 768], P('tower'), may hold values from -3 to 3
- bias_hidden: bfloat16 [2, 3072], P('tower'), may hold values from -3 to 3
- w_qkv: bfloat16 [2, 768, 2304], P('tower'), may hold values from -0.21875 to 0.21875
- w_out: bfloat16 [2, 768, 768], P('tower'), may hold values from -1.75 to 1.75
- w_up: bfloat16 [2, 768, 3072], P('tower'), may hold values from -0.21875 to 0.21875
- w_down: bfloat16 [2, 3072, 768], P('tower'), may hold values from -0.109375 to 0.109375
- w_proj: bfloat16 [2, 768, 768], P('tower'), may hold values from -0.21875 to 0.21875
- merged_grad: bfloat16 [2, 16, 1025, 768], P('tower', 'dp'), may hold values from -6 to 6
Outputs:
- merged_input: bfloat16 [2, 16, 1025, 768], P('tower', 'dp')
- tokens_grad: bfloat16 [2, 32, 512, 768], P('tower', 'dp')
- grad_cls: float32 [768], replicated
- grad_norm_gains: float32 [2, 2, 768], P('tower', None, 'dp')
- grad_shifts: float32 [2, 2, 768], P('tower', None, 'dp')
- grad_bias_model: float32 [2, 5, 768], P('tower', None, 'dp')
- grad_bias_hidden: float32 [2, 3072], P('tower', 'dp')
- grad_w_qkv: float32 [2, 768, 2304], P('tower', 'dp')
- grad_w_out: float32 [2, 768, 768], P('tower', 'dp')
- grad_w_up: float32 [2, 768, 3072], P('tower', 'dp')
- grad_w_down: float32 [2, 3072, 768], P('tower', 'dp')
- grad_w_proj: float32 [2, 768, 768], P('tower', 'dp')
The draws below stay inside these ranges and needn't reach their ends.
Inputs may be any that keep to these rules, and one draw needn't show every extreme that they name: `group_id`: 1 selects 325 image rows, 0 selects 197.
All inputs are finite; a program needn't handle non-finite values.
Results may differ from the reference program's by a relative error of at most 0.012.
The reference program's roundings to bfloat16 on the way count: a program that leaves them out, or rounds other values in their place, can miss the bound.
Values may be sent and summed in bfloat16 or wider, within the bound.
A program may use at most 192 MiB of HBM per device.

```python
from functools import partial
import jax
import jax.numpy as jnp
from jax import lax

D = 768
HEADS = 12
HEAD_DIM = 64
FF = 3072
SEQ = 512
IMG_SMALL = 197
IMG_LARGE = 325
PAIRS_DEV = 2
PAIRS = 32
ROWS_MM = 1025
N_DP = 16


def draw_caption_len(key, part):
    lengths = jax.random.randint(key, (PAIRS,), SEQ // 4, SEQ + 1)
    lengths = lengths.at[0].set(SEQ)
    return lengths.at[1].set(SEQ // 4).astype(jnp.int32)


def with_ends(values, own_key, least, largest):
    dims = values.shape
    spot = [jax.random.randint(jax.random.fold_in(own_key, axis), (), 0, dims[axis]) for axis in range(len(dims))]
    values = values.at[tuple(spot)].set(least)
    longest = dims.index(max(dims))
    spot[longest] = (spot[longest] + 1) % dims[longest]
    return values.at[tuple(spot)].set(largest)


def with_spikes(values, key, source, target, parts, factor):
    owner, partner = [(jnp.arange(values.shape[dim]) // (values.shape[dim] // parts)).reshape([-1 if axis == dim else 1 for axis in range(values.ndim)]) for dim in (source, target)]
    chosen = jax.random.permutation(key, parts)[partner]
    strong = (owner == chosen) | (owner == (partner + parts // 2) % parts)
    return jnp.where(strong, factor * values, values)


def block_levels(own_key, extent, split, low, top_value):
    gain = 1.0
    for dim, shards_of in split:
        draws = jax.random.uniform(jax.random.fold_in(jax.random.fold_in(own_key, 6), dim), (shards_of,), jnp.float32, low / len(split), top_value / len(split))
        gain = gain * jnp.repeat(jnp.exp(draws), extent[dim] // shards_of).reshape((-1,) + (1,) * (len(extent) - 1 - dim))
    return gain


def normal_values(rng, shape, scale, reach, shards=(), kind=jnp.bfloat16):
    entries = jax.random.normal(rng, shape, jnp.float32) * scale
    if len(shards) > 0:
        entries = block_levels(rng, shape, shards, -0.22, 0.18) * entries
    return jnp.clip(entries, min=-reach, max=reach).astype(kind)


def noise_with(key, dims, scale, limit, shards, heavy, kind=jnp.bfloat16):
    entries = scale * jax.random.normal(key, dims, jnp.float32)
    if shards:
        entries = entries * block_levels(key, dims, shards, -0.22, 0.18)
    return jnp.clip(with_spikes(entries, jax.random.fold_in(key, 3), *heavy), -limit, limit).astype(kind)


def setup_inputs(seed: int = 0) -> dict:
    splits = jax.random.split(jax.random.key(seed), 15)
    tokens = noise_with(splits[0], (2, PAIRS, SEQ, D), 1.0, 6.0, ((0, 2), (1, 16)), (1, 3, 16, 2.0))
    group_id = with_ends(jax.random.randint(splits[1], (PAIRS,), 0, 2), jax.random.fold_in(splits[1], 1), 0, 1).astype(jnp.int32)
    caption_len = draw_caption_len(jax.random.fold_in(splits[14], 71), 0)
    cls_row = normal_values(splits[3], (D,), 1.0, 6.0)
    norm_gains = jnp.clip(1.0 + 0.18 * jax.random.normal(splits[4], (2, 2, D), jnp.float32), 0.099609375, 1.8984375).astype(jnp.bfloat16)
    shifts = normal_values(splits[5], (2, 2, D), 0.5, 3.0, ((0, 2),))
    bias_model = normal_values(splits[6], (2, 5, D), 0.5, 3.0, ((0, 2),))
    bias_hidden = normal_values(splits[7], (2, FF), 0.5, 3.0, ((0, 2),))
    w_qkv = normal_values(splits[8], (2, D, 3 * D), D ** -0.5, 0.21875, ((0, 2),))
    w_out = normal_values(splits[9], (2, D, D), (D // 64) ** -0.5, 1.75, ((0, 2),))
    w_up = normal_values(splits[10], (2, D, FF), D ** -0.5, 0.21875, ((0, 2),))
    w_down = normal_values(splits[11], (2, FF, D), FF ** -0.5, 0.109375, ((0, 2),))
    w_proj = normal_values(splits[12], (2, D, D), D ** -0.5, 0.21875, ((0, 2),))
    merged_grad = noise_with(splits[13], (2, PAIRS // 2, ROWS_MM, D), 1.0, 6.0, ((0, 2), (1, 16)), (1, 3, 16, 2.0))
    return {"tokens": tokens, "group_id": group_id, "caption_len": caption_len, "cls_row": cls_row, "norm_gains": norm_gains, "shifts": shifts, "bias_model": bias_model, "bias_hidden": bias_hidden, "w_qkv": w_qkv, "w_out": w_out, "w_up": w_up, "w_down": w_down, "w_proj": w_proj, "merged_grad": merged_grad}


@jax.custom_vjp
def low(v):
    return lax.optimization_barrier(v.astype(jnp.bfloat16)).astype(jnp.float32)

@jax.custom_vjp
def low_back(v):
    return v

def low_keep(v):
    return (low(v), None)

def low_pass(kept, grad):
    return (grad,)

def back_keep(v):
    return (v, None)

def back_low(kept, grad):
    return (low(grad),)
low.defvjp(low_keep, low_pass)
low_back.defvjp(back_keep, back_low)
norm_eps = 1e-06
masked_score = -1e+30

def matmul(left, right):
    return jnp.dot(left, right, precision=lax.Precision.HIGHEST, preferred_element_type=jnp.float32)

def layer_norm(values, norm_gain, norm_shift):
    average = lax.optimization_barrier(jnp.mean(values, -1, keepdims=True))
    centred = values - average
    spread = lax.optimization_barrier(jnp.mean(centred * centred, -1, keepdims=True))
    return centred * lax.rsqrt(spread + norm_eps) * norm_gain + norm_shift

def one_sequence(params, inputs, key_ok):
    gains_here, shifts_here, biases, up_bias, qkv_mat, out_mat, up_mat, down_mat, proj_mat = params
    normed_one = low(layer_norm(inputs, gains_here[0], shifts_here[0]))
    joined = low_back(matmul(normed_one, qkv_mat))
    queries = low(joined[:, :D] + biases[0])
    keys_low = low(joined[:, D:2 * D])
    values_low = low(joined[:, 2 * D:] + biases[1])
    q_heads = queries.reshape(SEQ, HEADS, HEAD_DIM)
    k_heads = keys_low.reshape(SEQ, HEADS, HEAD_DIM)
    v_heads = values_low.reshape(SEQ, HEADS, HEAD_DIM)
    scores = low_back(jnp.einsum('qhd,khd->hqk', q_heads, k_heads, precision=lax.Precision.HIGHEST)) * HEAD_DIM ** (-0.5)
    scores = jnp.where(key_ok[None, None, :], scores, masked_score)
    probs_low = low(jax.nn.softmax(scores, axis=-1))
    mixed_out = jnp.einsum('hqk,khd->qhd', probs_low, v_heads, precision=lax.Precision.HIGHEST).reshape(SEQ, D)
    mixed_out = low(low_back(mixed_out))
    resid_one = inputs + low_back(matmul(mixed_out, out_mat)) + biases[2]
    normed_two = low(layer_norm(resid_one, gains_here[1], shifts_here[1]))
    upper = low_back(matmul(normed_two, up_mat)) + up_bias
    acted = low(jax.nn.gelu(upper, approximate=False))
    resid_two = resid_one + low_back(matmul(acted, down_mat)) + biases[3]
    projected = low_back(matmul(low(resid_two), proj_mat)) + biases[4]
    return projected * key_ok[:, None].astype(jnp.float32)

def run_tower(tower_params, inputs_all, mask_all):
    step_fn = jax.checkpoint(one_sequence)

    def apply_one(packed):
        return step_fn(tower_params, packed[0], packed[1])
    return lax.map(apply_one, (inputs_all, mask_all))

def arrange(outputs):
    shaped = outputs.reshape(N_DP, 2, PAIRS_DEV // 2, SEQ, D)
    return shaped.transpose(1, 0, 2, 3, 4).reshape(2, PAIRS // 2, SEQ, D)

def forward(cls_row, norm_gains, shifts, bias_model, bias_hidden, w_qkv, w_out, w_up, w_down, w_proj, tokens, lengths_both):
    positions = jnp.arange(SEQ, dtype=jnp.int32)
    halves = []
    for tower_side in range(2):
        params = tuple((member[tower_side] for member in (norm_gains, shifts, bias_model, bias_hidden, w_qkv, w_out, w_up, w_down, w_proj)))
        key_mask = positions[None, :] < lengths_both[tower_side][:, None]
        halves.append(arrange(run_tower(params, tokens[tower_side], key_mask)))
    cls_block = jnp.broadcast_to(cls_row.reshape(1, 1, 1, D), (2, PAIRS // 2, 1, D))
    return jnp.concatenate([cls_block, halves[0], halves[1]], axis=2)

def reference(tokens, group_id, caption_len, cls_row, norm_gains, shifts, bias_model, bias_hidden, w_qkv, w_out, w_up, w_down, w_proj, merged_grad):
    image_len = jnp.where(group_id == 1, IMG_LARGE, IMG_SMALL).astype(jnp.int32)
    lengths_both = (image_len, caption_len.astype(jnp.int32))
    float_args = tuple((member.astype(jnp.float32) for member in (cls_row, norm_gains, shifts, bias_model, bias_hidden, w_qkv, w_out, w_up, w_down, w_proj, tokens)))
    merged_input, pullback = jax.vjp(partial(forward, lengths_both=lengths_both), *float_args)
    gradients = pullback(merged_grad.astype(jnp.float32))
    return (merged_input.astype(jnp.bfloat16), gradients[10].astype(jnp.bfloat16), gradients[0], gradients[1], gradients[2], gradients[3], gradients[4], gradients[5], gradients[6], gradients[7], gradients[8], gradients[9])
```

```python
from functools import partial

import jax
import jax.numpy as jnp
from jax import lax
from jax.experimental import pallas as pl
from jax.experimental.pallas import tpu as pltpu
from jax.sharding import PartitionSpec as P

HEADS = 12
HEAD_DIM = 64
IMG_SMALL = 197
IMG_LARGE = 325
LANES = 128
BLOCKS = HEADS * HEAD_DIM // LANES

norm_eps = 1e-06
masked_score = -1e30
F32 = jnp.float32
BF16 = jnp.bfloat16
MIB = 1 << 20
SHARD = 48
QKV_Z_FIRST = True

ERF_P = 0.35
ERF_C = (0.1940220507, 0.238547805, -0.01775629821, 0.7010871662, -0.6969258034, 0.7808052856, -0.1997802124)


def nn(left, right):
    return jnp.dot(left, right, preferred_element_type=F32)


def nt(left, right):
    return lax.dot_general(left, right, (((1,), (1,)), ((), ())), preferred_element_type=F32)


def tn(left, right):
    return lax.dot_general(left, right, (((0,), (0,)), ((), ())), preferred_element_type=F32)


def params(vmem=48, semantics=None):
    return pltpu.CompilerParams(vmem_limit_bytes=vmem * MIB, dimension_semantics=semantics)


def cost(flops, nbytes, trans=0):
    return pl.CostEstimate(flops=int(flops), bytes_accessed=int(nbytes), transcendentals=int(trans))


def whole(shape):
    return pl.BlockSpec(shape, lambda *_: (0,) * len(shape), pipeline_mode=pl.Buffered(1))


def rows(tile, width):
    return pl.BlockSpec((tile, width), lambda i, *_: (i, 0))


def norm_stats(x):
    mean = jnp.mean(x, -1, keepdims=True)
    centred = x - mean
    spread = jnp.mean(centred * centred, -1, keepdims=True)
    scale = lax.rsqrt(spread + norm_eps)
    return centred * scale, scale


def norm_back(grad, hat, scale, gain):
    d_hat = grad * gain
    first = jnp.mean(d_hat, -1, keepdims=True)
    second = jnp.mean(d_hat * hat, -1, keepdims=True)
    return scale * (d_hat - first - hat * second)


def gelu_and_slope(u):
    bell = jnp.exp(-0.5 * u * u)
    t = 1.0 / (1.0 + (ERF_P * 0.5**0.5) * jnp.abs(u))
    poly = jnp.full_like(u, 0.5 * ERF_C[-1])
    for c in ERF_C[-2::-1]:
        poly = poly * t + 0.5 * c
    tail = poly * t * bell
    phi = jnp.where(u >= 0, 1.0 - tail, tail)
    slope = phi + u * bell * 0.3989422804014327
    return u * phi, slope


def slot_of(chunk, z_first):
    z_hi, z_lo, y, core = chunk // 8, chunk // 4 % 2, chunk // 2 % 2, chunk % 2
    second, third = (z_lo, y) if z_first else (y, z_lo)
    return ((core * 2 + second) * 2 + third) * 2 + z_hi


def put_slabs(ref, lead, value, z_first):
    turned = value.T
    for chunk in range(16):
        ref[(*lead, slot_of(chunk, z_first))] = turned[chunk * SHARD : (chunk + 1) * SHARD]


def add_sum(ref, index, value, first):
    ref[index : index + 1, :] = jnp.where(first, 0.0, ref[index : index + 1, :]) + jnp.sum(value, 0, keepdims=True)


def qkv_kernel(x_ref, gain_ref, shift_ref, bias_ref, w_ref, h_ref, out_ref):
    width = x_ref.shape[1]
    hat, _ = norm_stats(x_ref[...].astype(F32))
    h = (hat * gain_ref[0:1].astype(F32) + shift_ref[0:1].astype(F32)).astype(BF16)
    put_slabs(h_ref, (), h, QKV_Z_FIRST)
    q = nn(h, w_ref[:, :width]) + bias_ref[0:1].astype(F32)
    out_ref[:, :width] = q.astype(BF16) * BF16(HEAD_DIM**-0.5)
    out_ref[:, width : 2 * width] = nn(h, w_ref[:, width : 2 * width]).astype(BF16)
    v = nn(h, w_ref[:, 2 * width :]) + bias_ref[1:2].astype(F32)
    out_ref[:, 2 * width :] = v.astype(BF16)


def run_qkv(x, gains, shifts, biases, w, tile=256):
    count, width = x.shape
    return pl.pallas_call(
        qkv_kernel,
        grid=(count // tile,),
        in_specs=[rows(tile, width), whole(gains.shape), whole(shifts.shape), whole(biases.shape), whole(w.shape)],
        out_specs=[pl.BlockSpec((16, SHARD, tile), lambda i: (0, 0, i)), rows(tile, 3 * width)],
        out_shape=[
            jax.ShapeDtypeStruct((16, SHARD, count), BF16),
            jax.ShapeDtypeStruct((count, 3 * width), BF16),
        ],
        compiler_params=params(),
        cost_estimate=cost(6 * count * width * width, 2 * (count * width * 5 + 3 * width * width)),
        name="qkv",
    )(x, gains, shifts, biases, w)


def head_lanes(head, block):
    lane = lax.broadcasted_iota(jnp.int32, (1, LANES), 1)
    keep = (lane < HEAD_DIM) if head == 0 else (lane >= HEAD_DIM)
    return jnp.where(keep, block, jnp.zeros_like(block))


def attend_kernel(len_ref, q_ref, k_ref, v_ref, a_ref, l_ref):
    seq = q_ref.shape[0]
    valid = lax.broadcasted_iota(jnp.int32, (seq, 1), 0) < len_ref[pl.program_id(0)]
    q = q_ref[...]
    k = k_ref[...]
    v_t = v_ref[...].T
    parts = []
    for head in range(2):
        scores = jnp.where(valid, nt(k, head_lanes(head, q)), masked_score)
        largest = jnp.max(scores, 0, keepdims=True)
        weights = jnp.exp(scores - largest)
        total = jnp.sum(weights, 0, keepdims=True)
        mixed = nn(v_t[head * HEAD_DIM : (head + 1) * HEAD_DIM], weights.astype(BF16))
        parts.append((mixed * (1.0 / total)).astype(BF16))
        l_ref[0, 0, head : head + 1, :] = largest + jnp.log(total)
    a_ref[...] = jnp.concatenate(parts, 0).T


def column(seq, shift):
    return pl.BlockSpec((seq, LANES), lambda p, b, *_: (p, b + shift))


def run_attend(lengths, qkv, seq):
    count = qkv.shape[0]
    width = qkv.shape[1] // 3
    pairs = count // seq
    return pl.pallas_call(
        attend_kernel,
        grid_spec=pltpu.PrefetchScalarGridSpec(
            num_scalar_prefetch=1,
            grid=(pairs, BLOCKS),
            in_specs=[column(seq, 0), column(seq, BLOCKS), column(seq, 2 * BLOCKS)],
            out_specs=[column(seq, 0), pl.BlockSpec((1, 1, 2, seq), lambda p, b, *_: (p, b, 0, 0))],
        ),
        out_shape=[
            jax.ShapeDtypeStruct((count, width), BF16),
            jax.ShapeDtypeStruct((pairs, BLOCKS, 2, seq), F32),
        ],
        compiler_params=params(),
        cost_estimate=cost(16 * pairs * HEADS * seq * seq * HEAD_DIM, 8 * count * width, pairs * HEADS * seq * seq),
        name="attend",
    )(lengths, qkv, qkv, qkv)


def attend_back_kernel(len_ref, q_ref, k_ref, v_ref, a_ref, d_ref, l_ref, dq_ref, dk_ref, dv_ref, sq_ref, sv_ref):
    seq = q_ref.shape[0]
    valid = lax.broadcasted_iota(jnp.int32, (seq, 1), 0) < len_ref[pl.program_id(0)]
    q = q_ref[...]
    k = k_ref[...]
    v = v_ref[...]
    d = d_ref[...]
    k_t = k.T
    d_t = d.T
    prod_t = d_t.astype(F32) * a_ref[...].T.astype(F32)
    dq_parts = []
    dk = None
    dv = None
    for head in range(2):
        span = slice(head * HEAD_DIM, (head + 1) * HEAD_DIM)
        q_here = head_lanes(head, q)
        scores = jnp.where(valid, nt(k, q_here), masked_score)
        probs = jnp.exp(scores - l_ref[0, 0, head : head + 1, :])
        row_dot = jnp.sum(prod_t[span], 0, keepdims=True)
        d_probs = nn(head_lanes(head, v), d_t)
        d_scores = (probs * (d_probs - row_dot)).astype(BF16)
        dv_here = nn(probs.astype(BF16), head_lanes(head, d))
        dk_here = nn(d_scores, q_here)
        dq_parts.append(nn(k_t[span], d_scores))
        dk = dk_here if dk is None else dk + dk_here
        dv = dv_here if dv is None else dv + dv_here
    dq = jnp.concatenate(dq_parts, 0).T * HEAD_DIM**-0.5
    dq_ref[...] = dq.astype(BF16)
    dk_ref[...] = dk.astype(BF16)
    dv_ref[...] = dv.astype(BF16)
    sq_ref[0] = jnp.sum(dq, 0, keepdims=True)
    sv_ref[0] = jnp.sum(dv, 0, keepdims=True)


def run_attend_back(lengths, qkv, mixed, d_mixed, log_total, seq):
    count = qkv.shape[0]
    width = qkv.shape[1] // 3
    pairs = count // seq
    sums = pl.BlockSpec((1, 1, LANES), lambda p, b, *_: (p, 0, b))
    return pl.pallas_call(
        attend_back_kernel,
        grid_spec=pltpu.PrefetchScalarGridSpec(
            num_scalar_prefetch=1,
            grid=(pairs, BLOCKS),
            in_specs=[
                column(seq, 0),
                column(seq, BLOCKS),
                column(seq, 2 * BLOCKS),
                column(seq, 0),
                column(seq, 0),
                pl.BlockSpec((1, 1, 2, seq), lambda p, b, *_: (p, b, 0, 0)),
            ],
            out_specs=[column(seq, 0)] * 3 + [sums] * 2,
        ),
        out_shape=[jax.ShapeDtypeStruct((count, width), BF16)] * 3
        + [jax.ShapeDtypeStruct((pairs, 1, width), F32)] * 2,
        compiler_params=params(),
        cost_estimate=cost(40 * pairs * HEADS * seq * seq * HEAD_DIM, 16 * count * width, pairs * HEADS * seq * seq),
        name="attend_back",
    )(lengths, qkv, qkv, qkv, mixed, d_mixed, log_total)


def feed_kernel(
    valid_ref, x_ref, a_ref, g_ref, gain_ref, shift_ref, bias_ref, hidden_ref, out_w, up_w, down_w, proj_w,
    x1_ref, left_ref, slope_ref, y_ref, gm_ref, dx2_ref, e2_ref, sum_ref,
):
    width = x_ref.shape[1]
    first = pl.program_id(0) == 0
    valid = valid_ref[...]
    a = a_ref[...]
    put_slabs(left_ref, (6,), a, False)
    x1 = x_ref[...].astype(F32) + nn(a, out_w[...]) + bias_ref[2:3].astype(F32)
    x1_ref[...] = x1
    hat, _ = norm_stats(x1)
    h = (hat * gain_ref[1:2].astype(F32) + shift_ref[1:2].astype(F32)).astype(BF16)
    put_slabs(left_ref, (5,), h, False)
    x2 = x1 + bias_ref[3:4].astype(F32)
    for part in range(up_w.shape[1] // width):
        span = slice(part * width, (part + 1) * width)
        u = nn(h, up_w[:, span]) + hidden_ref[:, span].astype(F32)
        acted, slope = gelu_and_slope(u)
        z = acted.astype(BF16)
        slope_ref[:, span] = slope.astype(BF16)
        turned = z.T
        for piece in range(16):
            chunk, block = part * 4 + piece // 4, piece % 4
            left_ref[1 + block, slot_of(chunk, False)] = turned[piece * SHARD : (piece + 1) * SHARD]
        x2 = x2 + nn(z, down_w[span, :])
    x2_low = x2.astype(BF16)
    put_slabs(left_ref, (0,), x2_low, False)
    y_ref[...] = ((nn(x2_low, proj_w[...]) + bias_ref[4:5].astype(F32)) * valid).astype(BF16)
    g = g_ref[...].astype(F32) * valid
    g_low = g.astype(BF16)
    gm_ref[...] = g_low
    dx2 = nt(g_low, proj_w[...])
    dx2_ref[...] = dx2
    e2_ref[...] = dx2.astype(BF16)
    add_sum(sum_ref, 0, dx2, first)
    add_sum(sum_ref, 1, g, first)


def run_feed(valid, x, a, g, gains, shifts, biases, hidden, out_w, up_w, down_w, proj_w, tile=256):
    count, width = x.shape
    ff = up_w.shape[1]
    low = jax.ShapeDtypeStruct((count, width), BF16)
    full = jax.ShapeDtypeStruct((count, width), F32)
    weights = (gains, shifts, biases, hidden, out_w, up_w, down_w, proj_w)
    return pl.pallas_call(
        feed_kernel,
        grid=(count // tile,),
        in_specs=[rows(tile, 1)] + [rows(tile, width)] * 3 + [whole(w.shape) for w in weights],
        out_specs=[
            rows(tile, width), pl.BlockSpec((7, 16, SHARD, tile), lambda i: (0, 0, 0, i)), rows(tile, ff),
            rows(tile, width), rows(tile, width), rows(tile, width), rows(tile, width), whole((2, width)),
        ],
        out_shape=[
            full, jax.ShapeDtypeStruct((7, 16, SHARD, count), BF16), jax.ShapeDtypeStruct((count, ff), BF16),
            low, low, full, low, jax.ShapeDtypeStruct((2, width), F32),
        ],
        compiler_params=params(60),
        cost_estimate=cost(2 * count * width * (3 * width + 2 * ff), count * (width * 24 + ff * 6) + 11 * MIB),
        name="feed",
    )(valid, x, a, g, *weights)


def feed_back_kernel(
    e2_ref, dx2_ref, slope_ref, x1_ref, gain_ref, out_w, up_w, down_w,
    eu_ref, dx1_ref, e1_ref, da_ref, hid_ref, sum_ref,
):
    width = e2_ref.shape[1]
    first = pl.program_id(0) == 0
    e2 = e2_ref[...]
    dh = None
    for start in range(0, up_w.shape[1], width):
        span = slice(start, start + width)
        du = nt(e2, down_w[span, :]) * slope_ref[:, span].astype(F32)
        eu = du.astype(BF16)
        eu_ref[:, span] = eu
        hid_ref[:, span] = jnp.where(first, 0.0, hid_ref[:, span]) + jnp.sum(du, 0, keepdims=True)
        part = nt(eu, up_w[:, span])
        dh = part if dh is None else dh + part
    hat, scale = norm_stats(x1_ref[...])
    dx1 = dx2_ref[...] + norm_back(dh, hat, scale, gain_ref[1:2].astype(F32))
    dx1_ref[...] = dx1
    e1 = dx1.astype(BF16)
    e1_ref[...] = e1
    da_ref[...] = nt(e1, out_w[...]).astype(BF16)
    add_sum(sum_ref, 0, dh * hat, first)
    add_sum(sum_ref, 1, dh, first)
    add_sum(sum_ref, 2, dx1, first)


def run_feed_back(e2, dx2, slope, x1, gains, out_w, up_w, down_w, tile=256):
    count, width = x1.shape
    ff = up_w.shape[1]
    low = jax.ShapeDtypeStruct((count, width), BF16)
    return pl.pallas_call(
        feed_back_kernel,
        grid=(count // tile,),
        in_specs=[rows(tile, width), rows(tile, width), rows(tile, ff), rows(tile, width)]
        + [whole(w.shape) for w in (gains, out_w, up_w, down_w)],
        out_specs=[rows(tile, ff), rows(tile, width), rows(tile, width), rows(tile, width), whole((1, ff)), whole((3, width))],
        out_shape=[
            jax.ShapeDtypeStruct((count, ff), BF16),
            jax.ShapeDtypeStruct((count, width), F32),
            low,
            low,
            jax.ShapeDtypeStruct((1, ff), F32),
            jax.ShapeDtypeStruct((3, width), F32),
        ],
        compiler_params=params(60),
        cost_estimate=cost(2 * count * width * (width + 2 * ff), count * (width * 18 + ff * 6) + 10 * MIB),
        name="feed_back",
    )(e2, dx2, slope, x1, gains, out_w, up_w, down_w)


def qkv_back_kernel(dq_ref, dk_ref, dv_ref, dx1_ref, x_ref, gain_ref, w_ref, out_ref, sum_ref):
    width = x_ref.shape[1]
    first = pl.program_id(0) == 0
    dh = nt(dq_ref[...], w_ref[:, :width])
    dh = dh + nt(dk_ref[...], w_ref[:, width : 2 * width])
    dh = dh + nt(dv_ref[...], w_ref[:, 2 * width :])
    hat, scale = norm_stats(x_ref[...].astype(F32))
    out_ref[...] = (dx1_ref[...] + norm_back(dh, hat, scale, gain_ref[0:1].astype(F32))).astype(BF16)
    add_sum(sum_ref, 0, dh * hat, first)
    add_sum(sum_ref, 1, dh, first)


def run_qkv_back(dq, dk, dv, dx1, x, gains, w, tile=256):
    count, width = x.shape
    return pl.pallas_call(
        qkv_back_kernel,
        grid=(count // tile,),
        in_specs=[rows(tile, width)] * 5 + [whole(gains.shape), whole(w.shape)],
        out_specs=[rows(tile, width), whole((2, width))],
        out_shape=[jax.ShapeDtypeStruct((count, width), BF16), jax.ShapeDtypeStruct((2, width), F32)],
        compiler_params=params(),
        cost_estimate=cost(6 * count * width * width, count * width * 14 + 6 * width * width),
        name="qkv_back",
    )(dq, dk, dv, dx1, x, gains, w)


BLOCK_COUNT = 13
RING = 8
QUERIES = 128
VECTORS = 16
MESH = pl.DeviceIdType.MESH


def back_kernel(
    len_ref, log_ref, gain_ref, feed_sum_ref, cls_sum_ref, cls_row_ref,
    left_hbm, h1_hbm, slope_hbm, g_hbm, e2_hbm, dx2_hbm, x1_hbm, a_hbm, qkv_hbm, x_hbm, y_hbm,
    down_hbm, up_hbm, out_hbm, qkv_w_hbm,
    proj_ref, down_ref, up_ref, out_ref, qkv_ref, vec_ref, tokens_hbm, merged_hbm,
    grads, got_1, got_2, got_3, got_4, lefts, pool, eu, down_w, up_w, out_w, dx1, x1_ring, vec, vec_got,
    y_got, merged,
    send_sem, recv_sem, load_sem, left_sem, x1_sem, vec_send, vec_recv, y_sem,
):
    count, width = dx1.shape
    seq = log_ref.shape[3]
    pairs = count // seq
    half = pairs // 2
    parts = eu.shape[0]
    index = lax.axis_index("dp")
    tower = lax.axis_index("tower")
    core, y, z_lo, z_hi = index % 2, index // 2 % 2, index // 4 % 2, index // 8
    by_core = {"dp": index + 1 - 2 * core}
    by_y = {"dp": index + 2 - 4 * y}
    by_lo = {"dp": index + 4 - 8 * z_lo}
    by_hi = {"dp": index + 8 - 16 * z_hi}
    by_x = {"tower": 1 - tower}

    barrier = pltpu.get_barrier_semaphore()
    for partner in (by_core, by_y, by_lo, by_hi, by_x):
        pl.semaphore_signal(barrier, inc=1, device_id=partner, device_id_type=MESH)

    def copy(source, target, sem):
        return pltpu.make_async_copy(source, target, sem)

    def left_copy(number):
        source = left_hbm.at[number] if number < 7 else h1_hbm
        return copy(source, lefts.at[number % 3], left_sem.at[number % 3])

    def slope_copy(part):
        source = slope_hbm.at[:, pl.ds(part * width, width)]
        return copy(source, pool.at[(part + 1) % 2], load_sem.at[part])

    def x1_copy(tile):
        return copy(x1_hbm.at[pl.ds(tile * TILE, TILE)], x1_ring.at[tile % 2], x1_sem.at[tile % 2])

    g_copy = copy(g_hbm, pool.at[0], load_sem.at[4])
    e2_copy = copy(e2_hbm, pool.at[2], load_sem.at[5])
    down_copy = copy(down_hbm, down_w, load_sem.at[6])
    up_copy = copy(up_hbm, up_w, load_sem.at[7])
    out_copy = copy(out_hbm, out_w, load_sem.at[8])
    dx2_copy = copy(dx2_hbm, dx1, load_sem.at[9])
    qkv_copies = [copy(qkv_hbm.at[:, pl.ds(i * width, width)], eu.at[i], load_sem.at[10 + i]) for i in range(3)]
    a_copy = copy(a_hbm, eu.at[3], load_sem.at[13])
    qkv_w_copy = copy(qkv_w_hbm, up_w.at[:, pl.ds(0, 3 * width)], load_sem.at[14])
    x_copy = copy(x_hbm, pool.at[1], load_sem.at[15])
    y_copies = [copy(y_hbm.at[tower, i], eu.at[0, pl.ds(i * seq, seq)], load_sem.at[16]) for i in range(half)]

    for item in (left_copy(0), g_copy, left_copy(1), e2_copy, left_copy(2), slope_copy(0), down_copy, up_copy, out_copy):
        item.start()
    for item in (dx2_copy, x1_copy(0), x1_copy(1)):
        item.start()
    pl.semaphore_wait(barrier, 5)
    y_swap = pltpu.make_async_remote_copy(
        y_hbm.at[1 - tower], y_got, y_sem.at[0], y_sem.at[1], device_id=by_x, device_id_type=MESH
    )
    y_swap.start()

    def bits(block):
        if QKV_Z_FIRST and block >= 10:
            return (by_core, by_lo, by_y, by_hi), (z_lo, y, z_hi)
        return (by_core, by_y, by_lo, by_hi), (y, z_lo, z_hi)

    gots = (got_1, got_2, got_3, got_4)

    def swap_of(block, level):
        partners, (b1, b2, b3) = bits(block)
        here = grads.at[block % RING]
        if level == 0:
            source = here.at[1 - core]
        elif level == 1:
            source = here.at[core, pl.ds((1 - b1) * 4, 4)]
        elif level == 2:
            source = here.at[core, pl.ds(b1 * 4 + (1 - b2) * 2, 2)]
        else:
            source = here.at[core, pl.ds(b1 * 4 + b2 * 2 + 1 - b3, 1)]
        return pltpu.make_async_remote_copy(
            source,
            gots[level].at[block],
            send_sem.at[level, block],
            recv_sem.at[level, block],
            device_id=partners[level],
            device_id_type=MESH,
        )

    def advance(block, level):
        _, (b1, b2, b3) = bits(block)
        slot = block % RING
        swap_of(block, level - 1).wait_recv()
        got = gots[level - 1]
        size = 8 >> level
        bit = (b1, b2, b3)[level - 1]
        base = (0, b1 * 4, b1 * 4 + b2 * 2)[level - 1]
        for other in (1, 0):
            side = (1 - bit) if other else bit

            def add(i, carry, side=side):
                at = side * size + i
                total = grads[slot, core, base + at].astype(F32) + got[block, at].astype(F32)
                grads[slot, core, base + at] = total.astype(BF16)
                return carry

            lax.fori_loop(0, size, add, 0)
            if other:
                swap_of(block, level).start()

    def finish(block):
        _, (b1, b2, b3) = bits(block)
        swap_of(block, 3).wait_recv()
        total = grads[block % RING, core, b1 * 4 + b2 * 2 + b3].astype(F32) + got_4[block, 0].astype(F32)
        if block == 0:
            proj_ref[...] = total
        elif block < 5:
            down_ref[(block - 1) * SHARD : block * SHARD, :] = total
        elif block < 9:
            up_ref[:, (block - 5) * width : (block - 4) * width] = total
        elif block == 9:
            out_ref[...] = total
        else:
            qkv_ref[:, (block - 10) * width : (block - 9) * width] = total
        for level in range(4):
            swap_of(block, level).wait_send()

    done = set()

    def tick(*work):
        for block, level in work:
            assert (block, level) not in done and (level == 1 or (block, level - 1) in done)
            done.add((block, level))
            if level == 4:
                finish(block)
            else:
                advance(block, level)

    def weight_grad(block, number, right):
        assert block < RING or (block - RING, 4) in done
        left = lefts[number % 3].reshape(16 * SHARD, count)
        step = 256

        def columns(i, carry):
            at = pl.ds(pl.multiple_of(i * step, step), step)
            product = nn(left, right(at)).astype(BF16).reshape(2, 8, SHARD, step)
            grads[block % RING, :, :, :, at] = product
            return carry

        lax.fori_loop(0, width // step, columns, 0)
        swap_of(block, 0).start()

    sums = {}

    def add_to(row, value):
        value = jnp.sum(value, 0, keepdims=True)
        if row in sums:
            vec[0, row : row + 1, :] = vec[0, row : row + 1, :] + value
        else:
            sums[row] = True
            vec[0, row : row + 1, :] = value

    vec[0] = jnp.zeros((VECTORS, width), F32)
    vec[0, 3:5, :] = feed_sum_ref[...]
    vec[0, 13:14, :] = cls_sum_ref[...]

    left_copy(0).wait()
    g_copy.wait()
    weight_grad(0, 0, lambda at: pool[0, :, at])
    left_copy(3).start()
    slope_copy(1).start()
    e2_copy.wait()
    for part in range(parts):
        left_copy(1 + part).wait()
        weight_grad(1 + part, 1 + part, lambda at: pool[2, :, at])
        if part < parts - 1 or True:
            left_copy(4 + part).start()
        tick(*TICKS["down", part])

    down_copy.wait()
    for part in range(parts):
        slope_copy(part).wait()

        def tile_du(i, carry, part=part):
            at = pl.ds(pl.multiple_of(i * TILE, TILE), TILE)
            du = nt(pool[2, at, :], down_w[part * width : (part + 1) * width, :])
            du = du * pool[(part + 1) % 2, at, :].astype(F32)
            eu[part, at, :] = du.astype(BF16)
            row = 9 + part
            vec[0, row : row + 1, :] = vec[0, row : row + 1, :] + jnp.sum(du, 0, keepdims=True)
            return carry

        lax.fori_loop(0, count // TILE, tile_du, 0)
        if part + 2 < parts:
            slope_copy(part + 2).start()
        tick(*TICKS["du", part])
    x_copy.start()

    left_copy(5).wait()
    for part in range(parts):
        weight_grad(5 + part, 5, lambda at, part=part: eu[part, :, at])
        tick(*TICKS["up", part])

    up_copy.wait()
    out_copy.wait()
    dx2_copy.wait()
    gain_two = gain_ref[1:2].astype(F32)
    for tile in range(count // TILE):
        x1_copy(tile).wait()
        at = slice(tile * TILE, (tile + 1) * TILE)
        dh = nt(eu[0, at, :], up_w[:, :width])
        for part in range(1, parts):
            dh = dh + nt(eu[part, at, :], up_w[:, part * width : (part + 1) * width])
        hat, scale = norm_stats(x1_ring[tile % 2])
        here = dx1[at, :] + norm_back(dh, hat, scale, gain_two)
        dx1[at, :] = here
        e1 = here.astype(BF16)
        pool[2, at, :] = e1
        pool[0, at, :] = nt(e1, out_w[...]).astype(BF16)
        add_to(6, dh * hat)
        add_to(8, dh)
        add_to(2, here)
        if tile + 2 < count // TILE:
            x1_copy(tile + 2).start()
        tick(*TICKS["mid", tile])
    for item in (*qkv_copies, a_copy, qkv_w_copy):
        item.start()

    left_copy(6).wait()
    weight_grad(9, 6, lambda at: pool[2, :, at])
    tick(*TICKS["out", 0])

    for item in (*qkv_copies, a_copy):
        item.wait()
    per_loop = 3
    for turn in range(pairs * BLOCKS // per_loop):

        def attend(step, carry):
            pair, block = step // BLOCKS, step % BLOCKS
            at = pl.ds(pl.multiple_of(pair * seq, seq), seq)
            lanes = pl.ds(pl.multiple_of(block * LANES, LANES), LANES)
            valid = lax.broadcasted_iota(jnp.int32, (seq, 1), 0) < len_ref[pair]
            q = eu[0, at, lanes]
            k = eu[1, at, lanes]
            v = eu[2, at, lanes]
            d = pool[0, at, lanes]
            logs = log_ref[pair, block]
            k_t = k.T
            d_t = d.T
            prod_t = d_t.astype(F32) * eu[3, at, lanes].T.astype(F32)
            dq_rows = []
            dk = None
            dv = None
            for head in range(2):
                span = slice(head * HEAD_DIM, (head + 1) * HEAD_DIM)
                row_dot = jnp.sum(prod_t[span], 0, keepdims=True)
                v_here = head_lanes(head, v)
                dq_parts = []
                for start in range(0, seq, QUERIES):
                    some = slice(start, start + QUERIES)
                    q_here = head_lanes(head, q[some])
                    scores = jnp.where(valid, nt(k, q_here), masked_score)
                    probs = jnp.exp(scores - logs[head : head + 1, some])
                    d_probs = nn(v_here, d_t[:, some])
                    d_scores = (probs * (d_probs - row_dot[:, some])).astype(BF16)
                    dv_here = nn(probs.astype(BF16), head_lanes(head, d[some]))
                    dk_here = nn(d_scores, q_here)
                    dq_parts.append(nn(k_t[span], d_scores))
                    dk = dk_here if dk is None else dk + dk_here
                    dv = dv_here if dv is None else dv + dv_here
                dq_rows.append(jnp.concatenate(dq_parts, 1))
            dq = jnp.concatenate(dq_rows, 0).T * HEAD_DIM**-0.5
            for number, value in ((0, dq), (1, dk), (2, dv)):
                to = pl.ds(pl.multiple_of(number * count + pair * seq, seq), seq)
                down_w[to, lanes] = value.astype(BF16)
            vec[0, 0:1, lanes] = vec[0, 0:1, lanes] + jnp.sum(dq, 0, keepdims=True)
            vec[0, 1:2, lanes] = vec[0, 1:2, lanes] + jnp.sum(dv, 0, keepdims=True)
            return carry

        lax.fori_loop(turn * per_loop, (turn + 1) * per_loop, attend, 0)
        tick(*TICKS["attend", turn])

    for item in y_copies:
        item.start()
    left_copy(7).wait()
    for part in range(3):
        weight_grad(10 + part, 7, lambda at, part=part: down_w[part * count : (part + 1) * count, at])
        tick(*TICKS["qkv", part])

    x_copy.wait()
    qkv_w_copy.wait()
    gain_one = gain_ref[0:1].astype(F32)
    for tile in range(count // TILE):
        at = slice(tile * TILE, (tile + 1) * TILE)
        dh = None
        for part in range(3):
            dj = down_w[part * count + tile * TILE : part * count + (tile + 1) * TILE, :]
            term = nt(dj, up_w[:, part * width : (part + 1) * width])
            dh = term if dh is None else dh + term
        hat, scale = norm_stats(pool[1, at, :].astype(F32))
        pool[0, at, :] = (dx1[at, :] + norm_back(dh, hat, scale, gain_one)).astype(BF16)
        add_to(5, dh * hat)
        add_to(7, dh)
        tick(*TICKS["first", tile])
    tokens_copy = copy(pool.at[0], tokens_hbm, load_sem.at[17])
    tokens_copy.start()

    def vec_swap(level):
        return pltpu.make_async_remote_copy(
            vec.at[level],
            vec_got.at[level],
            vec_send.at[level],
            vec_recv.at[level],
            device_id=(by_core, by_y, by_lo, by_hi, by_x)[level],
            device_id_type=MESH,
        )

    def vec_add(level):
        vec_swap(level).wait_recv()
        vec[level + 1] = vec[level] + vec_got[level]

    vec_swap(0).start()

    y_swap.wait()
    for item in y_copies:
        item.wait()
    row = lax.broadcasted_iota(jnp.int32, (seq, 1), 0)
    for pair in range(half):
        own = eu[0, pair * seq : (pair + 1) * seq, :].astype(F32)
        got = y_got[pair].astype(F32)
        image = jnp.where(tower == 0, own, got)
        text = jnp.where(tower == 0, got, own)
        before = cls_row_ref[...].astype(F32)
        for number, value in ((0, image), (1, text)):
            moved = jnp.where(row == 0, before, pltpu.roll(value, 1, 0))
            merged[pair, number * seq : (number + 1) * seq, :] = moved.astype(BF16)
            before = value[seq - 1 : seq, :]
        merged[pair, 2 * seq : 2 * seq + 1, :] = before.astype(BF16)
    merged_copy = copy(merged, merged_hbm, load_sem.at[18])
    merged_copy.start()

    for number, work in enumerate(TICKS["tail", 0]):
        tick(work)
        if number < 4:
            vec_add(number)
            vec_swap(number + 1).start()
    vec_swap(4).wait_recv()
    vec_ref[0:13] = vec[4, 0:13]
    vec_ref[13:16] = vec[4, 13:16] + vec_got[4, 13:16]
    for level in range(5):
        vec_swap(level).wait_send()
    tokens_copy.wait()
    merged_copy.wait()
    assert len(done) == 4 * BLOCK_COUNT


TILE = 256
TICKS = {
    ('down', 0): [],
    ('down', 1): [(0, 1)],
    ('down', 2): [(1, 1), (2, 1)],
    ('down', 3): [(3, 1)],
    ('du', 0): [],
    ('du', 1): [(0, 2), (4, 1)],
    ('du', 2): [],
    ('du', 3): [],
    ('up', 0): [(0, 3), (1, 2)],
    ('up', 1): [],
    ('up', 2): [(5, 1), (0, 4)],
    ('up', 3): [(1, 3), (2, 2), (6, 1), (7, 1)],
    ('mid', 0): [(8, 1)],
    ('mid', 1): [(1, 4), (2, 3), (3, 2)],
    ('mid', 2): [],
    ('mid', 3): [(2, 4), (3, 3)],
    ('out', 0): [(4, 2)],
    ('attend', 0): [(3, 4), (4, 3), (5, 2), (9, 1)],
    ('attend', 1): [(4, 4), (5, 3), (6, 2)],
    ('attend', 2): [(5, 4), (6, 3)],
    ('attend', 3): [(6, 4), (7, 2)],
    ('qkv', 0): [(8, 2)],
    ('qkv', 1): [],
    ('qkv', 2): [(7, 3), (10, 1)],
    ('first', 0): [(8, 3), (9, 2), (11, 1), (12, 1)],
    ('first', 1): [(7, 4)],
    ('first', 2): [],
    ('first', 3): [(8, 4), (10, 2)],
    ('tail', 0): [(9, 3), (10, 3), (9, 4), (11, 2), (10, 4), (11, 3), (12, 2), (11, 4), (12, 3), (12, 4)],
}


def run_back(lengths, logs, gains, feed_sums, cls_sum, cls_row, left, h1, slope, g, e2, dx2, x1, a, qkv, x, y, down, up, out, qkv_w):
    count, width = x.shape
    ff = up.shape[1]
    half = y.shape[1]
    seq = y.shape[2]
    shard = jax.ShapeDtypeStruct
    vmem = pl.BlockSpec(memory_space=pltpu.VMEM)
    hbm = pl.BlockSpec(memory_space=pl.ANY)
    return pl.pallas_call(
        back_kernel,
        in_specs=[pl.BlockSpec(memory_space=pltpu.SMEM)] + [vmem] * 5 + [hbm] * 15,
        out_specs=[vmem] * 6 + [hbm] * 2,
        out_shape=[
            shard((SHARD, width), F32),
            shard((4 * SHARD, width), F32),
            shard((SHARD, ff), F32),
            shard((SHARD, width), F32),
            shard((SHARD, 3 * width), F32),
            shard((VECTORS, width), F32),
            shard((count, width), BF16),
            shard((half, 2 * seq + 1, width), BF16),
        ],
        scratch_shapes=[
            pltpu.VMEM((RING, 2, 8, SHARD, width), BF16),
            pltpu.VMEM((BLOCK_COUNT, 8, SHARD, width), BF16),
            pltpu.VMEM((BLOCK_COUNT, 4, SHARD, width), BF16),
            pltpu.VMEM((BLOCK_COUNT, 2, SHARD, width), BF16),
            pltpu.VMEM((BLOCK_COUNT, 1, SHARD, width), BF16),
            pltpu.VMEM((3, 16, SHARD, count), BF16),
            pltpu.VMEM((3, count, width), BF16),
            pltpu.VMEM((ff // width, count, width), BF16),
            pltpu.VMEM((ff, width), BF16),
            pltpu.VMEM((width, ff), BF16),
            pltpu.VMEM((width, width), BF16),
            pltpu.VMEM((count, width), F32),
            pltpu.VMEM((2, TILE, width), F32),
            pltpu.VMEM((5, VECTORS, width), F32),
            pltpu.VMEM((5, VECTORS, width), F32),
            pltpu.VMEM((half, seq, width), BF16),
            pltpu.VMEM((half, 2 * seq + 1, width), BF16),
            pltpu.SemaphoreType.DMA((4, BLOCK_COUNT)),
            pltpu.SemaphoreType.DMA((4, BLOCK_COUNT)),
            pltpu.SemaphoreType.DMA((19,)),
            pltpu.SemaphoreType.DMA((3,)),
            pltpu.SemaphoreType.DMA((2,)),
            pltpu.SemaphoreType.DMA((5,)),
            pltpu.SemaphoreType.DMA((5,)),
            pltpu.SemaphoreType.DMA((2,)),
        ],
        compiler_params=pltpu.CompilerParams(
            collective_id=0, has_side_effects=True, vmem_limit_bytes=63 * MIB
        ),
        cost_estimate=cost(30e9, 60 * MIB),
        name="back",
    )(lengths, logs, gains, feed_sums, cls_sum, cls_row, left, h1, slope, g, e2, dx2, x1, a, qkv, x, y, down, up, out, qkv_w)


def full_grad_kernel(left_ref, *refs):
    start = 0
    for right_ref in refs[:-1]:
        stop = start + right_ref.shape[1]
        refs[-1][:, start:stop] = nn(left_ref[...], right_ref[...])
        start = stop


def run_full_grad(left, *rights):
    height, count = left.shape
    width = sum(right.shape[1] for right in rights)
    tile = 384
    return pl.pallas_call(
        full_grad_kernel,
        grid=(height // tile,),
        in_specs=[rows(tile, count)] + [whole(right.shape) for right in rights],
        out_specs=rows(tile, width),
        out_shape=jax.ShapeDtypeStruct((height, width), F32),
        compiler_params=params(),
        name="full_grad",
    )(left, *rights)


def in_order(slabs, z_first):
    return jnp.stack([slabs[..., slot_of(chunk, z_first), :, :] for chunk in range(16)], -3)


def plain_back(lengths, logs, gains, feed_sums, cls_sum, left, h1, slope, g, e2, dx2, x1, a, qkv, x, y, down_w, up_w, out_w, qkv_w):
    count, width = x.shape
    seq = y.shape[2]
    eu, dx1, e1, da, hidden_sum, mid_sums = run_feed_back(e2, dx2, slope, x1, gains, out_w, up_w, down_w)
    dq, dk, dv, sum_q, sum_v = run_attend_back(lengths, qkv, a, da, logs, seq)
    tokens_grad, first_sums = run_qkv_back(dq, dk, dv, dx1, x, gains, qkv_w)
    turned = in_order(left, False)
    z = turned[1:5].transpose(1, 0, 2, 3).reshape(4 * width, count)
    x2, h2, a_t = (turned[i].reshape(width, count) for i in (0, 5, 6))
    h1 = in_order(h1, QKV_Z_FIRST).reshape(width, count)
    grads = (run_full_grad(x2, g), run_full_grad(z, e2), run_full_grad(h2, eu), run_full_grad(a_t, e1), run_full_grad(h1, dq, dk, dv))
    grads = [lax.psum_scatter(grad, "dp", scatter_dimension=0, tiled=True) for grad in grads]
    vectors = jnp.concatenate(
        [
            jnp.sum(sum_q, 0), jnp.sum(sum_v, 0), mid_sums[2:3], feed_sums, first_sums[0:1], mid_sums[0:1],
            first_sums[1:2], mid_sums[1:2], hidden_sum.reshape(-1, width),
        ],
        axis=0,
    )
    vectors = lax.psum(vectors, "dp")
    cls = lax.psum(cls_sum, ("tower", "dp"))
    y_got = lax.ppermute(take(y, 1 - lax.axis_index("tower")), "tower", [(0, 1), (1, 0)])
    return grads, vectors, cls, tokens_grad, y_got


def take(value, index):
    return lax.dynamic_index_in_dim(value, index, 0, keepdims=False)


def local(
    dp, tokens, group_id, caption_len, cls_row, norm_gains, shifts, bias_model, bias_hidden,
    w_qkv, w_out, w_up, w_down, w_proj, merged_grad,
):
    tower = lax.axis_index("tower")
    index = lax.axis_index("dp")
    pairs, seq, width = tokens.shape[1:]
    half = pairs // 2
    count = pairs * seq
    image_len = jnp.where(group_id == 1, IMG_LARGE, IMG_SMALL)
    lengths = jnp.where(tower == 0, image_len, caption_len).astype(jnp.int32)
    positions = lax.broadcasted_iota(jnp.int32, (pairs, seq), 1)
    valid = (positions < lengths[:, None]).reshape(count, 1).astype(F32)
    gains, shift_rows, biases, hidden = norm_gains[0], shifts[0], bias_model[0], bias_hidden
    qkv_w, out_w, up_w, down_w, proj_w = w_qkv[0], w_out[0], w_up[0], w_down[0], w_proj[0]
    x = tokens[0].reshape(count, width)

    image_grad = merged_grad[0, :, 1 : 1 + seq]
    text_grad = merged_grad[0, :, 1 + seq :]
    g_keep = jnp.where(tower == 0, image_grad, text_grad)
    g_send = jnp.where(tower == 0, text_grad, image_grad)
    g_got = lax.ppermute(g_send, "tower", [(0, 1), (1, 0)])
    cls_sum = jnp.sum(merged_grad[0, :, 0].astype(F32), 0)[None]

    h1, qkv = run_qkv(x, gains, shift_rows, biases, qkv_w)
    mixed, logs = run_attend(lengths, qkv, seq)
    g = jnp.where(tower == 0, jnp.stack([g_keep, g_got]), jnp.stack([g_got, g_keep])).reshape(count, width)
    x1, left, slope, y, g_low, dx2, e2, feed_sums = run_feed(
        valid, x, mixed, g, gains, shift_rows, biases, hidden, out_w, up_w, down_w, proj_w
    )
    y = y.reshape(2, half, seq, width)
    if dp == 16 and half == 1:
        *grads, vectors, tokens_grad, merged_input = run_back(
            lengths, logs, gains, feed_sums, cls_sum, cls_row[None], left, h1, slope, g_low, e2, dx2, x1, mixed, qkv, x, y,
            down_w, up_w, out_w, qkv_w,
        )
        proj, down, up, out, qkv_grad = grads
        cls = vectors[13:14]
    else:
        grads, vectors, cls, tokens_grad, y_got = plain_back(
            lengths, logs, gains, feed_sums, cls_sum, left, h1, slope, g_low, e2, dx2, x1, mixed, qkv, x, y,
            down_w, up_w, out_w, qkv_w,
        )
        proj, down, up, out, qkv_grad = grads
        y_own = take(y, tower)
        cls_block = jnp.broadcast_to(cls_row.reshape(1, 1, width), (half, 1, width))
        image_rows = jnp.where(tower == 0, y_own, y_got)
        text_rows = jnp.where(tower == 0, y_got, y_own)
        merged_input = jnp.concatenate([cls_block, image_rows, text_rows], axis=1)
    mine = lax.dynamic_slice_in_dim(vectors[:9], index * (width // dp), width // dp, 1)
    ff = up_w.shape[1]
    hidden_grad = lax.dynamic_slice_in_dim(vectors[9:13].reshape(ff), index * (ff // dp), ff // dp, 0)
    return (
        merged_input[None], tokens_grad.reshape(tokens.shape), cls.reshape(width), mine[5:7][None], mine[7:9][None],
        mine[0:5][None], hidden_grad[None], qkv_grad[None], out[None], up[None], down[None], proj[None],
    )


def solution(mesh):
    tower = P("tower", None, None)
    in_specs = (
        P("tower", "dp", None, None), P("dp"), P("dp"), P(), tower, tower, tower, P("tower", None),
        tower, tower, tower, tower, tower, P("tower", "dp", None, None),
    )
    spread = P("tower", None, "dp")
    weight = P("tower", "dp", None)
    out_specs = (
        P("tower", "dp", None, None), P("tower", "dp", None, None), P(), spread, spread, spread, P("tower", "dp"),
        weight, weight, weight, weight, weight,
    )
    return jax.shard_map(
        partial(local, mesh.shape["dp"]), mesh=mesh, in_specs=in_specs, out_specs=out_specs, check_vma=False
    )
```

```python
from functools import partial

import jax
import jax.numpy as jnp
from jax import lax
from jax.experimental import pallas as pl
from jax.experimental.pallas import tpu as pltpu
from jax.sharding import PartitionSpec as P

HEADS = 12
HEAD_DIM = 64
IMG_SMALL = 197
IMG_LARGE = 325
LANES = 128
BLOCKS = HEADS * HEAD_DIM // LANES

norm_eps = 1e-06
masked_score = -1e30
F32 = jnp.float32
BF16 = jnp.bfloat16
MIB = 1 << 20
SHARD = 48
QKV_Z_FIRST = True

ERF_P = 0.35
ERF_C = (0.1940220507, 0.238547805, -0.01775629821, 0.7010871662, -0.6969258034, 0.7808052856, -0.1997802124)


def nn(left, right):
    return jnp.dot(left, right, preferred_element_type=F32)


def nt(left, right):
    return lax.dot_general(left, right, (((1,), (1,)), ((), ())), preferred_element_type=F32)


def tn(left, right):
    return lax.dot_general(left, right, (((0,), (0,)), ((), ())), preferred_element_type=F32)


def params(vmem=48, semantics=None):
    return pltpu.CompilerParams(vmem_limit_bytes=vmem * MIB, dimension_semantics=semantics)


def cost(flops, nbytes, trans=0):
    return pl.CostEstimate(flops=int(flops), bytes_accessed=int(nbytes), transcendentals=int(trans))


def whole(shape):
    return pl.BlockSpec(shape, lambda *_: (0,) * len(shape), pipeline_mode=pl.Buffered(1))


def rows(tile, width):
    return pl.BlockSpec((tile, width), lambda i, *_: (i, 0))


def norm_stats(x):
    mean = jnp.mean(x, -1, keepdims=True)
    centred = x - mean
    spread = jnp.mean(centred * centred, -1, keepdims=True)
    scale = lax.rsqrt(spread + norm_eps)
    return centred * scale, scale


def norm_back(grad, hat, scale, gain):
    d_hat = grad * gain
    first = jnp.mean(d_hat, -1, keepdims=True)
    second = jnp.mean(d_hat * hat, -1, keepdims=True)
    return scale * (d_hat - first - hat * second)


def gelu_and_slope(u):
    bell = jnp.exp(-0.5 * u * u)
    t = 1.0 / (1.0 + (ERF_P * 0.5**0.5) * jnp.abs(u))
    poly = jnp.full_like(u, 0.5 * ERF_C[-1])
    for c in ERF_C[-2::-1]:
        poly = poly * t + 0.5 * c
    tail = poly * t * bell
    phi = jnp.where(u >= 0, 1.0 - tail, tail)
    slope = phi + u * bell * 0.3989422804014327
    return u * phi, slope


def slot_of(chunk, z_first):
    z_hi, z_lo, y, core = chunk // 8, chunk // 4 % 2, chunk // 2 % 2, chunk % 2
    second, third = (z_lo, y) if z_first else (y, z_lo)
    return ((core * 2 + second) * 2 + third) * 2 + z_hi


def put_slabs(ref, lead, value, z_first):
    turned = value.T
    for chunk in range(16):
        ref[(*lead, slot_of(chunk, z_first))] = turned[chunk * SHARD : (chunk + 1) * SHARD]


def add_sum(ref, index, value, first):
    ref[index : index + 1, :] = jnp.where(first, 0.0, ref[index : index + 1, :]) + jnp.sum(value, 0, keepdims=True)


def qkv_kernel(x_ref, gain_ref, shift_ref, bias_ref, w_ref, h_ref, out_ref):
    width = x_ref.shape[1]
    hat, _ = norm_stats(x_ref[...].astype(F32))
    h = (hat * gain_ref[0:1].astype(F32) + shift_ref[0:1].astype(F32)).astype(BF16)
    put_slabs(h_ref, (), h, QKV_Z_FIRST)
    q = nn(h, w_ref[:, :width]) + bias_ref[0:1].astype(F32)
    out_ref[:, :width] = q.astype(BF16) * BF16(HEAD_DIM**-0.5)
    out_ref[:, width : 2 * width] = nn(h, w_ref[:, width : 2 * width]).astype(BF16)
    v = nn(h, w_ref[:, 2 * width :]) + bias_ref[1:2].astype(F32)
    out_ref[:, 2 * width :] = v.astype(BF16)


def run_qkv(x, gains, shifts, biases, w, tile=256):
    count, width = x.shape
    return pl.pallas_call(
        qkv_kernel,
        grid=(count // tile,),
        in_specs=[rows(tile, width), whole(gains.shape), whole(shifts.shape), whole(biases.shape), whole(w.shape)],
        out_specs=[pl.BlockSpec((16, SHARD, tile), lambda i: (0, 0, i)), rows(tile, 3 * width)],
        out_shape=[
            jax.ShapeDtypeStruct((16, SHARD, count), BF16),
            jax.ShapeDtypeStruct((count, 3 * width), BF16),
        ],
        compiler_params=params(),
        cost_estimate=cost(6 * count * width * width, 2 * (count * width * 5 + 3 * width * width)),
        name="qkv",
    )(x, gains, shifts, biases, w)


def head_lanes(head, block):
    lane = lax.broadcasted_iota(jnp.int32, (1, LANES), 1)
    keep = (lane < HEAD_DIM) if head == 0 else (lane >= HEAD_DIM)
    return jnp.where(keep, block, jnp.zeros_like(block))


def attend_kernel(len_ref, q_ref, k_ref, v_ref, a_ref, l_ref):
    seq = q_ref.shape[0]
    valid = lax.broadcasted_iota(jnp.int32, (seq, 1), 0) < len_ref[pl.program_id(0)]
    q = q_ref[...]
    k = k_ref[...]
    v_t = v_ref[...].T
    parts = []
    for head in range(2):
        scores = jnp.where(valid, nt(k, head_lanes(head, q)), masked_score)
        largest = jnp.max(scores, 0, keepdims=True)
        weights = jnp.exp(scores - largest)
        total = jnp.sum(weights, 0, keepdims=True)
        mixed = nn(v_t[head * HEAD_DIM : (head + 1) * HEAD_DIM], weights.astype(BF16))
        parts.append((mixed * (1.0 / total)).astype(BF16))
        l_ref[0, 0, head : head + 1, :] = largest + jnp.log(total)
    a_ref[...] = jnp.concatenate(parts, 0).T


def column(seq, shift):
    return pl.BlockSpec((seq, LANES), lambda p, b, *_: (p, b + shift))


def run_attend(lengths, qkv, seq):
    count = qkv.shape[0]
    width = qkv.shape[1] // 3
    pairs = count // seq
    return pl.pallas_call(
        attend_kernel,
        grid_spec=pltpu.PrefetchScalarGridSpec(
            num_scalar_prefetch=1,
            grid=(pairs, BLOCKS),
            in_specs=[column(seq, 0), column(seq, BLOCKS), column(seq, 2 * BLOCKS)],
            out_specs=[column(seq, 0), pl.BlockSpec((1, 1, 2, seq), lambda p, b, *_: (p, b, 0, 0))],
        ),
        out_shape=[
            jax.ShapeDtypeStruct((count, width), BF16),
            jax.ShapeDtypeStruct((pairs, BLOCKS, 2, seq), F32),
        ],
        compiler_params=params(),
        cost_estimate=cost(16 * pairs * HEADS * seq * seq * HEAD_DIM, 8 * count * width, pairs * HEADS * seq * seq),
        name="attend",
    )(lengths, qkv, qkv, qkv)


def attend_back_kernel(len_ref, q_ref, k_ref, v_ref, a_ref, d_ref, l_ref, dq_ref, dk_ref, dv_ref, sq_ref, sv_ref):
    seq = q_ref.shape[0]
    valid = lax.broadcasted_iota(jnp.int32, (seq, 1), 0) < len_ref[pl.program_id(0)]
    q = q_ref[...]
    k = k_ref[...]
    v = v_ref[...]
    d = d_ref[...]
    k_t = k.T
    d_t = d.T
    prod_t = d_t.astype(F32) * a_ref[...].T.astype(F32)
    dq_parts = []
    dk = None
    dv = None
    for head in range(2):
        span = slice(head * HEAD_DIM, (head + 1) * HEAD_DIM)
        q_here = head_lanes(head, q)
        scores = jnp.where(valid, nt(k, q_here), masked_score)
        probs = jnp.exp(scores - l_ref[0, 0, head : head + 1, :])
        row_dot = jnp.sum(prod_t[span], 0, keepdims=True)
        d_probs = nn(head_lanes(head, v), d_t)
        d_scores = (probs * (d_probs - row_dot)).astype(BF16)
        dv_here = nn(probs.astype(BF16), head_lanes(head, d))
        dk_here = nn(d_scores, q_here)
        dq_parts.append(nn(k_t[span], d_scores))
        dk = dk_here if dk is None else dk + dk_here
        dv = dv_here if dv is None else dv + dv_here
    dq = jnp.concatenate(dq_parts, 0).T * HEAD_DIM**-0.5
    dq_ref[...] = dq.astype(BF16)
    dk_ref[...] = dk.astype(BF16)
    dv_ref[...] = dv.astype(BF16)
    sq_ref[0] = jnp.sum(dq, 0, keepdims=True)
    sv_ref[0] = jnp.sum(dv, 0, keepdims=True)


def run_attend_back(lengths, qkv, mixed, d_mixed, log_total, seq):
    count = qkv.shape[0]
    width = qkv.shape[1] // 3
    pairs = count // seq
    sums = pl.BlockSpec((1, 1, LANES), lambda p, b, *_: (p, 0, b))
    return pl.pallas_call(
        attend_back_kernel,
        grid_spec=pltpu.PrefetchScalarGridSpec(
            num_scalar_prefetch=1,
            grid=(pairs, BLOCKS),
            in_specs=[
                column(seq, 0),
                column(seq, BLOCKS),
                column(seq, 2 * BLOCKS),
                column(seq, 0),
                column(seq, 0),
                pl.BlockSpec((1, 1, 2, seq), lambda p, b, *_: (p, b, 0, 0)),
            ],
            out_specs=[column(seq, 0)] * 3 + [sums] * 2,
        ),
        out_shape=[jax.ShapeDtypeStruct((count, width), BF16)] * 3
        + [jax.ShapeDtypeStruct((pairs, 1, width), F32)] * 2,
        compiler_params=params(),
        cost_estimate=cost(40 * pairs * HEADS * seq * seq * HEAD_DIM, 16 * count * width, pairs * HEADS * seq * seq),
        name="attend_back",
    )(lengths, qkv, qkv, qkv, mixed, d_mixed, log_total)


def feed_kernel(
    valid_ref, x_ref, a_ref, g_ref, gain_ref, shift_ref, bias_ref, hidden_ref, out_w, up_w, down_w, proj_w,
    x1_ref, left_ref, slope_ref, y_ref, gm_ref, dx2_ref, e2_ref, sum_ref,
):
    width = x_ref.shape[1]
    first = pl.program_id(0) == 0
    valid = valid_ref[...]
    a = a_ref[...]
    put_slabs(left_ref, (6,), a, False)
    x1 = x_ref[...].astype(F32) + nn(a, out_w[...]) + bias_ref[2:3].astype(F32)
    x1_ref[...] = x1
    hat, _ = norm_stats(x1)
    h = (hat * gain_ref[1:2].astype(F32) + shift_ref[1:2].astype(F32)).astype(BF16)
    put_slabs(left_ref, (5,), h, False)
    x2 = x1 + bias_ref[3:4].astype(F32)
    for part in range(up_w.shape[1] // width):
        span = slice(part * width, (part + 1) * width)
        u = nn(h, up_w[:, span]) + hidden_ref[:, span].astype(F32)
        acted, slope = gelu_and_slope(u)
        z = acted.astype(BF16)
        slope_ref[:, span] = slope.astype(BF16)
        turned = z.T
        for piece in range(16):
            chunk, block = part * 4 + piece // 4, piece % 4
            left_ref[1 + block, slot_of(chunk, False)] = turned[piece * SHARD : (piece + 1) * SHARD]
        x2 = x2 + nn(z, down_w[span, :])
    x2_low = x2.astype(BF16)
    put_slabs(left_ref, (0,), x2_low, False)
    y_ref[...] = ((nn(x2_low, proj_w[...]) + bias_ref[4:5].astype(F32)) * valid).astype(BF16)
    g = g_ref[...].astype(F32) * valid
    g_low = g.astype(BF16)
    gm_ref[...] = g_low
    dx2 = nt(g_low, proj_w[...])
    dx2_ref[...] = dx2
    e2_ref[...] = dx2.astype(BF16)
    add_sum(sum_ref, 0, dx2, first)
    add_sum(sum_ref, 1, g, first)


def run_feed(valid, x, a, g, gains, shifts, biases, hidden, out_w, up_w, down_w, proj_w, tile=256):
    count, width = x.shape
    ff = up_w.shape[1]
    low = jax.ShapeDtypeStruct((count, width), BF16)
    full = jax.ShapeDtypeStruct((count, width), F32)
    weights = (gains, shifts, biases, hidden, out_w, up_w, down_w, proj_w)
    return pl.pallas_call(
        feed_kernel,
        grid=(count // tile,),
        in_specs=[rows(tile, 1)] + [rows(tile, width)] * 3 + [whole(w.shape) for w in weights],
        out_specs=[
            rows(tile, width), pl.BlockSpec((7, 16, SHARD, tile), lambda i: (0, 0, 0, i)), rows(tile, ff),
            rows(tile, width), rows(tile, width), rows(tile, width), rows(tile, width), whole((2, width)),
        ],
        out_shape=[
            full, jax.ShapeDtypeStruct((7, 16, SHARD, count), BF16), jax.ShapeDtypeStruct((count, ff), BF16),
            low, low, full, low, jax.ShapeDtypeStruct((2, width), F32),
        ],
        compiler_params=params(60),
        cost_estimate=cost(2 * count * width * (3 * width + 2 * ff), count * (width * 24 + ff * 6) + 11 * MIB),
        name="feed",
    )(valid, x, a, g, *weights)


def feed_back_kernel(
    e2_ref, dx2_ref, slope_ref, x1_ref, gain_ref, out_w, up_w, down_w,
    eu_ref, dx1_ref, e1_ref, da_ref, hid_ref, sum_ref,
):
    width = e2_ref.shape[1]
    first = pl.program_id(0) == 0
    e2 = e2_ref[...]
    dh = None
    for start in range(0, up_w.shape[1], width):
        span = slice(start, start + width)
        du = nt(e2, down_w[span, :]) * slope_ref[:, span].astype(F32)
        eu = du.astype(BF16)
        eu_ref[:, span] = eu
        hid_ref[:, span] = jnp.where(first, 0.0, hid_ref[:, span]) + jnp.sum(du, 0, keepdims=True)
        part = nt(eu, up_w[:, span])
        dh = part if dh is None else dh + part
    hat, scale = norm_stats(x1_ref[...])
    dx1 = dx2_ref[...] + norm_back(dh, hat, scale, gain_ref[1:2].astype(F32))
    dx1_ref[...] = dx1
    e1 = dx1.astype(BF16)
    e1_ref[...] = e1
    da_ref[...] = nt(e1, out_w[...]).astype(BF16)
    add_sum(sum_ref, 0, dh * hat, first)
    add_sum(sum_ref, 1, dh, first)
    add_sum(sum_ref, 2, dx1, first)


def run_feed_back(e2, dx2, slope, x1, gains, out_w, up_w, down_w, tile=256):
    count, width = x1.shape
    ff = up_w.shape[1]
    low = jax.ShapeDtypeStruct((count, width), BF16)
    return pl.pallas_call(
        feed_back_kernel,
        grid=(count // tile,),
        in_specs=[rows(tile, width), rows(tile, width), rows(tile, ff), rows(tile, width)]
        + [whole(w.shape) for w in (gains, out_w, up_w, down_w)],
        out_specs=[rows(tile, ff), rows(tile, width), rows(tile, width), rows(tile, width), whole((1, ff)), whole((3, width))],
        out_shape=[
            jax.ShapeDtypeStruct((count, ff), BF16),
            jax.ShapeDtypeStruct((count, width), F32),
            low,
            low,
            jax.ShapeDtypeStruct((1, ff), F32),
            jax.ShapeDtypeStruct((3, width), F32),
        ],
        compiler_params=params(60),
        cost_estimate=cost(2 * count * width * (width + 2 * ff), count * (width * 18 + ff * 6) + 10 * MIB),
        name="feed_back",
    )(e2, dx2, slope, x1, gains, out_w, up_w, down_w)


def qkv_back_kernel(dq_ref, dk_ref, dv_ref, dx1_ref, x_ref, gain_ref, w_ref, out_ref, sum_ref):
    width = x_ref.shape[1]
    first = pl.program_id(0) == 0
    dh = nt(dq_ref[...], w_ref[:, :width])
    dh = dh + nt(dk_ref[...], w_ref[:, width : 2 * width])
    dh = dh + nt(dv_ref[...], w_ref[:, 2 * width :])
    hat, scale = norm_stats(x_ref[...].astype(F32))
    out_ref[...] = (dx1_ref[...] + norm_back(dh, hat, scale, gain_ref[0:1].astype(F32))).astype(BF16)
    add_sum(sum_ref, 0, dh * hat, first)
    add_sum(sum_ref, 1, dh, first)


def run_qkv_back(dq, dk, dv, dx1, x, gains, w, tile=256):
    count, width = x.shape
    return pl.pallas_call(
        qkv_back_kernel,
        grid=(count // tile,),
        in_specs=[rows(tile, width)] * 5 + [whole(gains.shape), whole(w.shape)],
        out_specs=[rows(tile, width), whole((2, width))],
        out_shape=[jax.ShapeDtypeStruct((count, width), BF16), jax.ShapeDtypeStruct((2, width), F32)],
        compiler_params=params(),
        cost_estimate=cost(6 * count * width * width, count * width * 14 + 6 * width * width),
        name="qkv_back",
    )(dq, dk, dv, dx1, x, gains, w)


BLOCK_COUNT = 13
RING = 8
CORE_RING = 4
SECOND_RING = 7
QUERIES = 256
VECTORS = 16
TILE = 256
MESH = pl.DeviceIdType.MESH


def one_kernel(
    len_ref, gain_ref, shift_ref, bias_ref, hidden_ref, cls_row_ref,
    x_hbm, g_hbm, qkv_w_hbm, out_hbm, up_hbm, down_hbm, proj_hbm,
    proj_ref, down_ref, up_ref, out_ref, qkv_ref, vec_ref, tokens_hbm, merged_hbm, qkv_hbm, h1_hbm,
    grads, got_1, got_2, got_3, got_4, lefts, pool, eu, down_w, up_w, out_w, proj_w, x1, logs, vec, vec_got,
    y_send, y_got, merged, sums,
    send_sem, recv_sem, load_sem, sum_sem, vec_send, vec_recv, tower_sem, free_sem,
):
    count, width = x1.shape
    pairs, _, _, seq = logs.shape
    half = pairs // 2
    parts = eu.shape[0]
    tiles = count // TILE
    index = lax.axis_index("dp")
    tower = lax.axis_index("tower")
    core, y, z_lo, z_hi = index % 2, index // 2 % 2, index // 4 % 2, index // 8
    by_core = {"dp": index + 1 - 2 * core}
    by_y = {"dp": index + 2 - 4 * y}
    by_lo = {"dp": index + 4 - 8 * z_lo}
    by_hi = {"dp": index + 8 - 16 * z_hi}
    by_x = {"tower": 1 - tower}

    barrier = pltpu.get_barrier_semaphore()
    for partner in (by_core, by_y, by_lo, by_hi, by_x):
        pl.semaphore_signal(barrier, inc=1, device_id=partner, device_id_type=MESH)

    def copy(number, source, target):
        return pltpu.make_async_copy(source, target, load_sem.at[number])

    x_copy = copy(0, x_hbm, pool.at[1])
    qkv_w_copies = [
        copy(1 + i, qkv_w_hbm.at[:, pl.ds(i * width, width)], down_w.at[pl.ds(i * width, width)]) for i in range(3)
    ]
    g_copy = copy(4, g_hbm, merged)
    out_copy = copy(5, out_hbm, out_w)
    up_copy = copy(6, up_hbm, up_w)
    proj_copy = copy(7, proj_hbm, proj_w)
    down_copy = copy(8, down_hbm, down_w)
    qkv_saves = [copy(9 + i, eu.at[i], qkv_hbm.at[i]) for i in range(3)]
    h1_save = copy(12, lefts.at[0], h1_hbm)
    h1_copy = copy(13, h1_hbm, lefts.at[0])
    qkv_copies = [copy(14 + i, qkv_hbm.at[i], down_w.at[pl.ds(i * count, count)]) for i in range(3)]
    qkv_w_again = copy(17, qkv_w_hbm, up_w.at[:, pl.ds(0, 3 * width)])
    tokens_copy = copy(18, pool.at[0], tokens_hbm)
    merged_copy = copy(19, merged, merged_hbm)

    for item in (x_copy, *qkv_w_copies, g_copy):
        item.start()
    vec[0] = jnp.zeros((VECTORS, width), F32)

    def add_to(row, value, lanes=slice(None)):
        vec[0, row : row + 1, lanes] = vec[0, row : row + 1, lanes] + jnp.sum(value, 0, keepdims=True)

    def tile_rows(tile):
        return pl.ds(pl.multiple_of(tile * TILE, TILE), TILE)

    def tile_valid(tile):
        per_pair = seq // TILE
        row = lax.broadcasted_iota(jnp.int32, (TILE, 1), 0) + tile % per_pair * TILE
        return row < len_ref[tile // per_pair]

    def put(slot, value, at, z_first):
        turned = value.T
        for chunk in range(16):
            lefts[slot, slot_of(chunk, z_first), :, at] = turned[chunk * SHARD : (chunk + 1) * SHARD]

    gain_one, gain_two = gain_ref[0:1].astype(F32), gain_ref[1:2].astype(F32)
    shift_one, shift_two = shift_ref[0:1].astype(F32), shift_ref[1:2].astype(F32)
    biases = bias_ref[...].astype(F32)
    x_copy.wait()
    for item in qkv_w_copies:
        item.wait()

    def first_norm(tile, carry):
        at = tile_rows(tile)
        hat, _ = norm_stats(pool[1, at, :].astype(F32))
        h = (hat * gain_one + shift_one).astype(BF16)
        put(0, h, at, QKV_Z_FIRST)
        q = (nn(h, down_w[:width, :]) + biases[0:1]).astype(BF16)
        eu[0, at, :] = q * BF16(HEAD_DIM**-0.5)
        eu[1, at, :] = nn(h, down_w[width : 2 * width, :]).astype(BF16)
        eu[2, at, :] = (nn(h, down_w[2 * width : 3 * width, :]) + biases[1:2]).astype(BF16)
        return carry

    lax.fori_loop(0, tiles, first_norm, 0)
    for item in (h1_save, *qkv_saves, down_copy, out_copy, up_copy, proj_copy):
        item.start()

    g_copy.wait()
    pl.semaphore_wait(barrier, 5)
    strip = 128
    row = lax.broadcasted_iota(jnp.int32, (strip, 1), 0)

    def cotangent(side, put_strip):
        for start in range(0, seq, strip):
            first = pl.multiple_of(side * seq + start, strip)
            value = merged[0, pl.ds(first, strip), :].astype(F32)
            after = merged[0, pl.ds(first + strip, 1), :].astype(F32)
            put_strip(start, jnp.where(row == strip - 1, after, pltpu.roll(value, strip - 1, 0)).astype(BF16))

    def put_send(start, value):
        y_send[start : start + strip, :] = value

    def put_own(start, value):
        pool[0, pl.ds(pl.multiple_of(tower * seq + start, strip), strip), :] = value

    cotangent(1 - tower, put_send)
    own_rows = pl.ds(pl.multiple_of(tower * seq, seq), seq)
    g_swap = pltpu.make_async_remote_copy(
        y_send, pool.at[0, own_rows], tower_sem.at[0], tower_sem.at[1], device_id=by_x, device_id_type=MESH
    )
    g_swap.start()
    cotangent(tower, put_own)
    vec[0, 13:14, :] = merged[0, 0:1, :].astype(F32)

    def attend(step, carry):
        pair, block = step // BLOCKS, step % BLOCKS
        at = pl.ds(pl.multiple_of(pair * seq, seq), seq)
        lanes = pl.ds(pl.multiple_of(block * LANES, LANES), LANES)
        valid = lax.broadcasted_iota(jnp.int32, (1, seq), 1) < len_ref[pair]
        q, k, v = (eu[number, at, lanes] for number in range(3))
        mixed = None
        for head in range(2):
            scores = jnp.where(valid, nt(head_lanes(head, q), k), masked_score)
            largest = jnp.max(scores, 1, keepdims=True)
            weights = jnp.exp(scores - largest)
            total = jnp.sum(weights, 1, keepdims=True)
            here = nn(weights.astype(BF16), head_lanes(head, v)) * (1.0 / total)
            mixed = here if mixed is None else mixed + here
            logs[pair, block, head : head + 1, :] = (largest + jnp.log(total)).reshape(1, seq)
        pool[3, at, lanes] = mixed.astype(BF16)
        return carry

    lax.fori_loop(0, pairs * BLOCKS, attend, 0)

    for item in (h1_save, *qkv_saves, out_copy, up_copy, down_copy, proj_copy):
        item.wait()
    g_swap.wait_send()

    def feed(tile, carry):
        at = tile_rows(tile)
        a = pool[3, at, :]
        put(6, a, at, False)
        mid = pool[1, at, :].astype(F32) + nn(a, out_w[...]) + biases[2:3]
        x1[at, :] = mid
        hat, _ = norm_stats(mid)
        h = (hat * gain_two + shift_two).astype(BF16)
        put(5, h, at, False)
        x2 = mid + biases[3:4]
        for part in range(parts):
            span = slice(part * width, (part + 1) * width)
            u = nn(h, up_w[:, span]) + hidden_ref[:, span].astype(F32)
            acted, slope = gelu_and_slope(u)
            z = acted.astype(BF16)
            eu[part, at, :] = slope.astype(BF16)
            turned = z.T
            for piece in range(16):
                chunk, block = part * 4 + piece // 4, piece % 4
                lefts[1 + block, slot_of(chunk, False), :, at] = turned[piece * SHARD : (piece + 1) * SHARD]
            x2 = x2 + nn(z, down_w[span, :])
        x2_low = x2.astype(BF16)
        put(0, x2_low, at, False)
        rows_y = jnp.where(tile_valid(tile), nn(x2_low, proj_w[...]) + biases[4:5], 0.0).astype(BF16)
        per_pair = seq // TILE
        here = pl.ds(pl.multiple_of(tile % per_pair * TILE, TILE), TILE)

        @pl.when(tile // per_pair == tower)
        def _():
            merged[0, here, :] = rows_y

        @pl.when(tile // per_pair != tower)
        def _():
            y_send[here, :] = rows_y

        return carry

    lax.fori_loop(0, tiles, feed, 0)
    y_swap = pltpu.make_async_remote_copy(
        y_send, y_got, tower_sem.at[2], tower_sem.at[3], device_id=by_x, device_id_type=MESH
    )
    y_swap.start()

    g_swap.wait_recv()

    def project_back(tile, carry):
        at = tile_rows(tile)
        g = jnp.where(tile_valid(tile), pool[0, at, :].astype(F32), 0.0)
        g_low = g.astype(BF16)
        pool[0, at, :] = g_low
        dx2 = nt(g_low, proj_w[...])
        pool[2, at, :] = dx2.astype(BF16)
        add_to(3, dx2)
        add_to(4, g)
        return carry

    lax.fori_loop(0, tiles, project_back, 0)

    def bits(block):
        if QKV_Z_FIRST and block >= 10:
            return (by_core, by_lo, by_y, by_hi), (z_lo, y, z_hi)
        return (by_core, by_y, by_lo, by_hi), (y, z_lo, z_hi)

    gots = (got_1, got_2, got_3, got_4)

    def place(block, level):
        return block % (CORE_RING, SECOND_RING, BLOCK_COUNT, BLOCK_COUNT)[level]

    def swap_of(block, level):
        partners, (b1, b2, b3) = bits(block)
        here = grads.at[block % RING]
        if level == 0:
            source = here.at[1 - core]
        elif level == 1:
            source = here.at[core, pl.ds((1 - b1) * 4, 4)]
        elif level == 2:
            source = here.at[core, pl.ds(b1 * 4 + (1 - b2) * 2, 2)]
        else:
            source = here.at[core, pl.ds(b1 * 4 + b2 * 2 + 1 - b3, 1)]
        return pltpu.make_async_remote_copy(
            source,
            gots[level].at[place(block, level)],
            send_sem.at[level, block],
            recv_sem.at[level, block],
            device_id=partners[level],
            device_id_type=MESH,
        )

    def advance(block, level):
        _, (b1, b2, b3) = bits(block)
        slot = block % RING
        swap_of(block, level - 1).wait_recv()
        got = gots[level - 1]
        size = 8 >> level
        bit = (b1, b2, b3)[level - 1]
        base = (0, b1 * 4, b1 * 4 + b2 * 2)[level - 1]
        for other in (1, 0):
            side = (1 - bit) if other else bit

            def add(i, carry, side=side):
                at = side * size + i
                total = grads[slot, core, base + at].astype(F32) + got[place(block, level - 1), at].astype(F32)
                grads[slot, core, base + at] = total.astype(BF16)
                return carry

            lax.fori_loop(0, size, add, 0)
            if other:
                if level == 1 and block >= SECOND_RING:
                    assert (block - SECOND_RING, 2) in done
                    pl.semaphore_wait(free_sem.at[1, block], 1)
                swap_of(block, level).start()
        later = block + (CORE_RING, SECOND_RING, BLOCK_COUNT)[level - 1]
        if later < BLOCK_COUNT:
            pl.semaphore_signal(
                free_sem.at[level - 1, later], inc=1, device_id=bits(later)[0][level - 1], device_id_type=MESH
            )

    def sum_copy(block, slot):
        if block == 0:
            target = proj_ref
        elif block < 5:
            target = down_ref.at[pl.ds((block - 1) * SHARD, SHARD)]
        elif block < 9:
            target = up_ref.at[:, pl.ds((block - 5) * width, width)]
        elif block == 9:
            target = out_ref
        else:
            target = qkv_ref.at[:, pl.ds((block - 10) * width, width)]
        return pltpu.make_async_copy(sums.at[slot], target, sum_sem.at[slot])

    finished = []

    def finish(block):
        _, (b1, b2, b3) = bits(block)
        swap_of(block, 3).wait_recv()
        total = grads[block % RING, core, b1 * 4 + b2 * 2 + b3].astype(F32) + got_4[block, 0].astype(F32)
        if len(finished) >= 3:
            sum_copy(finished[-3], (len(finished) - 3) % 3).wait()
        place_now = len(finished) % 3
        sums[place_now] = total
        sum_copy(block, place_now).start()
        finished.append(block)
        for level in range(4):
            swap_of(block, level).wait_send()

    done = set()

    def tick(*work):
        for block, level in work:
            assert (block, level) not in done and (level == 1 or (block, level - 1) in done)
            done.add((block, level))
            if level == 4:
                finish(block)
            else:
                advance(block, level)

    def weight_grad(block, number, right):
        assert block < RING or (block - RING, 4) in done
        assert block < CORE_RING or (block - CORE_RING, 1) in done
        left = lefts[number].reshape(16 * SHARD, count)
        step = 256

        def columns(i, carry):
            at = pl.ds(pl.multiple_of(i * step, step), step)
            product = nn(left, right(at)).astype(BF16).reshape(2, 8, SHARD, step)
            grads[block % RING, :, :, :, at] = product
            return carry

        lax.fori_loop(0, width // step, columns, 0)
        if block >= CORE_RING:
            pl.semaphore_wait(free_sem.at[0, block], 1)
        swap_of(block, 0).start()

    weight_grad(0, 0, lambda at: pool[0, :, at])
    h1_copy.start()
    for part in range(parts):
        weight_grad(1 + part, 1 + part, lambda at: pool[2, :, at])
        tick(*TICKS["down", part])

    for part in range(parts):

        def tile_du(tile, carry, part=part):
            at = tile_rows(tile)
            du = nt(pool[2, at, :], down_w[part * width : (part + 1) * width, :])
            du = du * eu[part, at, :].astype(F32)
            eu[part, at, :] = du.astype(BF16)
            add_to(9 + part, du)
            return carry

        lax.fori_loop(0, tiles, tile_du, 0)
        tick(*TICKS["du", part])
    for item in qkv_copies:
        item.start()

    for part in range(parts):
        weight_grad(5 + part, 5, lambda at, part=part: eu[part, :, at])
        tick(*TICKS["up", part])

    for number in range(tiles):

        def mid_back(tile, carry):
            at = tile_rows(tile)
            dh = nt(eu[0, at, :], up_w[:, :width])
            for part in range(1, parts):
                dh = dh + nt(eu[part, at, :], up_w[:, part * width : (part + 1) * width])
            hat, scale = norm_stats(x1[at, :])
            dx1 = nt(pool[0, at, :], proj_w[...]) + norm_back(dh, hat, scale, gain_two)
            x1[at, :] = dx1
            e1 = dx1.astype(BF16)
            pool[2, at, :] = e1
            pool[0, at, :] = nt(e1, out_w[...]).astype(BF16)
            add_to(6, dh * hat)
            add_to(8, dh)
            add_to(2, dx1)
            return carry

        lax.fori_loop(number, number + 1, mid_back, 0)
        tick(*TICKS["mid", number])
    qkv_w_again.start()

    weight_grad(9, 6, lambda at: pool[2, :, at])
    tick(*TICKS["out", 0])

    for item in qkv_copies:
        item.wait()
    per_loop = 3
    for turn in range(pairs * BLOCKS // per_loop):

        def attend_back(step, carry):
            pair, block = step // BLOCKS, step % BLOCKS
            at = pl.ds(pl.multiple_of(pair * seq, seq), seq)
            lanes = pl.ds(pl.multiple_of(block * LANES, LANES), LANES)
            valid = lax.broadcasted_iota(jnp.int32, (seq, 1), 0) < len_ref[pair]
            q, k, v = (
                down_w[pl.ds(pl.multiple_of(number * count + pair * seq, seq), seq), lanes] for number in range(3)
            )
            d = pool[0, at, lanes]
            log_rows = logs[pair, block]
            k_t = k.T
            d_t = d.T
            prod_t = d_t.astype(F32) * pool[3, at, lanes].T.astype(F32)
            dq_rows = []
            dk = None
            dv = None
            for head in range(2):
                span = slice(head * HEAD_DIM, (head + 1) * HEAD_DIM)
                row_dot = jnp.sum(prod_t[span], 0, keepdims=True)
                v_here = head_lanes(head, v)
                dq_parts = []
                for start in range(0, seq, QUERIES):
                    some = slice(start, start + QUERIES)
                    q_here = head_lanes(head, q[some])
                    scores = jnp.where(valid, nt(k, q_here), masked_score)
                    probs = jnp.exp(scores - log_rows[head : head + 1, some])
                    d_probs = nn(v_here, d_t[:, some])
                    d_scores = (probs * (d_probs - row_dot[:, some])).astype(BF16)
                    dv_here = nn(probs.astype(BF16), head_lanes(head, d[some]))
                    dk_here = nn(d_scores, q_here)
                    dq_parts.append(nn(k_t[span], d_scores))
                    dk = dk_here if dk is None else dk + dk_here
                    dv = dv_here if dv is None else dv + dv_here
                dq_rows.append(jnp.concatenate(dq_parts, 1))
            dq = jnp.concatenate(dq_rows, 0).T * HEAD_DIM**-0.5
            for number, value in ((0, dq), (1, dk), (2, dv)):
                eu[number, at, lanes] = value.astype(BF16)
            add_to(0, dq, lanes)
            add_to(1, dv, lanes)
            return carry

        lax.fori_loop(turn * per_loop, (turn + 1) * per_loop, attend_back, 0)
        tick(*TICKS["attend", turn])

    h1_copy.wait()
    for part in range(3):
        weight_grad(10 + part, 0, lambda at, part=part: eu[part, :, at])
        tick(*TICKS["qkv", part])

    qkv_w_again.wait()
    for number in range(tiles):

        def first_back(tile, carry):
            at = tile_rows(tile)
            dh = nt(eu[0, at, :], up_w[:, :width])
            for part in (1, 2):
                dh = dh + nt(eu[part, at, :], up_w[:, part * width : (part + 1) * width])
            hat, scale = norm_stats(pool[1, at, :].astype(F32))
            pool[0, at, :] = (x1[at, :] + norm_back(dh, hat, scale, gain_one)).astype(BF16)
            add_to(5, dh * hat)
            add_to(7, dh)
            return carry

        lax.fori_loop(number, number + 1, first_back, 0)
        tick(*TICKS["first", number])
    tokens_copy.start()

    def vec_swap(level):
        return pltpu.make_async_remote_copy(
            vec.at[level],
            vec_got.at[level],
            vec_send.at[level],
            vec_recv.at[level],
            device_id=(by_core, by_y, by_lo, by_hi, by_x)[level],
            device_id_type=MESH,
        )

    vec_swap(0).start()

    y_swap.wait()

    def projected(side, start, size):
        own = merged[0, start : start + size, :].astype(F32)
        got = y_got[start : start + size, :].astype(F32)
        return jnp.where(tower == side, own, got)

    merged[0, 2 * seq : 2 * seq + 1, :] = projected(1, seq - 16, 16)[15:16].astype(BF16)
    for side in (1, 0):
        for start in range(seq - strip, -1, -strip):
            value = projected(side, start, strip)
            if start > 0:
                before = projected(side, start - 16, 16)[15:16]
            elif side == 1:
                before = projected(0, seq - 16, 16)[15:16]
            else:
                before = cls_row_ref[...].astype(F32)
            moved = jnp.where(row == 0, before, pltpu.roll(value, 1, 0))
            merged[0, side * seq + start : side * seq + start + strip, :] = moved.astype(BF16)
    merged_copy.start()

    for number, work in enumerate(TICKS["tail", 0]):
        tick(work)
        if number < 4:
            vec_swap(number).wait_recv()
            vec[number + 1] = vec[number] + vec_got[number]
            vec_swap(number + 1).start()
    vec_swap(4).wait_recv()
    vec_ref[0:13] = vec[4, 0:13]
    vec_ref[13:16] = vec[4, 13:16] + vec_got[4, 13:16]
    for level in range(5):
        vec_swap(level).wait_send()
    for number in range(BLOCK_COUNT - 3, BLOCK_COUNT):
        sum_copy(finished[number], number % 3).wait()
    tokens_copy.wait()
    merged_copy.wait()
    assert len(done) == 4 * BLOCK_COUNT


TICKS = {
    ('down', 0): [],
    ('down', 1): [],
    ('down', 2): [(0, 1)],
    ('down', 3): [(1, 1), (2, 1)],
    ('du', 0): [(3, 1)],
    ('du', 1): [(4, 1)],
    ('du', 2): [(0, 2)],
    ('du', 3): [],
    ('up', 0): [],
    ('up', 1): [(0, 3)],
    ('up', 2): [(1, 2), (5, 1), (0, 4)],
    ('up', 3): [(6, 1)],
    ('mid', 0): [(1, 3), (7, 1), (8, 1)],
    ('mid', 1): [(2, 2)],
    ('mid', 2): [(1, 4)],
    ('mid', 3): [(2, 3), (3, 2)],
    ('out', 0): [],
    ('attend', 0): [(2, 4), (3, 3), (4, 2), (9, 1)],
    ('attend', 1): [(3, 4), (4, 3), (5, 2)],
    ('attend', 2): [(4, 4), (5, 3)],
    ('attend', 3): [(5, 4), (6, 2)],
    ('qkv', 0): [(7, 2)],
    ('qkv', 1): [],
    ('qkv', 2): [(10, 1), (6, 3)],
    ('first', 0): [(11, 1)],
    ('first', 1): [(7, 3), (8, 2), (12, 1), (6, 4)],
    ('first', 2): [],
    ('first', 3): [],
    ('tail', 0): [(7, 4), (9, 2), (10, 2), (10, 3), (11, 2), (10, 4), (8, 3), (11, 3), (8, 4), (12, 2), (11, 4), (9, 3), (12, 3), (9, 4), (12, 4)],
}


def run_one(lengths, gains, shifts, biases, hidden, cls_row, x, g, qkv_w, out_w, up_w, down_w, proj_w):
    count, width = x.shape
    ff = up_w.shape[1]
    pairs = lengths.shape[0]
    seq = count // pairs
    shard = jax.ShapeDtypeStruct
    vmem = pl.BlockSpec(memory_space=pltpu.VMEM)
    hbm = pl.BlockSpec(memory_space=pl.ANY)
    return pl.pallas_call(
        one_kernel,
        in_specs=[pl.BlockSpec(memory_space=pltpu.SMEM)] + [vmem] * 5 + [hbm] * 7,
        out_specs=[hbm] * 5 + [vmem] + [hbm] * 4,
        out_shape=[
            shard((SHARD, width), F32),
            shard((4 * SHARD, width), F32),
            shard((SHARD, ff), F32),
            shard((SHARD, width), F32),
            shard((SHARD, 3 * width), F32),
            shard((VECTORS, width), F32),
            shard((count, width), BF16),
            shard(g.shape, BF16),
            shard((3, count, width), BF16),
            shard((16, SHARD, count), BF16),
        ],
        scratch_shapes=[
            pltpu.VMEM((RING, 2, 8, SHARD, width), BF16),
            pltpu.VMEM((CORE_RING, 8, SHARD, width), BF16),
            pltpu.VMEM((SECOND_RING, 4, SHARD, width), BF16),
            pltpu.VMEM((BLOCK_COUNT, 2, SHARD, width), BF16),
            pltpu.VMEM((BLOCK_COUNT, 1, SHARD, width), BF16),
            pltpu.VMEM((7, 16, SHARD, count), BF16),
            pltpu.VMEM((4, count, width), BF16),
            pltpu.VMEM((ff // width, count, width), BF16),
            pltpu.VMEM((ff, width), BF16),
            pltpu.VMEM((width, ff), BF16),
            pltpu.VMEM((width, width), BF16),
            pltpu.VMEM((width, width), BF16),
            pltpu.VMEM((count, width), F32),
            pltpu.VMEM((pairs, BLOCKS, 2, seq), F32),
            pltpu.VMEM((5, VECTORS, width), F32),
            pltpu.VMEM((5, VECTORS, width), F32),
            pltpu.VMEM((seq, width), BF16),
            pltpu.VMEM((seq, width), BF16),
            pltpu.VMEM(g.shape, BF16),
            pltpu.VMEM((3, SHARD, width), F32),
            pltpu.SemaphoreType.DMA((4, BLOCK_COUNT)),
            pltpu.SemaphoreType.DMA((4, BLOCK_COUNT)),
            pltpu.SemaphoreType.DMA((20,)),
            pltpu.SemaphoreType.DMA((3,)),
            pltpu.SemaphoreType.DMA((5,)),
            pltpu.SemaphoreType.DMA((5,)),
            pltpu.SemaphoreType.DMA((4,)),
            pltpu.SemaphoreType.REGULAR((2, BLOCK_COUNT)),
        ],
        compiler_params=pltpu.CompilerParams(
            collective_id=0, has_side_effects=True, vmem_limit_bytes=63 * MIB
        ),
        cost_estimate=cost(60e9, 60 * MIB),
        name="one",
    )(lengths, gains, shifts, biases, hidden, cls_row, x, g, qkv_w, out_w, up_w, down_w, proj_w)


def full_grad_kernel(left_ref, *refs):
    start = 0
    for right_ref in refs[:-1]:
        stop = start + right_ref.shape[1]
        refs[-1][:, start:stop] = nn(left_ref[...], right_ref[...])
        start = stop


def run_full_grad(left, *rights):
    height, count = left.shape
    width = sum(right.shape[1] for right in rights)
    tile = 384
    return pl.pallas_call(
        full_grad_kernel,
        grid=(height // tile,),
        in_specs=[rows(tile, count)] + [whole(right.shape) for right in rights],
        out_specs=rows(tile, width),
        out_shape=jax.ShapeDtypeStruct((height, width), F32),
        compiler_params=params(),
        name="full_grad",
    )(left, *rights)


def in_order(slabs, z_first):
    return jnp.stack([slabs[..., slot_of(chunk, z_first), :, :] for chunk in range(16)], -3)


def plain_back(lengths, logs, gains, feed_sums, cls_sum, left, h1, slope, g, e2, dx2, x1, a, qkv, x, y, down_w, up_w, out_w, qkv_w):
    count, width = x.shape
    seq = y.shape[2]
    eu, dx1, e1, da, hidden_sum, mid_sums = run_feed_back(e2, dx2, slope, x1, gains, out_w, up_w, down_w)
    dq, dk, dv, sum_q, sum_v = run_attend_back(lengths, qkv, a, da, logs, seq)
    tokens_grad, first_sums = run_qkv_back(dq, dk, dv, dx1, x, gains, qkv_w)
    turned = in_order(left, False)
    z = turned[1:5].transpose(1, 0, 2, 3).reshape(4 * width, count)
    x2, h2, a_t = (turned[i].reshape(width, count) for i in (0, 5, 6))
    h1 = in_order(h1, QKV_Z_FIRST).reshape(width, count)
    grads = (run_full_grad(x2, g), run_full_grad(z, e2), run_full_grad(h2, eu), run_full_grad(a_t, e1), run_full_grad(h1, dq, dk, dv))
    grads = [lax.psum_scatter(grad, "dp", scatter_dimension=0, tiled=True) for grad in grads]
    vectors = jnp.concatenate(
        [
            jnp.sum(sum_q, 0), jnp.sum(sum_v, 0), mid_sums[2:3], feed_sums, first_sums[0:1], mid_sums[0:1],
            first_sums[1:2], mid_sums[1:2], hidden_sum.reshape(-1, width),
        ],
        axis=0,
    )
    vectors = lax.psum(vectors, "dp")
    cls = lax.psum(cls_sum, ("tower", "dp"))
    y_got = lax.ppermute(take(y, 1 - lax.axis_index("tower")), "tower", [(0, 1), (1, 0)])
    return grads, vectors, cls, tokens_grad, y_got


def take(value, index):
    return lax.dynamic_index_in_dim(value, index, 0, keepdims=False)


def spread_kernel(index_ref, vec_ref, *refs):
    sources, (gain_ref, shift_ref, bias_ref, hidden_ref, cls_ref), targets, held = refs[:7], refs[7:12], refs[12:19], refs[19:26]
    sem_in, sem_out = refs[26:]
    ins = [pltpu.make_async_copy(source, there, sem_in.at[i]) for i, (source, there) in enumerate(zip(sources, held))]
    outs = [pltpu.make_async_copy(there, target, sem_out.at[i]) for i, (there, target) in enumerate(zip(held, targets))]
    for item in ins:
        item.start()
    index = index_ref[0]
    width = vec_ref.shape[1]
    piece = gain_ref.shape[1]
    mine = pltpu.roll(vec_ref[...], width - piece * index, 1)[:, :piece]
    bias_ref[...] = mine[0:5]
    gain_ref[...] = mine[5:7]
    shift_ref[...] = mine[7:9]
    share = hidden_ref.shape[1]
    per_row = width // share
    row = vec_ref[pl.ds(9 + index // per_row, 1), :]
    hidden_ref[...] = pltpu.roll(row, width - share * (index % per_row), 1)[:, :share]
    cls_ref[...] = vec_ref[13:14]
    for before, after in zip(ins, outs):
        before.wait()
        after.start()
    for item in outs:
        item.wait()


def run_spread(index, vectors, *arrays):
    width = vectors.shape[1]
    small = [jax.ShapeDtypeStruct(shape, F32) for shape in ((2, width // 16), (2, width // 16), (5, width // 16), (1, width // 4), (1, width))]
    vmem = pl.BlockSpec(memory_space=pltpu.VMEM)
    hbm = pl.BlockSpec(memory_space=pl.ANY)
    return pl.pallas_call(
        spread_kernel,
        in_specs=[pl.BlockSpec(memory_space=pltpu.SMEM), vmem] + [hbm] * len(arrays),
        out_specs=[vmem] * 5 + [hbm] * len(arrays),
        out_shape=small + [jax.ShapeDtypeStruct(array.shape, array.dtype) for array in arrays],
        scratch_shapes=[pltpu.VMEM(array.shape, array.dtype) for array in arrays]
        + [pltpu.SemaphoreType.DMA((len(arrays),))] * 2,
        compiler_params=params(62),
        name="spread",
    )(index, vectors, *arrays)


def local(
    dp, tokens, group_id, caption_len, cls_row, norm_gains, shifts, bias_model, bias_hidden,
    w_qkv, w_out, w_up, w_down, w_proj, merged_grad,
):
    tower = lax.axis_index("tower")
    index = lax.axis_index("dp")
    pairs, seq, width = tokens.shape[1:]
    half = pairs // 2
    count = pairs * seq
    image_len = jnp.where(group_id == 1, IMG_LARGE, IMG_SMALL)
    lengths = jnp.where(tower == 0, image_len, caption_len).astype(jnp.int32)
    gains, shift_rows, biases, hidden = norm_gains[0], shifts[0], bias_model[0], bias_hidden
    qkv_w, out_w, up_w, down_w, proj_w = w_qkv[0], w_out[0], w_up[0], w_down[0], w_proj[0]
    x = tokens[0].reshape(count, width)

    if dp == 16 and pairs == 2:
        *grads, vectors, tokens_grad, merged_input, _, _ = run_one(
            lengths, gains, shift_rows, biases, hidden, cls_row[None], x, merged_grad[0], qkv_w, out_w, up_w, down_w, proj_w
        )
        gain_sum, shift_sum, bias_sum, hidden_sum, cls, *arrays = run_spread(
            index.astype(jnp.int32)[None], vectors, *grads, tokens_grad, merged_input
        )
        proj, down, up, out, qkv_grad, tokens_grad, merged_input = arrays
    else:
        positions = lax.broadcasted_iota(jnp.int32, (pairs, seq), 1)
        valid = (positions < lengths[:, None]).reshape(count, 1).astype(F32)
        image_grad = merged_grad[0, :, 1 : 1 + seq]
        text_grad = merged_grad[0, :, 1 + seq :]
        g_keep = jnp.where(tower == 0, image_grad, text_grad)
        g_send = jnp.where(tower == 0, text_grad, image_grad)
        g_got = lax.ppermute(g_send, "tower", [(0, 1), (1, 0)])
        cls_sum = jnp.sum(merged_grad[0, :, 0].astype(F32), 0)[None]
        h1, qkv = run_qkv(x, gains, shift_rows, biases, qkv_w)
        mixed, logs = run_attend(lengths, qkv, seq)
        g = jnp.where(tower == 0, jnp.stack([g_keep, g_got]), jnp.stack([g_got, g_keep])).reshape(count, width)
        x1, left, slope, y, g_low, dx2, e2, feed_sums = run_feed(
            valid, x, mixed, g, gains, shift_rows, biases, hidden, out_w, up_w, down_w, proj_w
        )
        y = y.reshape(2, half, seq, width)
        grads, vectors, cls, tokens_grad, y_got = plain_back(
            lengths, logs, gains, feed_sums, cls_sum, left, h1, slope, g_low, e2, dx2, x1, mixed, qkv, x, y,
            down_w, up_w, out_w, qkv_w,
        )
        proj, down, up, out, qkv_grad = grads
        y_own = take(y, tower)
        cls_block = jnp.broadcast_to(cls_row.reshape(1, 1, width), (half, 1, width))
        image_rows = jnp.where(tower == 0, y_own, y_got)
        text_rows = jnp.where(tower == 0, y_got, y_own)
        merged_input = jnp.concatenate([cls_block, image_rows, text_rows], axis=1)
        mine = lax.dynamic_slice_in_dim(vectors[:9], index * (width // dp), width // dp, 1)
        bias_sum, gain_sum, shift_sum = mine[0:5], mine[5:7], mine[7:9]
        ff = up_w.shape[1]
        hidden_sum = lax.dynamic_slice_in_dim(vectors[9:13].reshape(1, ff), index * (ff // dp), ff // dp, 1)
    return (
        merged_input[None], tokens_grad.reshape(tokens.shape), cls.reshape(width), gain_sum[None], shift_sum[None],
        bias_sum[None], hidden_sum, qkv_grad[None], out[None], up[None], down[None], proj[None],
    )


def solution(mesh):
    tower = P("tower", None, None)
    in_specs = (
        P("tower", "dp", None, None), P("dp"), P("dp"), P(), tower, tower, tower, P("tower", None),
        tower, tower, tower, tower, tower, P("tower", "dp", None, None),
    )
    spread = P("tower", None, "dp")
    weight = P("tower", "dp", None)
    out_specs = (
        P("tower", "dp", None, None), P("tower", "dp", None, None), P(), spread, spread, spread, P("tower", "dp"),
        weight, weight, weight, weight, weight,
    )
    return jax.shard_map(
        partial(local, mesh.shape["dp"]), mesh=mesh, in_specs=in_specs, out_specs=out_specs, check_vma=False
    )
```

```python
from functools import partial

import jax
import jax.numpy as jnp
from jax import lax
from jax.experimental import pallas as pl
from jax.experimental.pallas import tpu as pltpu
from jax.sharding import PartitionSpec as P

HEADS = 12
HEAD_DIM = 64
IMG_SMALL = 197
IMG_LARGE = 325
LANES = 128
BLOCKS = HEADS * HEAD_DIM // LANES

norm_eps = 1e-06
masked_score = -1e30
F32 = jnp.float32
BF16 = jnp.bfloat16
MIB = 1 << 20
SHARD = 48

ERF_P = 0.39
ERF_C = (0.2344334842, 0.09695712066, 0.6357617632, -0.6184387086, 0.8763152235, -0.225028871)


def nn(left, right):
    return jnp.dot(left, right, preferred_element_type=F32)


def nt(left, right):
    return lax.dot_general(left, right, (((1,), (1,)), ((), ())), preferred_element_type=F32)


def tn(left, right):
    return lax.dot_general(left, right, (((0,), (0,)), ((), ())), preferred_element_type=F32)


def params(vmem=48, semantics=None):
    return pltpu.CompilerParams(vmem_limit_bytes=vmem * MIB, dimension_semantics=semantics)


def cost(flops, nbytes, trans=0):
    return pl.CostEstimate(flops=int(flops), bytes_accessed=int(nbytes), transcendentals=int(trans))


def whole(shape):
    return pl.BlockSpec(shape, lambda *_: (0,) * len(shape), pipeline_mode=pl.Buffered(1))


def rows(tile, width):
    return pl.BlockSpec((tile, width), lambda i, *_: (i, 0))


def norm_stats(x):
    mean = jnp.mean(x, -1, keepdims=True)
    centred = x - mean
    spread = jnp.mean(centred * centred, -1, keepdims=True)
    scale = lax.rsqrt(spread + norm_eps)
    return centred * scale, scale


def norm_back(grad, hat, scale, gain):
    d_hat = grad * gain
    first = jnp.mean(d_hat, -1, keepdims=True)
    second = jnp.mean(d_hat * hat, -1, keepdims=True)
    return scale * (d_hat - first - hat * second)


def gelu_and_slope(u):
    bell = jnp.exp2(u * u * (-0.5 * 1.4426950408889634))
    t = 1.0 / (1.0 + (ERF_P * 0.5**0.5) * jnp.abs(u))
    poly = jnp.full_like(u, 0.5 * ERF_C[-1])
    for c in ERF_C[-2::-1]:
        poly = poly * t + 0.5 * c
    tail = poly * t * bell
    phi = jnp.where(u >= 0, 1.0 - tail, tail)
    slope = phi + u * bell * 0.3989422804014327
    return u * phi, slope


def slot_of(chunk):
    z_hi, z_lo, y, core = chunk // 8, chunk // 4 % 2, chunk // 2 % 2, chunk % 2
    return ((core * 2 + y) * 2 + z_lo) * 2 + z_hi


def put_slabs(ref, lead, value):
    turned = value.T
    for chunk in range(16):
        ref[(*lead, slot_of(chunk))] = turned[chunk * SHARD : (chunk + 1) * SHARD]


def add_sum(ref, index, value, first):
    ref[index : index + 1, :] = jnp.where(first, 0.0, ref[index : index + 1, :]) + jnp.sum(value, 0, keepdims=True)


def qkv_kernel(x_ref, gain_ref, shift_ref, bias_ref, w_ref, h_ref, out_ref):
    width = x_ref.shape[1]
    hat, _ = norm_stats(x_ref[...].astype(F32))
    h = (hat * gain_ref[0:1].astype(F32) + shift_ref[0:1].astype(F32)).astype(BF16)
    put_slabs(h_ref, (), h)
    q = nn(h, w_ref[:, :width]) + bias_ref[0:1].astype(F32)
    out_ref[:, :width] = q.astype(BF16) * BF16(HEAD_DIM**-0.5)
    out_ref[:, width : 2 * width] = nn(h, w_ref[:, width : 2 * width]).astype(BF16)
    v = nn(h, w_ref[:, 2 * width :]) + bias_ref[1:2].astype(F32)
    out_ref[:, 2 * width :] = v.astype(BF16)


def run_qkv(x, gains, shifts, biases, w, tile=256):
    count, width = x.shape
    return pl.pallas_call(
        qkv_kernel,
        grid=(count // tile,),
        in_specs=[rows(tile, width), whole(gains.shape), whole(shifts.shape), whole(biases.shape), whole(w.shape)],
        out_specs=[pl.BlockSpec((16, SHARD, tile), lambda i: (0, 0, i)), rows(tile, 3 * width)],
        out_shape=[
            jax.ShapeDtypeStruct((16, SHARD, count), BF16),
            jax.ShapeDtypeStruct((count, 3 * width), BF16),
        ],
        compiler_params=params(),
        cost_estimate=cost(6 * count * width * width, 2 * (count * width * 5 + 3 * width * width)),
        name="qkv",
    )(x, gains, shifts, biases, w)


def head_lanes(head, block):
    lane = lax.broadcasted_iota(jnp.int32, (1, LANES), 1)
    keep = (lane < HEAD_DIM) if head == 0 else (lane >= HEAD_DIM)
    return jnp.where(keep, block, jnp.zeros_like(block))


def attend_kernel(len_ref, q_ref, k_ref, v_ref, a_ref, l_ref):
    seq = q_ref.shape[0]
    valid = lax.broadcasted_iota(jnp.int32, (seq, 1), 0) < len_ref[pl.program_id(0)]
    q = q_ref[...]
    k = k_ref[...]
    v_t = v_ref[...].T
    parts = []
    for head in range(2):
        scores = jnp.where(valid, nt(k, head_lanes(head, q)), masked_score)
        largest = jnp.max(scores, 0, keepdims=True)
        weights = jnp.exp(scores - largest)
        total = jnp.sum(weights, 0, keepdims=True)
        mixed = nn(v_t[head * HEAD_DIM : (head + 1) * HEAD_DIM], weights.astype(BF16))
        parts.append((mixed * (1.0 / total)).astype(BF16))
        l_ref[0, 0, head : head + 1, :] = largest + jnp.log(total)
    a_ref[...] = jnp.concatenate(parts, 0).T


def column(seq, shift):
    return pl.BlockSpec((seq, LANES), lambda p, b, *_: (p, b + shift))


def run_attend(lengths, qkv, seq):
    count = qkv.shape[0]
    width = qkv.shape[1] // 3
    pairs = count // seq
    return pl.pallas_call(
        attend_kernel,
        grid_spec=pltpu.PrefetchScalarGridSpec(
            num_scalar_prefetch=1,
            grid=(pairs, BLOCKS),
            in_specs=[column(seq, 0), column(seq, BLOCKS), column(seq, 2 * BLOCKS)],
            out_specs=[column(seq, 0), pl.BlockSpec((1, 1, 2, seq), lambda p, b, *_: (p, b, 0, 0))],
        ),
        out_shape=[
            jax.ShapeDtypeStruct((count, width), BF16),
            jax.ShapeDtypeStruct((pairs, BLOCKS, 2, seq), F32),
        ],
        compiler_params=params(),
        cost_estimate=cost(16 * pairs * HEADS * seq * seq * HEAD_DIM, 8 * count * width, pairs * HEADS * seq * seq),
        name="attend",
    )(lengths, qkv, qkv, qkv)


def attend_back_kernel(len_ref, q_ref, k_ref, v_ref, a_ref, d_ref, l_ref, dq_ref, dk_ref, dv_ref, sq_ref, sv_ref):
    seq = q_ref.shape[0]
    valid = lax.broadcasted_iota(jnp.int32, (seq, 1), 0) < len_ref[pl.program_id(0)]
    q = q_ref[...]
    k = k_ref[...]
    v = v_ref[...]
    d = d_ref[...]
    k_t = k.T
    d_t = d.T
    prod_t = d_t.astype(F32) * a_ref[...].T.astype(F32)
    dq_parts = []
    dk = None
    dv = None
    for head in range(2):
        span = slice(head * HEAD_DIM, (head + 1) * HEAD_DIM)
        q_here = head_lanes(head, q)
        scores = jnp.where(valid, nt(k, q_here), masked_score)
        probs = jnp.exp(scores - l_ref[0, 0, head : head + 1, :])
        row_dot = jnp.sum(prod_t[span], 0, keepdims=True)
        d_probs = nn(head_lanes(head, v), d_t)
        d_scores = (probs * (d_probs - row_dot)).astype(BF16)
        dv_here = nn(probs.astype(BF16), head_lanes(head, d))
        dk_here = nn(d_scores, q_here)
        dq_parts.append(nn(k_t[span], d_scores))
        dk = dk_here if dk is None else dk + dk_here
        dv = dv_here if dv is None else dv + dv_here
    dq = jnp.concatenate(dq_parts, 0).T * HEAD_DIM**-0.5
    dq_ref[...] = dq.astype(BF16)
    dk_ref[...] = dk.astype(BF16)
    dv_ref[...] = dv.astype(BF16)
    sq_ref[0] = jnp.sum(dq, 0, keepdims=True)
    sv_ref[0] = jnp.sum(dv, 0, keepdims=True)


def run_attend_back(lengths, qkv, mixed, d_mixed, log_total, seq):
    count = qkv.shape[0]
    width = qkv.shape[1] // 3
    pairs = count // seq
    sums = pl.BlockSpec((1, 1, LANES), lambda p, b, *_: (p, 0, b))
    return pl.pallas_call(
        attend_back_kernel,
        grid_spec=pltpu.PrefetchScalarGridSpec(
            num_scalar_prefetch=1,
            grid=(pairs, BLOCKS),
            in_specs=[
                column(seq, 0),
                column(seq, BLOCKS),
                column(seq, 2 * BLOCKS),
                column(seq, 0),
                column(seq, 0),
                pl.BlockSpec((1, 1, 2, seq), lambda p, b, *_: (p, b, 0, 0)),
            ],
            out_specs=[column(seq, 0)] * 3 + [sums] * 2,
        ),
        out_shape=[jax.ShapeDtypeStruct((count, width), BF16)] * 3
        + [jax.ShapeDtypeStruct((pairs, 1, width), F32)] * 2,
        compiler_params=params(),
        cost_estimate=cost(40 * pairs * HEADS * seq * seq * HEAD_DIM, 16 * count * width, pairs * HEADS * seq * seq),
        name="attend_back",
    )(lengths, qkv, qkv, qkv, mixed, d_mixed, log_total)


def feed_kernel(
    valid_ref, x_ref, a_ref, g_ref, gain_ref, shift_ref, bias_ref, hidden_ref, out_w, up_w, down_w, proj_w,
    x1_ref, left_ref, slope_ref, y_ref, gm_ref, dx2_ref, e2_ref, sum_ref,
):
    width = x_ref.shape[1]
    first = pl.program_id(0) == 0
    valid = valid_ref[...]
    a = a_ref[...]
    put_slabs(left_ref, (6,), a)
    x1 = x_ref[...].astype(F32) + nn(a, out_w[...]) + bias_ref[2:3].astype(F32)
    x1_ref[...] = x1
    hat, _ = norm_stats(x1)
    h = (hat * gain_ref[1:2].astype(F32) + shift_ref[1:2].astype(F32)).astype(BF16)
    put_slabs(left_ref, (5,), h)
    x2 = x1 + bias_ref[3:4].astype(F32)
    for part in range(up_w.shape[1] // width):
        span = slice(part * width, (part + 1) * width)
        u = nn(h, up_w[:, span]) + hidden_ref[:, span].astype(F32)
        acted, slope = gelu_and_slope(u)
        z = acted.astype(BF16)
        slope_ref[:, span] = slope.astype(BF16)
        turned = z.T
        for piece in range(16):
            chunk, block = part * 4 + piece // 4, piece % 4
            left_ref[1 + block, slot_of(chunk)] = turned[piece * SHARD : (piece + 1) * SHARD]
        x2 = x2 + nn(z, down_w[span, :])
    x2_low = x2.astype(BF16)
    put_slabs(left_ref, (0,), x2_low)
    y_ref[...] = ((nn(x2_low, proj_w[...]) + bias_ref[4:5].astype(F32)) * valid).astype(BF16)
    g = g_ref[...].astype(F32) * valid
    g_low = g.astype(BF16)
    gm_ref[...] = g_low
    dx2 = nt(g_low, proj_w[...])
    dx2_ref[...] = dx2
    e2_ref[...] = dx2.astype(BF16)
    add_sum(sum_ref, 0, dx2, first)
    add_sum(sum_ref, 1, g, first)


def run_feed(valid, x, a, g, gains, shifts, biases, hidden, out_w, up_w, down_w, proj_w, tile=256):
    count, width = x.shape
    ff = up_w.shape[1]
    low = jax.ShapeDtypeStruct((count, width), BF16)
    full = jax.ShapeDtypeStruct((count, width), F32)
    weights = (gains, shifts, biases, hidden, out_w, up_w, down_w, proj_w)
    return pl.pallas_call(
        feed_kernel,
        grid=(count // tile,),
        in_specs=[rows(tile, 1)] + [rows(tile, width)] * 3 + [whole(w.shape) for w in weights],
        out_specs=[
            rows(tile, width), pl.BlockSpec((7, 16, SHARD, tile), lambda i: (0, 0, 0, i)), rows(tile, ff),
            rows(tile, width), rows(tile, width), rows(tile, width), rows(tile, width), whole((2, width)),
        ],
        out_shape=[
            full, jax.ShapeDtypeStruct((7, 16, SHARD, count), BF16), jax.ShapeDtypeStruct((count, ff), BF16),
            low, low, full, low, jax.ShapeDtypeStruct((2, width), F32),
        ],
        compiler_params=params(60),
        cost_estimate=cost(2 * count * width * (3 * width + 2 * ff), count * (width * 24 + ff * 6) + 11 * MIB),
        name="feed",
    )(valid, x, a, g, *weights)


def feed_back_kernel(
    e2_ref, dx2_ref, slope_ref, x1_ref, gain_ref, out_w, up_w, down_w,
    eu_ref, dx1_ref, e1_ref, da_ref, hid_ref, sum_ref,
):
    width = e2_ref.shape[1]
    first = pl.program_id(0) == 0
    e2 = e2_ref[...]
    dh = None
    for start in range(0, up_w.shape[1], width):
        span = slice(start, start + width)
        du = nt(e2, down_w[span, :]) * slope_ref[:, span].astype(F32)
        eu = du.astype(BF16)
        eu_ref[:, span] = eu
        hid_ref[:, span] = jnp.where(first, 0.0, hid_ref[:, span]) + jnp.sum(du, 0, keepdims=True)
        part = nt(eu, up_w[:, span])
        dh = part if dh is None else dh + part
    hat, scale = norm_stats(x1_ref[...])
    dx1 = dx2_ref[...] + norm_back(dh, hat, scale, gain_ref[1:2].astype(F32))
    dx1_ref[...] = dx1
    e1 = dx1.astype(BF16)
    e1_ref[...] = e1
    da_ref[...] = nt(e1, out_w[...]).astype(BF16)
    add_sum(sum_ref, 0, dh * hat, first)
    add_sum(sum_ref, 1, dh, first)
    add_sum(sum_ref, 2, dx1, first)


def run_feed_back(e2, dx2, slope, x1, gains, out_w, up_w, down_w, tile=256):
    count, width = x1.shape
    ff = up_w.shape[1]
    low = jax.ShapeDtypeStruct((count, width), BF16)
    return pl.pallas_call(
        feed_back_kernel,
        grid=(count // tile,),
        in_specs=[rows(tile, width), rows(tile, width), rows(tile, ff), rows(tile, width)]
        + [whole(w.shape) for w in (gains, out_w, up_w, down_w)],
        out_specs=[rows(tile, ff), rows(tile, width), rows(tile, width), rows(tile, width), whole((1, ff)), whole((3, width))],
        out_shape=[
            jax.ShapeDtypeStruct((count, ff), BF16),
            jax.ShapeDtypeStruct((count, width), F32),
            low,
            low,
            jax.ShapeDtypeStruct((1, ff), F32),
            jax.ShapeDtypeStruct((3, width), F32),
        ],
        compiler_params=params(60),
        cost_estimate=cost(2 * count * width * (width + 2 * ff), count * (width * 18 + ff * 6) + 10 * MIB),
        name="feed_back",
    )(e2, dx2, slope, x1, gains, out_w, up_w, down_w)


def qkv_back_kernel(dq_ref, dk_ref, dv_ref, dx1_ref, x_ref, gain_ref, w_ref, out_ref, sum_ref):
    width = x_ref.shape[1]
    first = pl.program_id(0) == 0
    dh = nt(dq_ref[...], w_ref[:, :width])
    dh = dh + nt(dk_ref[...], w_ref[:, width : 2 * width])
    dh = dh + nt(dv_ref[...], w_ref[:, 2 * width :])
    hat, scale = norm_stats(x_ref[...].astype(F32))
    out_ref[...] = (dx1_ref[...] + norm_back(dh, hat, scale, gain_ref[0:1].astype(F32))).astype(BF16)
    add_sum(sum_ref, 0, dh * hat, first)
    add_sum(sum_ref, 1, dh, first)


def run_qkv_back(dq, dk, dv, dx1, x, gains, w, tile=256):
    count, width = x.shape
    return pl.pallas_call(
        qkv_back_kernel,
        grid=(count // tile,),
        in_specs=[rows(tile, width)] * 5 + [whole(gains.shape), whole(w.shape)],
        out_specs=[rows(tile, width), whole((2, width))],
        out_shape=[jax.ShapeDtypeStruct((count, width), BF16), jax.ShapeDtypeStruct((2, width), F32)],
        compiler_params=params(),
        cost_estimate=cost(6 * count * width * width, count * width * 14 + 6 * width * width),
        name="qkv_back",
    )(dq, dk, dv, dx1, x, gains, w)


BLOCK_COUNT = 13
RING = 7
CORE_RING = 4
SECOND_RING = 8
MODES = ('ylh', 'lyh', 'ylh', 'ylh', 'ylh', 'ylh', 'lyh', 'ylh', 'ylh', 'lyh', 'ylh', 'lyh', 'ylh')
QUERIES = 256
ABREAST = 3
VECTORS = 16
TILE = 256
MESH = pl.DeviceIdType.MESH


def one_kernel(
    group_ref, caption_ref, gain_ref, shift_ref, bias_ref, hidden_ref, cls_row_ref,
    x_hbm, g_hbm, qkv_w_hbm, out_hbm, up_hbm, down_hbm, proj_hbm,
    proj_ref, down_ref, up_ref, out_ref, qkv_ref, vec_ref, tokens_hbm, merged_hbm, qkv_hbm, h1_hbm,
    grads, got_1, got_2, got_3, got_4, lefts, pool, eu, down_w, up_w, out_w, proj_w, x1, logs, vec, vec_got,
    y_send, y_got, merged, sums,
    send_sem, recv_sem, load_sem, sum_sem, vec_send, vec_recv, tower_sem, free_sem,
):
    count, width = x1.shape
    pairs, _, _, seq = logs.shape
    half = pairs // 2
    parts = eu.shape[0]
    tiles = count // TILE
    index = lax.axis_index("dp")
    tower = lax.axis_index("tower")
    core, y, z_lo, z_hi = index % 2, index // 2 % 2, index // 4 % 2, index // 8
    by_core = {"dp": index + 1 - 2 * core}
    by_y = {"dp": index + 2 - 4 * y}
    by_lo = {"dp": index + 4 - 8 * z_lo}
    by_hi = {"dp": index + 8 - 16 * z_hi}
    by_x = {"tower": 1 - tower}

    def length(pair):
        image = jnp.where(group_ref[pair] == 1, IMG_LARGE, IMG_SMALL)
        return jnp.where(tower == 0, image, caption_ref[pair])

    barrier = pltpu.get_barrier_semaphore()
    for partner in (by_core, by_y, by_lo, by_hi, by_x):
        pl.semaphore_signal(barrier, inc=1, device_id=partner, device_id_type=MESH)

    def copy(number, source, target):
        return pltpu.make_async_copy(source, target, load_sem.at[number])

    x_copy = copy(0, x_hbm, pool.at[1])
    qkv_w_copies = [
        copy(1 + i, qkv_w_hbm.at[:, pl.ds(i * width, width)], down_w.at[pl.ds(i * width, width)]) for i in range(3)
    ]
    g_copy = copy(4, g_hbm, merged)
    out_copy = copy(5, out_hbm, out_w)
    up_copy = copy(6, up_hbm, up_w)
    proj_copy = copy(7, proj_hbm, proj_w)
    down_copy = copy(8, down_hbm, down_w)
    qkv_saves = [copy(9 + i, eu.at[i], qkv_hbm.at[i]) for i in range(3)]
    h1_save = copy(12, lefts.at[0], h1_hbm)
    h1_copy = copy(13, h1_hbm, lefts.at[0])
    qkv_copies = [copy(14 + i, qkv_hbm.at[i], down_w.at[pl.ds(i * count, count)]) for i in range(3)]
    qkv_w_again = copy(17, qkv_w_hbm, up_w.at[:, pl.ds(0, 3 * width)])
    tokens_copy = copy(18, pool.at[0], tokens_hbm)
    merged_copy = copy(19, merged, merged_hbm)

    for item in (x_copy, *qkv_w_copies, g_copy):
        item.start()
    vec[0] = jnp.zeros((VECTORS, width), F32)

    def add_to(row, value, lanes=slice(None)):
        vec[0, row : row + 1, lanes] = vec[0, row : row + 1, lanes] + jnp.sum(value, 0, keepdims=True)

    def tile_rows(tile):
        return pl.ds(pl.multiple_of(tile * TILE, TILE), TILE)

    def tile_valid(tile):
        per_pair = seq // TILE
        row = lax.broadcasted_iota(jnp.int32, (TILE, 1), 0) + tile % per_pair * TILE
        return row < length(tile // per_pair)

    def put(slot, value, at):
        turned = value.T
        for chunk in range(16):
            lefts[slot, slot_of(chunk), :, at] = turned[chunk * SHARD : (chunk + 1) * SHARD]

    gain_one, gain_two = gain_ref[0:1].astype(F32), gain_ref[1:2].astype(F32)
    shift_one, shift_two = shift_ref[0:1].astype(F32), shift_ref[1:2].astype(F32)
    biases = bias_ref[...].astype(F32)
    x_copy.wait()
    for item in qkv_w_copies:
        item.wait()

    def first_norm(tile, carry):
        at = tile_rows(tile)
        hat, _ = norm_stats(pool[1, at, :].astype(F32))
        h = (hat * gain_one + shift_one).astype(BF16)
        put(0, h, at)
        q = (nn(h, down_w[:width, :]) + biases[0:1]).astype(BF16)
        eu[0, at, :] = q * BF16(HEAD_DIM**-0.5)
        eu[1, at, :] = nn(h, down_w[width : 2 * width, :]).astype(BF16)
        eu[2, at, :] = (nn(h, down_w[2 * width : 3 * width, :]) + biases[1:2]).astype(BF16)
        return carry

    lax.fori_loop(0, tiles, first_norm, 0)
    for item in (h1_save, *qkv_saves, down_copy, out_copy, up_copy, proj_copy):
        item.start()

    g_copy.wait()
    pl.semaphore_wait(barrier, 5)
    strip = 128
    row = lax.broadcasted_iota(jnp.int32, (strip, 1), 0)

    def cotangent(side, put_strip):
        for start in range(0, seq, strip):
            first = pl.multiple_of(side * seq + start, strip)
            value = merged[0, pl.ds(first, strip), :].astype(F32)
            after = merged[0, pl.ds(first + strip, 1), :].astype(F32)
            put_strip(start, jnp.where(row == strip - 1, after, pltpu.roll(value, strip - 1, 0)).astype(BF16))

    def put_send(start, value):
        pool[2, start : start + strip, :] = value

    def put_own(start, value):
        pool[0, pl.ds(pl.multiple_of(tower * seq + start, strip), strip), :] = value

    cotangent(1 - tower, put_send)
    own_rows = pl.ds(pl.multiple_of(tower * seq, seq), seq)
    g_swap = pltpu.make_async_remote_copy(
        pool.at[2, pl.ds(0, seq)], pool.at[0, own_rows], tower_sem.at[0], tower_sem.at[1], device_id=by_x, device_id_type=MESH
    )
    g_swap.start()
    cotangent(tower, put_own)
    vec[0, 13:14, :] = merged[0, 0:1, :].astype(F32)

    def attend_one(pair, block):
        at = pl.ds(pl.multiple_of(pair * seq, seq), seq)
        lanes = pl.ds(pl.multiple_of(block * LANES, LANES), LANES)
        valid = lax.broadcasted_iota(jnp.int32, (1, seq), 1) < length(pair)
        q, k, v = (eu[number, at, lanes] for number in range(3))
        mixed = None
        for head in range(2):
            scores = jnp.where(valid, nt(head_lanes(head, q), k), masked_score)
            largest = jnp.max(scores, 1, keepdims=True)
            weights = jnp.exp(scores - largest)
            total = jnp.sum(weights, 1, keepdims=True)
            here = nn(weights.astype(BF16), head_lanes(head, v)) * (1.0 / total)
            mixed = here if mixed is None else mixed + here
            logs[pair, block, head : head + 1, :] = (largest + jnp.log(total)).reshape(1, seq)
        pool[3, at, lanes] = mixed.astype(BF16)

    def attend(step, carry):
        steps = BLOCKS // ABREAST
        for number in range(ABREAST):
            attend_one(step // steps, step % steps * ABREAST + number)
        return carry

    lax.fori_loop(0, pairs * BLOCKS // ABREAST, attend, 0)

    for item in (h1_save, *qkv_saves, out_copy, up_copy, down_copy, proj_copy):
        item.wait()

    def feed(tile, carry):
        at = tile_rows(tile)
        a = pool[3, at, :]
        put(6, a, at)
        mid = pool[1, at, :].astype(F32) + nn(a, out_w[...]) + biases[2:3]
        x1[at, :] = mid
        hat, _ = norm_stats(mid)
        h = (hat * gain_two + shift_two).astype(BF16)
        put(5, h, at)
        x2 = mid + biases[3:4]
        for part in range(parts):
            span = slice(part * width, (part + 1) * width)
            u = nn(h, up_w[:, span]) + hidden_ref[:, span].astype(F32)
            acted, slope = gelu_and_slope(u)
            z = acted.astype(BF16)
            eu[part, at, :] = slope.astype(BF16)
            turned = z.T
            for piece in range(16):
                chunk, block = part * 4 + piece // 4, piece % 4
                lefts[1 + block, slot_of(chunk), :, at] = turned[piece * SHARD : (piece + 1) * SHARD]
            x2 = x2 + nn(z, down_w[span, :])
        x2_low = x2.astype(BF16)
        put(0, x2_low, at)
        rows_y = jnp.where(tile_valid(tile), nn(x2_low, proj_w[...]) + biases[4:5], 0.0).astype(BF16)
        per_pair = seq // TILE
        here = pl.ds(pl.multiple_of(tile % per_pair * TILE, TILE), TILE)

        @pl.when(tile // per_pair == tower)
        def _():
            merged[0, here, :] = rows_y

        @pl.when(tile // per_pair != tower)
        def _():
            y_send[here, :] = rows_y

        return carry

    lax.fori_loop(0, tiles, feed, 0)
    y_swap = pltpu.make_async_remote_copy(
        y_send, y_got, tower_sem.at[2], tower_sem.at[3], device_id=by_x, device_id_type=MESH
    )
    y_swap.start()

    g_swap.wait()

    def project_back(tile, carry):
        at = tile_rows(tile)
        g = jnp.where(tile_valid(tile), pool[0, at, :].astype(F32), 0.0)
        g_low = g.astype(BF16)
        pool[0, at, :] = g_low
        dx2 = nt(g_low, proj_w[...])
        pool[2, at, :] = dx2.astype(BF16)
        add_to(3, dx2)
        add_to(4, g)
        return carry

    lax.fori_loop(0, tiles, project_back, 0)

    def bits(block):
        ways = {"y": (by_y, y), "l": (by_lo, z_lo), "h": (by_hi, z_hi)}
        partners, sides = zip(*(ways[letter] for letter in MODES[block]))
        return (by_core, *partners), sides

    def shelf(block):
        if 5 <= block < 9:
            return lefts, block - 4
        return grads, (block if block < 5 else block - 4) % RING

    def shards(block, of_core, first, size):
        buffer, slot = shelf(block)
        return buffer.at[slot, pl.ds(of_core * 8 + first, size), :, pl.ds(0, width)]

    gots = (got_1, got_2, got_3, got_4)

    def place(block, level):
        return block % (CORE_RING, SECOND_RING, BLOCK_COUNT, BLOCK_COUNT)[level]

    def swap_of(block, level):
        partners, (b1, b2, b3) = bits(block)
        if level == 0:
            source = shards(block, 1 - core, 0, 8)
        elif level == 1:
            source = shards(block, core, (1 - b1) * 4, 4)
        elif level == 2:
            source = shards(block, core, b1 * 4 + (1 - b2) * 2, 2)
        else:
            source = shards(block, core, b1 * 4 + b2 * 2 + 1 - b3, 1)
        return pltpu.make_async_remote_copy(
            source,
            gots[level].at[place(block, level)],
            send_sem.at[level, block],
            recv_sem.at[level, block],
            device_id=partners[level],
            device_id_type=MESH,
        )

    def advance(block, level):
        _, (b1, b2, b3) = bits(block)
        buffer, slot = shelf(block)
        swap_of(block, level - 1).wait_recv()
        got = gots[level - 1]
        size = 8 >> level
        bit = (b1, b2, b3)[level - 1]
        base = (0, b1 * 4, b1 * 4 + b2 * 2)[level - 1]
        for other in (1, 0):
            side = (1 - bit) if other else bit

            def add(i, carry, side=side):
                at = side * size + i
                here = core * 8 + base + at
                total = buffer[slot, here, :, :width].astype(F32) + got[place(block, level - 1), at].astype(F32)
                buffer[slot, here, :, :width] = total.astype(BF16)
                return carry

            lax.fori_loop(0, size, add, 0)
            if other:
                if level == 1 and block >= SECOND_RING:
                    assert (block - SECOND_RING, 2) in done
                    pl.semaphore_wait(free_sem.at[1, block], 1)
                swap_of(block, level).start()
        later = block + (CORE_RING, SECOND_RING, BLOCK_COUNT)[level - 1]
        if later < BLOCK_COUNT:
            pl.semaphore_signal(
                free_sem.at[level - 1, later], inc=1, device_id=bits(later)[0][level - 1], device_id_type=MESH
            )

    def sum_copy(block, slot):
        if block == 0:
            target = proj_ref
        elif block < 5:
            target = down_ref.at[pl.ds((block - 1) * SHARD, SHARD)]
        elif block < 9:
            target = up_ref.at[:, pl.ds((block - 5) * width, width)]
        elif block == 9:
            target = out_ref
        else:
            target = qkv_ref.at[:, pl.ds((block - 10) * width, width)]
        return pltpu.make_async_copy(sums.at[slot], target, sum_sem.at[slot])

    finished = []

    def finish(block):
        _, (b1, b2, b3) = bits(block)
        swap_of(block, 3).wait_recv()
        buffer, slot = shelf(block)
        total = buffer[slot, core * 8 + b1 * 4 + b2 * 2 + b3, :, :width].astype(F32) + got_4[block, 0].astype(F32)
        if len(finished) >= 3:
            sum_copy(finished[-3], (len(finished) - 3) % 3).wait()
        place_now = len(finished) % 3
        sums[place_now] = total
        sum_copy(block, place_now).start()
        finished.append(block)
        for level in range(4):
            swap_of(block, level).wait_send()

    done = set()

    def tick(*work):
        for block, level in work:
            assert (block, level) not in done and (level == 1 or (block, level - 1) in done)
            done.add((block, level))
            if level == 4:
                finish(block)
            else:
                advance(block, level)

    def weight_grad(block, number, right):
        assert block < 11 or (block - 11, 4) in done
        assert block < CORE_RING or (block - CORE_RING, 1) in done
        left = lefts[number].reshape(16 * SHARD, count)
        buffer, slot = shelf(block)
        step = 256

        def columns(i, carry):
            at = pl.ds(pl.multiple_of(i * step, step), step)
            product = nn(left, right(at)).astype(BF16).reshape(16, SHARD, step)
            if MODES[block] == "ylh":
                buffer[slot, :, :, at] = product
            else:
                for number in range(16):
                    side = {"y": number // 4 % 2, "l": number // 2 % 2, "h": number % 2}
                    a, b, c = (side[letter] for letter in MODES[block])
                    buffer[slot, number // 8 * 8 + a * 4 + b * 2 + c, :, at] = product[number]
            return carry

        lax.fori_loop(0, width // step, columns, 0)
        if block >= CORE_RING:
            pl.semaphore_wait(free_sem.at[0, block], 1)
        swap_of(block, 0).start()

    weight_grad(0, 0, lambda at: pool[0, :, at])
    tick(*TICKS["proj", 0])
    h1_copy.start()
    for part in range(parts):
        weight_grad(1 + part, 1 + part, lambda at: pool[2, :, at])
        tick(*TICKS["down", part])

    for part in range(parts):

        def tile_du(tile, carry, part=part):
            at = tile_rows(tile)
            du = nt(pool[2, at, :], down_w[part * width : (part + 1) * width, :])
            du = du * eu[part, at, :].astype(F32)
            eu[part, at, :] = du.astype(BF16)
            add_to(9 + part, du)
            return carry

        lax.fori_loop(0, tiles, tile_du, 0)
        tick(*TICKS["du", part])
    for item in qkv_copies:
        item.start()

    for part in range(parts):
        weight_grad(5 + part, 5, lambda at, part=part: eu[part, :, at])
        tick(*TICKS["up", part])

    for number in range(tiles):

        def mid_back(tile, carry):
            at = tile_rows(tile)
            dh = nt(eu[0, at, :], up_w[:, :width])
            for part in range(1, parts):
                dh = dh + nt(eu[part, at, :], up_w[:, part * width : (part + 1) * width])
            hat, scale = norm_stats(x1[at, :])
            dx1 = nt(pool[0, at, :], proj_w[...]) + norm_back(dh, hat, scale, gain_two)
            x1[at, :] = dx1
            e1 = dx1.astype(BF16)
            pool[2, at, :] = e1
            pool[0, at, :] = nt(e1, out_w[...]).astype(BF16)
            add_to(6, dh * hat)
            add_to(8, dh)
            add_to(2, dx1)
            return carry

        lax.fori_loop(number, number + 1, mid_back, 0)
        tick(*TICKS["mid", number])
    qkv_w_again.start()

    weight_grad(9, 6, lambda at: pool[2, :, at])
    tick(*TICKS["out", 0])

    for item in qkv_copies:
        item.wait()
    per_loop = 2
    for turn in range(pairs * BLOCKS // per_loop):

        def attend_back_one(step):
            pair, block = step // BLOCKS, step % BLOCKS
            at = pl.ds(pl.multiple_of(pair * seq, seq), seq)
            lanes = pl.ds(pl.multiple_of(block * LANES, LANES), LANES)
            valid = lax.broadcasted_iota(jnp.int32, (seq, 1), 0) < length(pair)
            q, k, v = (
                down_w[pl.ds(pl.multiple_of(number * count + pair * seq, seq), seq), lanes] for number in range(3)
            )
            d = pool[0, at, lanes]
            log_rows = logs[pair, block]
            k_t = k.T
            d_t = d.T
            prod_t = d_t.astype(F32) * pool[3, at, lanes].T.astype(F32)
            dq_rows = []
            dk = None
            dv = None
            for head in range(2):
                span = slice(head * HEAD_DIM, (head + 1) * HEAD_DIM)
                row_dot = jnp.sum(prod_t[span], 0, keepdims=True)
                v_here = head_lanes(head, v)
                dq_parts = []
                for start in range(0, seq, QUERIES):
                    some = slice(start, start + QUERIES)
                    q_here = head_lanes(head, q[some])
                    scores = jnp.where(valid, nt(k, q_here), masked_score)
                    probs = jnp.exp(scores - log_rows[head : head + 1, some])
                    d_probs = nn(v_here, d_t[:, some])
                    d_scores = (probs * (d_probs - row_dot[:, some])).astype(BF16)
                    dv_here = nn(probs.astype(BF16), head_lanes(head, d[some]))
                    dk_here = nn(d_scores, q_here)
                    dq_parts.append(nn(k_t[span], d_scores))
                    dk = dk_here if dk is None else dk + dk_here
                    dv = dv_here if dv is None else dv + dv_here
                dq_rows.append(jnp.concatenate(dq_parts, 1))
            dq = jnp.concatenate(dq_rows, 0).T * HEAD_DIM**-0.5
            for number, value in ((0, dq), (1, dk), (2, dv)):
                eu[number, at, lanes] = value.astype(BF16)
            add_to(0, dq, lanes)
            add_to(1, dv, lanes)

        def attend_back(step, carry):
            for number in range(per_loop):
                attend_back_one(step * per_loop + number)
            return carry

        lax.fori_loop(turn, turn + 1, attend_back, 0)
        tick(*TICKS["attend", turn])

    h1_copy.wait()
    for part in range(3):
        weight_grad(10 + part, 0, lambda at, part=part: eu[part, :, at])
        tick(*TICKS["qkv", part])

    qkv_w_again.wait()
    for number in range(tiles):

        def first_back(tile, carry):
            at = tile_rows(tile)
            dh = nt(eu[0, at, :], up_w[:, :width])
            for part in (1, 2):
                dh = dh + nt(eu[part, at, :], up_w[:, part * width : (part + 1) * width])
            hat, scale = norm_stats(pool[1, at, :].astype(F32))
            pool[0, at, :] = (x1[at, :] + norm_back(dh, hat, scale, gain_one)).astype(BF16)
            add_to(5, dh * hat)
            add_to(7, dh)
            return carry

        lax.fori_loop(number, number + 1, first_back, 0)
        tick(*TICKS["first", number])
    tokens_copy.start()

    def vec_swap(level):
        return pltpu.make_async_remote_copy(
            vec.at[level],
            vec_got.at[level],
            vec_send.at[level],
            vec_recv.at[level],
            device_id=(by_core, by_y, by_lo, by_hi, by_x)[level],
            device_id_type=MESH,
        )

    vec_swap(0).start()

    y_swap.wait()

    def projected(side, start, size):
        own = merged[0, start : start + size, :].astype(F32)
        got = y_got[start : start + size, :].astype(F32)
        return jnp.where(tower == side, own, got)

    merged[0, 2 * seq : 2 * seq + 1, :] = projected(1, seq - 16, 16)[15:16].astype(BF16)
    for side in (1, 0):
        for start in range(seq - strip, -1, -strip):
            value = projected(side, start, strip)
            if start > 0:
                before = projected(side, start - 16, 16)[15:16]
            elif side == 1:
                before = projected(0, seq - 16, 16)[15:16]
            else:
                before = cls_row_ref[...].reshape(1, width).astype(F32)
            moved = jnp.where(row == 0, before, pltpu.roll(value, 1, 0))
            merged[0, side * seq + start : side * seq + start + strip, :] = moved.astype(BF16)
    merged_copy.start()

    for number, work in enumerate(TICKS["tail", 0]):
        tick(work)
        if number < 4:
            vec_swap(number).wait_recv()
            vec[number + 1] = vec[number] + vec_got[number]
            vec_swap(number + 1).start()
    vec_swap(4).wait_recv()
    vec_ref[0:13] = vec[4, 0:13]
    vec_ref[13:16] = vec[4, 13:16] + vec_got[4, 13:16]
    for level in range(5):
        vec_swap(level).wait_send()
    for number in range(BLOCK_COUNT - 3, BLOCK_COUNT):
        sum_copy(finished[number], number % 3).wait()
    tokens_copy.wait()
    merged_copy.wait()
    assert len(done) == 4 * BLOCK_COUNT


TICKS = {
    ('proj', 0): [],
    ('down', 0): [],
    ('down', 1): [],
    ('down', 2): [(0, 1)],
    ('down', 3): [(1, 1)],
    ('du', 0): [(2, 1), (3, 1)],
    ('du', 1): [(4, 1)],
    ('du', 2): [(0, 2)],
    ('du', 3): [(1, 2)],
    ('up', 0): [],
    ('up', 1): [(0, 3)],
    ('up', 2): [(2, 2), (5, 1)],
    ('up', 3): [(6, 1)],
    ('mid', 0): [(0, 4), (7, 1), (2, 3), (8, 1)],
    ('mid', 1): [(3, 2)],
    ('mid', 2): [],
    ('mid', 3): [(4, 2), (6, 2), (2, 4)],
    ('out', 0): [],
    ('attend', 0): [(1, 3), (3, 3), (9, 1)],
    ('attend', 1): [(4, 3), (5, 2), (1, 4)],
    ('attend', 2): [(3, 4)],
    ('attend', 3): [(7, 2), (9, 2), (4, 4)],
    ('attend', 4): [(5, 3), (8, 2)],
    ('attend', 5): [(6, 3), (7, 3)],
    ('qkv', 0): [(5, 4)],
    ('qkv', 1): [(9, 3), (8, 3)],
    ('qkv', 2): [(10, 1), (6, 4)],
    ('first', 0): [(11, 1)],
    ('first', 1): [(7, 4), (12, 1)],
    ('first', 2): [(9, 4)],
    ('first', 3): [(10, 2)],
    ('tail', 0): [(8, 4), (11, 2), (10, 3), (12, 2), (11, 3), (10, 4), (12, 3), (11, 4), (12, 4)],
}


def run_one(group_id, caption_len, gains, shifts, biases, hidden, cls_row, x, g, qkv_w, out_w, up_w, down_w, proj_w):
    count, width = x.shape
    ff = up_w.shape[1]
    pairs = group_id.shape[0]
    seq = count // pairs
    shard = jax.ShapeDtypeStruct
    vmem = pl.BlockSpec(memory_space=pltpu.VMEM)
    hbm = pl.BlockSpec(memory_space=pl.ANY)
    return pl.pallas_call(
        one_kernel,
        in_specs=[pl.BlockSpec(memory_space=pltpu.SMEM)] * 2 + [vmem] * 5 + [hbm] * 7,
        out_specs=[hbm] * 5 + [vmem] + [hbm] * 4,
        out_shape=[
            shard((SHARD, width), F32),
            shard((4 * SHARD, width), F32),
            shard((SHARD, ff), F32),
            shard((SHARD, width), F32),
            shard((SHARD, 3 * width), F32),
            shard((VECTORS, width), F32),
            shard((count, width), BF16),
            shard(g.shape, BF16),
            shard((3, count, width), BF16),
            shard((16, SHARD, count), BF16),
        ],
        scratch_shapes=[
            pltpu.VMEM((RING, 16, SHARD, width), BF16),
            pltpu.VMEM((CORE_RING, 8, SHARD, width), BF16),
            pltpu.VMEM((SECOND_RING, 4, SHARD, width), BF16),
            pltpu.VMEM((BLOCK_COUNT, 2, SHARD, width), BF16),
            pltpu.VMEM((BLOCK_COUNT, 1, SHARD, width), BF16),
            pltpu.VMEM((7, 16, SHARD, count), BF16),
            pltpu.VMEM((4, count, width), BF16),
            pltpu.VMEM((ff // width, count, width), BF16),
            pltpu.VMEM((ff, width), BF16),
            pltpu.VMEM((width, ff), BF16),
            pltpu.VMEM((width, width), BF16),
            pltpu.VMEM((width, width), BF16),
            pltpu.VMEM((count, width), F32),
            pltpu.VMEM((pairs, BLOCKS, 2, seq), F32),
            pltpu.VMEM((5, VECTORS, width), F32),
            pltpu.VMEM((5, VECTORS, width), F32),
            pltpu.VMEM((seq, width), BF16),
            pltpu.VMEM((seq, width), BF16),
            pltpu.VMEM(g.shape, BF16),
            pltpu.VMEM((3, SHARD, width), F32),
            pltpu.SemaphoreType.DMA((4, BLOCK_COUNT)),
            pltpu.SemaphoreType.DMA((4, BLOCK_COUNT)),
            pltpu.SemaphoreType.DMA((20,)),
            pltpu.SemaphoreType.DMA((3,)),
            pltpu.SemaphoreType.DMA((5,)),
            pltpu.SemaphoreType.DMA((5,)),
            pltpu.SemaphoreType.DMA((4,)),
            pltpu.SemaphoreType.REGULAR((2, BLOCK_COUNT)),
        ],
        compiler_params=pltpu.CompilerParams(
            collective_id=0, has_side_effects=True, vmem_limit_bytes=63 * MIB
        ),
        cost_estimate=cost(60e9, 60 * MIB),
        name="one",
    )(group_id, caption_len, gains, shifts, biases, hidden, cls_row, x, g, qkv_w, out_w, up_w, down_w, proj_w)


def full_grad_kernel(left_ref, *refs):
    start = 0
    for right_ref in refs[:-1]:
        stop = start + right_ref.shape[1]
        refs[-1][:, start:stop] = nn(left_ref[...], right_ref[...])
        start = stop


def run_full_grad(left, *rights):
    height, count = left.shape
    width = sum(right.shape[1] for right in rights)
    tile = 384
    return pl.pallas_call(
        full_grad_kernel,
        grid=(height // tile,),
        in_specs=[rows(tile, count)] + [whole(right.shape) for right in rights],
        out_specs=rows(tile, width),
        out_shape=jax.ShapeDtypeStruct((height, width), F32),
        compiler_params=params(),
        name="full_grad",
    )(left, *rights)


def in_order(slabs):
    return jnp.stack([slabs[..., slot_of(chunk), :, :] for chunk in range(16)], -3)


def plain_back(lengths, logs, gains, feed_sums, cls_sum, left, h1, slope, g, e2, dx2, x1, a, qkv, x, y, down_w, up_w, out_w, qkv_w):
    count, width = x.shape
    seq = y.shape[2]
    eu, dx1, e1, da, hidden_sum, mid_sums = run_feed_back(e2, dx2, slope, x1, gains, out_w, up_w, down_w)
    dq, dk, dv, sum_q, sum_v = run_attend_back(lengths, qkv, a, da, logs, seq)
    tokens_grad, first_sums = run_qkv_back(dq, dk, dv, dx1, x, gains, qkv_w)
    turned = in_order(left)
    z = turned[1:5].transpose(1, 0, 2, 3).reshape(4 * width, count)
    x2, h2, a_t = (turned[i].reshape(width, count) for i in (0, 5, 6))
    h1 = in_order(h1).reshape(width, count)
    grads = (run_full_grad(x2, g), run_full_grad(z, e2), run_full_grad(h2, eu), run_full_grad(a_t, e1), run_full_grad(h1, dq, dk, dv))
    grads = [lax.psum_scatter(grad, "dp", scatter_dimension=0, tiled=True) for grad in grads]
    vectors = jnp.concatenate(
        [
            jnp.sum(sum_q, 0), jnp.sum(sum_v, 0), mid_sums[2:3], feed_sums, first_sums[0:1], mid_sums[0:1],
            first_sums[1:2], mid_sums[1:2], hidden_sum.reshape(-1, width),
        ],
        axis=0,
    )
    vectors = lax.psum(vectors, "dp")
    cls = lax.psum(cls_sum, ("tower", "dp"))
    y_got = lax.ppermute(take(y, 1 - lax.axis_index("tower")), "tower", [(0, 1), (1, 0)])
    return grads, vectors, cls, tokens_grad, y_got


def take(value, index):
    return lax.dynamic_index_in_dim(value, index, 0, keepdims=False)


PIECE = 256


def spread_kernel(index_ref, vec_ref, *refs):
    sources, (gain_ref, shift_ref, bias_ref, hidden_ref, cls_ref), targets, held = refs[:7], refs[7:12], refs[12:19], refs[19:26]
    sem_in, sem_out = refs[26:]
    ins, outs = [], []
    for source, there, target in zip(sources, held, targets):
        size = source.shape[0]
        step = PIECE if size % PIECE == 0 else size
        for start in range(0, size, step):
            number, at = len(ins), pl.ds(start, step)
            ins.append(pltpu.make_async_copy(source.at[at], there.at[at], sem_in.at[number]))
            outs.append(pltpu.make_async_copy(there.at[at], target.at[at], sem_out.at[number]))
    for item in ins:
        item.start()
    index = index_ref[0]
    width = vec_ref.shape[1]
    piece = gain_ref.shape[1]
    mine = pltpu.roll(vec_ref[...], width - piece * index, 1)[:, :piece]
    for number in range(5):
        bias_ref[number] = mine[number : number + 1]
    gain_ref[...] = mine[5:7]
    shift_ref[...] = mine[7:9]
    share = hidden_ref.shape[1]
    per_row = width // share
    row = vec_ref[pl.ds(9 + index // per_row, 1), :]
    hidden_ref[...] = pltpu.roll(row, width - share * (index % per_row), 1)[:, :share]
    cls_ref[...] = vec_ref[13]
    for before, after in zip(ins, outs):
        before.wait()
        after.start()
    for item in outs:
        item.wait()


def run_spread(index, vectors, *arrays):
    width = vectors.shape[1]
    small = [jax.ShapeDtypeStruct(shape, F32) for shape in ((2, width // 16), (2, width // 16), (5, 1, width // 16), (1, width // 4), (width,))]
    vmem = pl.BlockSpec(memory_space=pltpu.VMEM)
    hbm = pl.BlockSpec(memory_space=pl.ANY)
    return pl.pallas_call(
        spread_kernel,
        in_specs=[pl.BlockSpec(memory_space=pltpu.SMEM), vmem] + [hbm] * len(arrays),
        out_specs=[vmem] * 5 + [hbm] * len(arrays),
        out_shape=small + [jax.ShapeDtypeStruct(array.shape, array.dtype) for array in arrays],
        scratch_shapes=[pltpu.VMEM(array.shape, array.dtype) for array in arrays]
        + [pltpu.SemaphoreType.DMA((16,))] * 2,
        compiler_params=params(62),
        name="spread",
    )(index, vectors, *arrays)


def local(
    dp, tokens, group_id, caption_len, cls_row, norm_gains, shifts, bias_model, bias_hidden,
    w_qkv, w_out, w_up, w_down, w_proj, merged_grad,
):
    tower = lax.axis_index("tower")
    index = lax.axis_index("dp")
    pairs, seq, width = tokens.shape[1:]
    half = pairs // 2
    count = pairs * seq
    image_len = jnp.where(group_id == 1, IMG_LARGE, IMG_SMALL)
    lengths = jnp.where(tower == 0, image_len, caption_len).astype(jnp.int32)
    gains, shift_rows, biases, hidden = norm_gains[0], shifts[0], bias_model[0], bias_hidden
    qkv_w, out_w, up_w, down_w, proj_w = w_qkv[0], w_out[0], w_up[0], w_down[0], w_proj[0]
    x = tokens[0].reshape(count, width)

    if dp == 16 and pairs == 2:
        *grads, vectors, tokens_grad, merged_input, _, _ = run_one(
            group_id, caption_len, gains, shift_rows, biases, hidden, cls_row, x, merged_grad[0], qkv_w, out_w, up_w, down_w, proj_w
        )
        gain_sum, shift_sum, bias_sum, hidden_sum, cls, *arrays = run_spread(
            index.astype(jnp.int32)[None], vectors, *grads, tokens_grad, merged_input
        )
        bias_sum = bias_sum.transpose(1, 0, 2)[0]
        proj, down, up, out, qkv_grad, tokens_grad, merged_input = arrays
    else:
        positions = lax.broadcasted_iota(jnp.int32, (pairs, seq), 1)
        valid = (positions < lengths[:, None]).reshape(count, 1).astype(F32)
        image_grad = merged_grad[0, :, 1 : 1 + seq]
        text_grad = merged_grad[0, :, 1 + seq :]
        g_keep = jnp.where(tower == 0, image_grad, text_grad)
        g_send = jnp.where(tower == 0, text_grad, image_grad)
        g_got = lax.ppermute(g_send, "tower", [(0, 1), (1, 0)])
        cls_sum = jnp.sum(merged_grad[0, :, 0].astype(F32), 0)[None]
        h1, qkv = run_qkv(x, gains, shift_rows, biases, qkv_w)
        mixed, logs = run_attend(lengths, qkv, seq)
        g = jnp.where(tower == 0, jnp.stack([g_keep, g_got]), jnp.stack([g_got, g_keep])).reshape(count, width)
        x1, left, slope, y, g_low, dx2, e2, feed_sums = run_feed(
            valid, x, mixed, g, gains, shift_rows, biases, hidden, out_w, up_w, down_w, proj_w
        )
        y = y.reshape(2, half, seq, width)
        grads, vectors, cls, tokens_grad, y_got = plain_back(
            lengths, logs, gains, feed_sums, cls_sum, left, h1, slope, g_low, e2, dx2, x1, mixed, qkv, x, y,
            down_w, up_w, out_w, qkv_w,
        )
        proj, down, up, out, qkv_grad = grads
        y_own = take(y, tower)
        cls_block = jnp.broadcast_to(cls_row.reshape(1, 1, width), (half, 1, width))
        image_rows = jnp.where(tower == 0, y_own, y_got)
        text_rows = jnp.where(tower == 0, y_got, y_own)
        merged_input = jnp.concatenate([cls_block, image_rows, text_rows], axis=1)
        mine = lax.dynamic_slice_in_dim(vectors[:9], index * (width // dp), width // dp, 1)
        bias_sum, gain_sum, shift_sum = mine[0:5], mine[5:7], mine[7:9]
        ff = up_w.shape[1]
        hidden_sum = lax.dynamic_slice_in_dim(vectors[9:13].reshape(1, ff), index * (ff // dp), ff // dp, 1)
    return (
        merged_input[None], tokens_grad.reshape(tokens.shape), cls.reshape(width), gain_sum[None], shift_sum[None],
        bias_sum[None], hidden_sum, qkv_grad[None], out[None], up[None], down[None], proj[None],
    )


def solution(mesh):
    tower = P("tower", None, None)
    in_specs = (
        P("tower", "dp", None, None), P("dp"), P("dp"), P(), tower, tower, tower, P("tower", None),
        tower, tower, tower, tower, tower, P("tower", "dp", None, None),
    )
    spread = P("tower", None, "dp")
    weight = P("tower", "dp", None)
    out_specs = (
        P("tower", "dp", None, None), P("tower", "dp", None, None), P(), spread, spread, spread, P("tower", "dp"),
        weight, weight, weight, weight, weight,
    )
    return jax.shard_map(
        partial(local, mesh.shape["dp"]), mesh=mesh, in_specs=in_specs, out_specs=out_specs, check_vma=False
    )
```

```python
from functools import partial

import jax
import jax.numpy as jnp
from jax import lax
from jax.experimental import pallas as pl
from jax.experimental.pallas import tpu as pltpu
from jax.sharding import PartitionSpec as P

HEADS = 12
HEAD_DIM = 64
IMG_SMALL = 197
IMG_LARGE = 325
LANES = 128
BLOCKS = HEADS * HEAD_DIM // LANES

norm_eps = 1e-06
masked_score = -1e30
F32 = jnp.float32
BF16 = jnp.bfloat16
MIB = 1 << 20
SHARD = 48

ERF_P = 0.39
ERF_C = (0.2344334842, 0.09695712066, 0.6357617632, -0.6184387086, 0.8763152235, -0.225028871)


def nn(left, right):
    return jnp.dot(left, right, preferred_element_type=F32)


def nt(left, right):
    return lax.dot_general(left, right, (((1,), (1,)), ((), ())), preferred_element_type=F32)


def tn(left, right):
    return lax.dot_general(left, right, (((0,), (0,)), ((), ())), preferred_element_type=F32)


def params(vmem=48, semantics=None):
    return pltpu.CompilerParams(vmem_limit_bytes=vmem * MIB, dimension_semantics=semantics)


def cost(flops, nbytes, trans=0):
    return pl.CostEstimate(flops=int(flops), bytes_accessed=int(nbytes), transcendentals=int(trans))


def whole(shape):
    return pl.BlockSpec(shape, lambda *_: (0,) * len(shape), pipeline_mode=pl.Buffered(1))


def rows(tile, width):
    return pl.BlockSpec((tile, width), lambda i, *_: (i, 0))


def norm_stats(x):
    mean = jnp.mean(x, -1, keepdims=True)
    centred = x - mean
    spread = jnp.mean(centred * centred, -1, keepdims=True)
    scale = lax.rsqrt(spread + norm_eps)
    return centred * scale, scale


def norm_back(grad, hat, scale, gain):
    d_hat = grad * gain
    first = jnp.mean(d_hat, -1, keepdims=True)
    second = jnp.mean(d_hat * hat, -1, keepdims=True)
    return scale * (d_hat - first - hat * second)


def gelu_and_slope(u):
    bell = jnp.exp2(u * u * (-0.5 * 1.4426950408889634))
    t = 1.0 / (1.0 + (ERF_P * 0.5**0.5) * jnp.abs(u))
    poly = jnp.full_like(u, 0.5 * ERF_C[-1])
    for c in ERF_C[-2::-1]:
        poly = poly * t + 0.5 * c
    tail = poly * t * bell
    phi = jnp.where(u >= 0, 1.0 - tail, tail)
    slope = phi + u * bell * 0.3989422804014327
    return u * phi, slope


def slot_of(chunk):
    z_hi, z_lo, y, core = chunk // 8, chunk // 4 % 2, chunk // 2 % 2, chunk % 2
    return ((core * 2 + y) * 2 + z_lo) * 2 + z_hi


def put_slabs(ref, lead, value):
    turned = value.T
    for chunk in range(16):
        ref[(*lead, slot_of(chunk))] = turned[chunk * SHARD : (chunk + 1) * SHARD]


def add_sum(ref, index, value, first):
    ref[index : index + 1, :] = jnp.where(first, 0.0, ref[index : index + 1, :]) + jnp.sum(value, 0, keepdims=True)


def qkv_kernel(x_ref, gain_ref, shift_ref, bias_ref, w_ref, h_ref, out_ref):
    width = x_ref.shape[1]
    hat, _ = norm_stats(x_ref[...].astype(F32))
    h = (hat * gain_ref[0:1].astype(F32) + shift_ref[0:1].astype(F32)).astype(BF16)
    put_slabs(h_ref, (), h)
    q = nn(h, w_ref[:, :width]) + bias_ref[0:1].astype(F32)
    out_ref[:, :width] = q.astype(BF16) * BF16(HEAD_DIM**-0.5)
    out_ref[:, width : 2 * width] = nn(h, w_ref[:, width : 2 * width]).astype(BF16)
    v = nn(h, w_ref[:, 2 * width :]) + bias_ref[1:2].astype(F32)
    out_ref[:, 2 * width :] = v.astype(BF16)


def run_qkv(x, gains, shifts, biases, w, tile=256):
    count, width = x.shape
    return pl.pallas_call(
        qkv_kernel,
        grid=(count // tile,),
        in_specs=[rows(tile, width), whole(gains.shape), whole(shifts.shape), whole(biases.shape), whole(w.shape)],
        out_specs=[pl.BlockSpec((16, SHARD, tile), lambda i: (0, 0, i)), rows(tile, 3 * width)],
        out_shape=[
            jax.ShapeDtypeStruct((16, SHARD, count), BF16),
            jax.ShapeDtypeStruct((count, 3 * width), BF16),
        ],
        compiler_params=params(),
        cost_estimate=cost(6 * count * width * width, 2 * (count * width * 5 + 3 * width * width)),
        name="qkv",
    )(x, gains, shifts, biases, w)


def head_lanes(head, block):
    lane = lax.broadcasted_iota(jnp.int32, (1, LANES), 1)
    keep = (lane < HEAD_DIM) if head == 0 else (lane >= HEAD_DIM)
    return jnp.where(keep, block, jnp.zeros_like(block))


def attend_kernel(len_ref, q_ref, k_ref, v_ref, a_ref, l_ref):
    seq = q_ref.shape[0]
    valid = lax.broadcasted_iota(jnp.int32, (seq, 1), 0) < len_ref[pl.program_id(0)]
    q = q_ref[...]
    k = k_ref[...]
    v_t = v_ref[...].T
    parts = []
    for head in range(2):
        scores = jnp.where(valid, nt(k, head_lanes(head, q)), masked_score)
        largest = jnp.max(scores, 0, keepdims=True)
        weights = jnp.exp(scores - largest)
        total = jnp.sum(weights, 0, keepdims=True)
        mixed = nn(v_t[head * HEAD_DIM : (head + 1) * HEAD_DIM], weights.astype(BF16))
        parts.append((mixed * (1.0 / total)).astype(BF16))
        l_ref[0, 0, head : head + 1, :] = largest + jnp.log(total)
    a_ref[...] = jnp.concatenate(parts, 0).T


def column(seq, shift):
    return pl.BlockSpec((seq, LANES), lambda p, b, *_: (p, b + shift))


def run_attend(lengths, qkv, seq):
    count = qkv.shape[0]
    width = qkv.shape[1] // 3
    pairs = count // seq
    return pl.pallas_call(
        attend_kernel,
        grid_spec=pltpu.PrefetchScalarGridSpec(
            num_scalar_prefetch=1,
            grid=(pairs, BLOCKS),
            in_specs=[column(seq, 0), column(seq, BLOCKS), column(seq, 2 * BLOCKS)],
            out_specs=[column(seq, 0), pl.BlockSpec((1, 1, 2, seq), lambda p, b, *_: (p, b, 0, 0))],
        ),
        out_shape=[
            jax.ShapeDtypeStruct((count, width), BF16),
            jax.ShapeDtypeStruct((pairs, BLOCKS, 2, seq), F32),
        ],
        compiler_params=params(),
        cost_estimate=cost(16 * pairs * HEADS * seq * seq * HEAD_DIM, 8 * count * width, pairs * HEADS * seq * seq),
        name="attend",
    )(lengths, qkv, qkv, qkv)


def attend_back_kernel(len_ref, q_ref, k_ref, v_ref, a_ref, d_ref, l_ref, dq_ref, dk_ref, dv_ref, sq_ref, sv_ref):
    seq = q_ref.shape[0]
    valid = lax.broadcasted_iota(jnp.int32, (seq, 1), 0) < len_ref[pl.program_id(0)]
    q = q_ref[...]
    k = k_ref[...]
    v = v_ref[...]
    d = d_ref[...]
    k_t = k.T
    d_t = d.T
    prod_t = d_t.astype(F32) * a_ref[...].T.astype(F32)
    dq_parts = []
    dk = None
    dv = None
    for head in range(2):
        span = slice(head * HEAD_DIM, (head + 1) * HEAD_DIM)
        q_here = head_lanes(head, q)
        scores = jnp.where(valid, nt(k, q_here), masked_score)
        probs = jnp.exp(scores - l_ref[0, 0, head : head + 1, :])
        row_dot = jnp.sum(prod_t[span], 0, keepdims=True)
        d_probs = nn(head_lanes(head, v), d_t)
        d_scores = (probs * (d_probs - row_dot)).astype(BF16)
        dv_here = nn(probs.astype(BF16), head_lanes(head, d))
        dk_here = nn(d_scores, q_here)
        dq_parts.append(nn(k_t[span], d_scores))
        dk = dk_here if dk is None else dk + dk_here
        dv = dv_here if dv is None else dv + dv_here
    dq = jnp.concatenate(dq_parts, 0).T * HEAD_DIM**-0.5
    dq_ref[...] = dq.astype(BF16)
    dk_ref[...] = dk.astype(BF16)
    dv_ref[...] = dv.astype(BF16)
    sq_ref[0] = jnp.sum(dq, 0, keepdims=True)
    sv_ref[0] = jnp.sum(dv, 0, keepdims=True)


def run_attend_back(lengths, qkv, mixed, d_mixed, log_total, seq):
    count = qkv.shape[0]
    width = qkv.shape[1] // 3
    pairs = count // seq
    sums = pl.BlockSpec((1, 1, LANES), lambda p, b, *_: (p, 0, b))
    return pl.pallas_call(
        attend_back_kernel,
        grid_spec=pltpu.PrefetchScalarGridSpec(
            num_scalar_prefetch=1,
            grid=(pairs, BLOCKS),
            in_specs=[
                column(seq, 0),
                column(seq, BLOCKS),
                column(seq, 2 * BLOCKS),
                column(seq, 0),
                column(seq, 0),
                pl.BlockSpec((1, 1, 2, seq), lambda p, b, *_: (p, b, 0, 0)),
            ],
            out_specs=[column(seq, 0)] * 3 + [sums] * 2,
        ),
        out_shape=[jax.ShapeDtypeStruct((count, width), BF16)] * 3
        + [jax.ShapeDtypeStruct((pairs, 1, width), F32)] * 2,
        compiler_params=params(),
        cost_estimate=cost(40 * pairs * HEADS * seq * seq * HEAD_DIM, 16 * count * width, pairs * HEADS * seq * seq),
        name="attend_back",
    )(lengths, qkv, qkv, qkv, mixed, d_mixed, log_total)


def feed_kernel(
    valid_ref, x_ref, a_ref, g_ref, gain_ref, shift_ref, bias_ref, hidden_ref, out_w, up_w, down_w, proj_w,
    x1_ref, left_ref, slope_ref, y_ref, gm_ref, dx2_ref, e2_ref, sum_ref,
):
    width = x_ref.shape[1]
    first = pl.program_id(0) == 0
    valid = valid_ref[...]
    a = a_ref[...]
    put_slabs(left_ref, (6,), a)
    x1 = x_ref[...].astype(F32) + nn(a, out_w[...]) + bias_ref[2:3].astype(F32)
    x1_ref[...] = x1
    hat, _ = norm_stats(x1)
    h = (hat * gain_ref[1:2].astype(F32) + shift_ref[1:2].astype(F32)).astype(BF16)
    put_slabs(left_ref, (5,), h)
    x2 = x1 + bias_ref[3:4].astype(F32)
    for part in range(up_w.shape[1] // width):
        span = slice(part * width, (part + 1) * width)
        u = nn(h, up_w[:, span]) + hidden_ref[:, span].astype(F32)
        acted, slope = gelu_and_slope(u)
        z = acted.astype(BF16)
        slope_ref[:, span] = slope.astype(BF16)
        turned = z.T
        for piece in range(16):
            chunk, block = part * 4 + piece // 4, piece % 4
            left_ref[1 + block, slot_of(chunk)] = turned[piece * SHARD : (piece + 1) * SHARD]
        x2 = x2 + nn(z, down_w[span, :])
    x2_low = x2.astype(BF16)
    put_slabs(left_ref, (0,), x2_low)
    y_ref[...] = ((nn(x2_low, proj_w[...]) + bias_ref[4:5].astype(F32)) * valid).astype(BF16)
    g = g_ref[...].astype(F32) * valid
    g_low = g.astype(BF16)
    gm_ref[...] = g_low
    dx2 = nt(g_low, proj_w[...])
    dx2_ref[...] = dx2
    e2_ref[...] = dx2.astype(BF16)
    add_sum(sum_ref, 0, dx2, first)
    add_sum(sum_ref, 1, g, first)


def run_feed(valid, x, a, g, gains, shifts, biases, hidden, out_w, up_w, down_w, proj_w, tile=256):
    count, width = x.shape
    ff = up_w.shape[1]
    low = jax.ShapeDtypeStruct((count, width), BF16)
    full = jax.ShapeDtypeStruct((count, width), F32)
    weights = (gains, shifts, biases, hidden, out_w, up_w, down_w, proj_w)
    return pl.pallas_call(
        feed_kernel,
        grid=(count // tile,),
        in_specs=[rows(tile, 1)] + [rows(tile, width)] * 3 + [whole(w.shape) for w in weights],
        out_specs=[
            rows(tile, width), pl.BlockSpec((7, 16, SHARD, tile), lambda i: (0, 0, 0, i)), rows(tile, ff),
            rows(tile, width), rows(tile, width), rows(tile, width), rows(tile, width), whole((2, width)),
        ],
        out_shape=[
            full, jax.ShapeDtypeStruct((7, 16, SHARD, count), BF16), jax.ShapeDtypeStruct((count, ff), BF16),
            low, low, full, low, jax.ShapeDtypeStruct((2, width), F32),
        ],
        compiler_params=params(60),
        cost_estimate=cost(2 * count * width * (3 * width + 2 * ff), count * (width * 24 + ff * 6) + 11 * MIB),
        name="feed",
    )(valid, x, a, g, *weights)


def feed_back_kernel(
    e2_ref, dx2_ref, slope_ref, x1_ref, gain_ref, out_w, up_w, down_w,
    eu_ref, dx1_ref, e1_ref, da_ref, hid_ref, sum_ref,
):
    width = e2_ref.shape[1]
    first = pl.program_id(0) == 0
    e2 = e2_ref[...]
    dh = None
    for start in range(0, up_w.shape[1], width):
        span = slice(start, start + width)
        du = nt(e2, down_w[span, :]) * slope_ref[:, span].astype(F32)
        eu = du.astype(BF16)
        eu_ref[:, span] = eu
        hid_ref[:, span] = jnp.where(first, 0.0, hid_ref[:, span]) + jnp.sum(du, 0, keepdims=True)
        part = nt(eu, up_w[:, span])
        dh = part if dh is None else dh + part
    hat, scale = norm_stats(x1_ref[...])
    dx1 = dx2_ref[...] + norm_back(dh, hat, scale, gain_ref[1:2].astype(F32))
    dx1_ref[...] = dx1
    e1 = dx1.astype(BF16)
    e1_ref[...] = e1
    da_ref[...] = nt(e1, out_w[...]).astype(BF16)
    add_sum(sum_ref, 0, dh * hat, first)
    add_sum(sum_ref, 1, dh, first)
    add_sum(sum_ref, 2, dx1, first)


def run_feed_back(e2, dx2, slope, x1, gains, out_w, up_w, down_w, tile=256):
    count, width = x1.shape
    ff = up_w.shape[1]
    low = jax.ShapeDtypeStruct((count, width), BF16)
    return pl.pallas_call(
        feed_back_kernel,
        grid=(count // tile,),
        in_specs=[rows(tile, width), rows(tile, width), rows(tile, ff), rows(tile, width)]
        + [whole(w.shape) for w in (gains, out_w, up_w, down_w)],
        out_specs=[rows(tile, ff), rows(tile, width), rows(tile, width), rows(tile, width), whole((1, ff)), whole((3, width))],
        out_shape=[
            jax.ShapeDtypeStruct((count, ff), BF16),
            jax.ShapeDtypeStruct((count, width), F32),
            low,
            low,
            jax.ShapeDtypeStruct((1, ff), F32),
            jax.ShapeDtypeStruct((3, width), F32),
        ],
        compiler_params=params(60),
        cost_estimate=cost(2 * count * width * (width + 2 * ff), count * (width * 18 + ff * 6) + 10 * MIB),
        name="feed_back",
    )(e2, dx2, slope, x1, gains, out_w, up_w, down_w)


def qkv_back_kernel(dq_ref, dk_ref, dv_ref, dx1_ref, x_ref, gain_ref, w_ref, out_ref, sum_ref):
    width = x_ref.shape[1]
    first = pl.program_id(0) == 0
    dh = nt(dq_ref[...], w_ref[:, :width])
    dh = dh + nt(dk_ref[...], w_ref[:, width : 2 * width])
    dh = dh + nt(dv_ref[...], w_ref[:, 2 * width :])
    hat, scale = norm_stats(x_ref[...].astype(F32))
    out_ref[...] = (dx1_ref[...] + norm_back(dh, hat, scale, gain_ref[0:1].astype(F32))).astype(BF16)
    add_sum(sum_ref, 0, dh * hat, first)
    add_sum(sum_ref, 1, dh, first)


def run_qkv_back(dq, dk, dv, dx1, x, gains, w, tile=256):
    count, width = x.shape
    return pl.pallas_call(
        qkv_back_kernel,
        grid=(count // tile,),
        in_specs=[rows(tile, width)] * 5 + [whole(gains.shape), whole(w.shape)],
        out_specs=[rows(tile, width), whole((2, width))],
        out_shape=[jax.ShapeDtypeStruct((count, width), BF16), jax.ShapeDtypeStruct((2, width), F32)],
        compiler_params=params(),
        cost_estimate=cost(6 * count * width * width, count * width * 14 + 6 * width * width),
        name="qkv_back",
    )(dq, dk, dv, dx1, x, gains, w)


BLOCK_COUNT = 13
RING = 6
CORE_RING = 4
SECOND_RING = 8
MODES = ('lhy', 'ylh', 'lyh', 'ylh', 'ylh', 'lyh', 'ylh', 'ylh', 'lyh', 'ylh', 'ylh', 'lyh', 'ylh')
QUERIES = 256
ABREAST = 3
VECTORS = 16
TILE = 256
MESH = pl.DeviceIdType.MESH


def one_kernel(
    group_ref, caption_ref, gain_ref, shift_ref, bias_ref, hidden_ref, cls_row_ref,
    x_hbm, g_hbm, qkv_w_hbm, out_hbm, up_hbm, down_hbm, proj_hbm,
    proj_ref, down_ref, up_ref, out_ref, qkv_ref, vec_ref, tokens_hbm, merged_hbm, qkv_hbm, h1_hbm,
    grads, got_1, got_2, got_3, got_4, lefts, pool, eu, down_w, up_w, out_w, proj_w, x1, logs, vec, vec_got,
    y_send, y_got, merged, sums,
    send_sem, recv_sem, load_sem, sum_sem, vec_send, vec_recv, tower_sem, free_sem,
):
    count, width = x1.shape
    pairs, _, _, seq = logs.shape
    half = pairs // 2
    parts = eu.shape[0]
    tiles = count // TILE
    index = lax.axis_index("dp")
    tower = lax.axis_index("tower")
    core, y, z_lo, z_hi = index % 2, index // 2 % 2, index // 4 % 2, index // 8
    by_core = {"dp": index + 1 - 2 * core}
    by_y = {"dp": index + 2 - 4 * y}
    by_lo = {"dp": index + 4 - 8 * z_lo}
    by_hi = {"dp": index + 8 - 16 * z_hi}
    by_x = {"tower": 1 - tower}

    def length(pair):
        image = jnp.where(group_ref[pair] == 1, IMG_LARGE, IMG_SMALL)
        return jnp.where(tower == 0, image, caption_ref[pair])

    barrier = pltpu.get_barrier_semaphore()
    for partner in (by_core, by_y, by_lo, by_hi, by_x):
        pl.semaphore_signal(barrier, inc=1, device_id=partner, device_id_type=MESH)

    def copy(number, source, target):
        return pltpu.make_async_copy(source, target, load_sem.at[number])

    x_copy = copy(0, x_hbm, pool.at[1])
    qkv_w_copies = [
        copy(1 + i, qkv_w_hbm.at[:, pl.ds(i * width, width)], down_w.at[pl.ds(i * width, width)]) for i in range(3)
    ]
    g_copy = copy(4, g_hbm, merged)
    out_copy = copy(5, out_hbm, out_w)
    up_copy = copy(6, up_hbm, up_w)
    proj_copy = copy(7, proj_hbm, proj_w)
    down_copy = copy(8, down_hbm, down_w)
    qkv_saves = [copy(9 + i, eu.at[i], qkv_hbm.at[i]) for i in range(3)]
    h1_save = copy(12, lefts.at[0], h1_hbm)
    h1_copy = copy(13, h1_hbm, lefts.at[0])
    qkv_copies = [copy(14 + i, qkv_hbm.at[i], down_w.at[pl.ds(i * count, count)]) for i in range(3)]
    qkv_w_again = copy(17, qkv_w_hbm, up_w.at[:, pl.ds(0, 3 * width)])
    tokens_copy = copy(18, pool.at[0], tokens_hbm)
    merged_copy = copy(19, merged, merged_hbm)

    for item in (x_copy, *qkv_w_copies, g_copy):
        item.start()
    vec[0] = jnp.zeros((VECTORS, width), F32)

    def add_to(row, value, lanes=slice(None)):
        vec[0, row : row + 1, lanes] = vec[0, row : row + 1, lanes] + jnp.sum(value, 0, keepdims=True)

    def tile_rows(tile):
        return pl.ds(pl.multiple_of(tile * TILE, TILE), TILE)

    def tile_valid(tile):
        per_pair = seq // TILE
        row = lax.broadcasted_iota(jnp.int32, (TILE, 1), 0) + tile % per_pair * TILE
        return row < length(tile // per_pair)

    def put(slot, value, at):
        turned = value.T
        for chunk in range(16):
            lefts[slot, slot_of(chunk), :, at] = turned[chunk * SHARD : (chunk + 1) * SHARD]

    gain_one, gain_two = gain_ref[0:1].astype(F32), gain_ref[1:2].astype(F32)
    shift_one, shift_two = shift_ref[0:1].astype(F32), shift_ref[1:2].astype(F32)
    biases = bias_ref[...].astype(F32)
    x_copy.wait()

    def first_norm(tile, carry):
        at = tile_rows(tile)
        hat, _ = norm_stats(pool[1, at, :].astype(F32))
        h = (hat * gain_one + shift_one).astype(BF16)
        pool[2, at, :] = h
        put(0, h, at)
        return carry

    def first_products(tile, carry):
        at = tile_rows(tile)
        h = pool[2, at, :]
        q = (nn(h, down_w[:width, :]) + biases[0:1]).astype(BF16)
        eu[0, at, :] = q * BF16(HEAD_DIM**-0.5)
        eu[1, at, :] = nn(h, down_w[width : 2 * width, :]).astype(BF16)
        eu[2, at, :] = (nn(h, down_w[2 * width : 3 * width, :]) + biases[1:2]).astype(BF16)
        return carry

    lax.fori_loop(0, tiles, first_norm, 0)
    h1_save.start()
    for item in qkv_w_copies:
        item.wait()
    lax.fori_loop(0, tiles, first_products, 0)
    for item in (*qkv_saves, down_copy, out_copy, up_copy, proj_copy):
        item.start()

    g_copy.wait()
    pl.semaphore_wait(barrier, 5)
    strip = 128
    row = lax.broadcasted_iota(jnp.int32, (strip, 1), 0)

    def cotangent(side, put_strip):
        for start in range(0, seq, strip):
            first = pl.multiple_of(side * seq + start, strip)
            value = merged[0, pl.ds(first, strip), :].astype(F32)
            after = merged[0, pl.ds(first + strip, 1), :].astype(F32)
            put_strip(start, jnp.where(row == strip - 1, after, pltpu.roll(value, strip - 1, 0)).astype(BF16))

    def put_send(start, value):
        pool[2, start : start + strip, :] = value

    def put_own(start, value):
        pool[0, pl.ds(pl.multiple_of(tower * seq + start, strip), strip), :] = value

    cotangent(1 - tower, put_send)
    own_rows = pl.ds(pl.multiple_of(tower * seq, seq), seq)
    g_swap = pltpu.make_async_remote_copy(
        pool.at[2, pl.ds(0, seq)], pool.at[0, own_rows], tower_sem.at[0], tower_sem.at[1], device_id=by_x, device_id_type=MESH
    )
    g_swap.start()
    cotangent(tower, put_own)
    vec[0, 13:14, :] = merged[0, 0:1, :].astype(F32)

    def attend_one(pair, block):
        at = pl.ds(pl.multiple_of(pair * seq, seq), seq)
        lanes = pl.ds(pl.multiple_of(block * LANES, LANES), LANES)
        valid = lax.broadcasted_iota(jnp.int32, (1, seq), 1) < length(pair)
        q, k, v = (eu[number, at, lanes] for number in range(3))
        mixed = None
        for head in range(2):
            scores = jnp.where(valid, nt(head_lanes(head, q), k), masked_score)
            largest = jnp.max(scores, 1, keepdims=True)
            weights = jnp.exp(scores - largest)
            total = jnp.sum(weights, 1, keepdims=True)
            here = nn(weights.astype(BF16), head_lanes(head, v)) * (1.0 / total)
            mixed = here if mixed is None else mixed + here
            logs[pair, block, head : head + 1, :] = (largest + jnp.log(total)).reshape(1, seq)
        pool[3, at, lanes] = mixed.astype(BF16)

    def attend(step, carry):
        steps = BLOCKS // ABREAST
        for number in range(ABREAST):
            attend_one(step // steps, step % steps * ABREAST + number)
        return carry

    lax.fori_loop(0, pairs * BLOCKS // ABREAST, attend, 0)

    for item in (h1_save, *qkv_saves, out_copy, up_copy, down_copy, proj_copy):
        item.wait()

    def feed(tile, carry):
        at = tile_rows(tile)
        a = pool[3, at, :]
        put(6, a, at)
        mid = pool[1, at, :].astype(F32) + nn(a, out_w[...]) + biases[2:3]
        x1[at, :] = mid
        hat, _ = norm_stats(mid)
        h = (hat * gain_two + shift_two).astype(BF16)
        put(5, h, at)
        x2 = mid + biases[3:4]
        for part in range(parts):
            span = slice(part * width, (part + 1) * width)
            u = nn(h, up_w[:, span]) + hidden_ref[:, span].astype(F32)
            acted, slope = gelu_and_slope(u)
            z = acted.astype(BF16)
            eu[part, at, :] = slope.astype(BF16)
            turned = z.T
            for piece in range(16):
                chunk, block = part * 4 + piece // 4, piece % 4
                lefts[1 + block, slot_of(chunk), :, at] = turned[piece * SHARD : (piece + 1) * SHARD]
            x2 = x2 + nn(z, down_w[span, :])
        x2_low = x2.astype(BF16)
        put(0, x2_low, at)
        rows_y = jnp.where(tile_valid(tile), nn(x2_low, proj_w[...]) + biases[4:5], 0.0).astype(BF16)
        per_pair = seq // TILE
        here = pl.ds(pl.multiple_of(tile % per_pair * TILE, TILE), TILE)

        @pl.when(tile // per_pair == tower)
        def _():
            merged[0, here, :] = rows_y

        @pl.when(tile // per_pair != tower)
        def _():
            y_send[here, :] = rows_y

        return carry

    lax.fori_loop(0, tiles, feed, 0)
    y_swap = pltpu.make_async_remote_copy(
        y_send, y_got, tower_sem.at[2], tower_sem.at[3], device_id=by_x, device_id_type=MESH
    )
    y_swap.start()

    g_swap.wait()

    def cotangent_rows(tile, carry):
        at = tile_rows(tile)
        g = jnp.where(tile_valid(tile), pool[0, at, :].astype(F32), 0.0)
        pool[0, at, :] = g.astype(BF16)
        add_to(4, g)
        return carry

    lax.fori_loop(0, tiles, cotangent_rows, 0)

    def project_back(tile, carry):
        at = tile_rows(tile)
        dx2 = nt(pool[0, at, :], proj_w[...])
        pool[2, at, :] = dx2.astype(BF16)
        add_to(3, dx2)
        return carry

    def bits(block):
        ways = {"y": (by_y, y), "l": (by_lo, z_lo), "h": (by_hi, z_hi)}
        partners, sides = zip(*(ways[letter] for letter in MODES[block]))
        return (by_core, *partners), sides

    def shelf(block):
        if 5 <= block < 9:
            return lefts, block - 4
        return grads, (block if block < 5 else block - 4) % RING

    def shards(block, of_core, first, size):
        buffer, slot = shelf(block)
        return buffer.at[slot, pl.ds(of_core * 8 + first, size), :, pl.ds(0, width)]

    gots = (got_1, got_2, got_3, got_4)

    def place(block, level):
        return block % (CORE_RING, SECOND_RING, BLOCK_COUNT, BLOCK_COUNT)[level]

    def swap_of(block, level):
        partners, (b1, b2, b3) = bits(block)
        if level == 0:
            source = shards(block, 1 - core, 0, 8)
        elif level == 1:
            source = shards(block, core, (1 - b1) * 4, 4)
        elif level == 2:
            source = shards(block, core, b1 * 4 + (1 - b2) * 2, 2)
        else:
            source = shards(block, core, b1 * 4 + b2 * 2 + 1 - b3, 1)
        return pltpu.make_async_remote_copy(
            source,
            gots[level].at[place(block, level)],
            send_sem.at[level, block],
            recv_sem.at[level, block],
            device_id=partners[level],
            device_id_type=MESH,
        )

    def advance(block, level):
        _, (b1, b2, b3) = bits(block)
        buffer, slot = shelf(block)
        swap_of(block, level - 1).wait_recv()
        got = gots[level - 1]
        size = 8 >> level
        bit = (b1, b2, b3)[level - 1]
        base = (0, b1 * 4, b1 * 4 + b2 * 2)[level - 1]
        for other in (1, 0):
            side = (1 - bit) if other else bit

            def add(i, carry, side=side):
                at = side * size + i
                here = core * 8 + base + at
                total = buffer[slot, here, :, :width].astype(F32) + got[place(block, level - 1), at].astype(F32)
                buffer[slot, here, :, :width] = total.astype(BF16)
                return carry

            lax.fori_loop(0, size, add, 0)
            if other:
                if level == 1 and block >= SECOND_RING:
                    assert (block - SECOND_RING, 2) in done
                    pl.semaphore_wait(free_sem.at[1, block], 1)
                swap_of(block, level).start()
        later = block + (CORE_RING, SECOND_RING, BLOCK_COUNT)[level - 1]
        if later < BLOCK_COUNT:
            pl.semaphore_signal(
                free_sem.at[level - 1, later], inc=1, device_id=bits(later)[0][level - 1], device_id_type=MESH
            )

    def sum_copy(block, slot):
        if block == 0:
            target = proj_ref
        elif block < 5:
            target = down_ref.at[pl.ds((block - 1) * SHARD, SHARD)]
        elif block < 9:
            target = up_ref.at[:, pl.ds((block - 5) * width, width)]
        elif block == 9:
            target = out_ref
        else:
            target = qkv_ref.at[:, pl.ds((block - 10) * width, width)]
        return pltpu.make_async_copy(sums.at[slot], target, sum_sem.at[slot])

    finished = []

    def finish(block):
        _, (b1, b2, b3) = bits(block)
        swap_of(block, 3).wait_recv()
        buffer, slot = shelf(block)
        total = buffer[slot, core * 8 + b1 * 4 + b2 * 2 + b3, :, :width].astype(F32) + got_4[block, 0].astype(F32)
        if len(finished) >= 3:
            sum_copy(finished[-3], (len(finished) - 3) % 3).wait()
        place_now = len(finished) % 3
        sums[place_now] = total
        sum_copy(block, place_now).start()
        finished.append(block)
        for level in range(4):
            swap_of(block, level).wait_send()

    done = set()

    def tick(*work):
        for block, level in work:
            assert (block, level) not in done and (level == 1 or (block, level - 1) in done)
            done.add((block, level))
            if level == 4:
                finish(block)
            else:
                advance(block, level)

    def weight_grad(block, number, right):
        assert block < 10 or (block - 10, 4) in done
        assert block < CORE_RING or (block - CORE_RING, 1) in done
        left = lefts[number].reshape(16 * SHARD, count)
        buffer, slot = shelf(block)
        step = 256

        def columns(i, carry):
            at = pl.ds(pl.multiple_of(i * step, step), step)
            product = nn(left, right(at)).astype(BF16).reshape(16, SHARD, step)
            if MODES[block] == "ylh":
                buffer[slot, :, :, at] = product
            else:
                for number in range(16):
                    side = {"y": number // 4 % 2, "l": number // 2 % 2, "h": number % 2}
                    a, b, c = (side[letter] for letter in MODES[block])
                    buffer[slot, number // 8 * 8 + a * 4 + b * 2 + c, :, at] = product[number]
            return carry

        lax.fori_loop(0, width // step, columns, 0)
        if block >= CORE_RING:
            pl.semaphore_wait(free_sem.at[0, block], 1)
        swap_of(block, 0).start()

    weight_grad(0, 0, lambda at: pool[0, :, at])
    tick(*TICKS["proj", 0])
    h1_copy.start()
    lax.fori_loop(0, tiles, project_back, 0)
    tick(*TICKS["e2", 0])
    for part in range(parts):
        weight_grad(1 + part, 1 + part, lambda at: pool[2, :, at])
        tick(*TICKS["down", part])

    for part in range(parts):

        def tile_du(tile, carry, part=part):
            at = tile_rows(tile)
            du = nt(pool[2, at, :], down_w[part * width : (part + 1) * width, :])
            du = du * eu[part, at, :].astype(F32)
            eu[part, at, :] = du.astype(BF16)
            add_to(9 + part, du)
            return carry

        lax.fori_loop(0, tiles, tile_du, 0)
        tick(*TICKS["du", part])
    for item in qkv_copies:
        item.start()

    for part in range(parts):
        weight_grad(5 + part, 5, lambda at, part=part: eu[part, :, at])
        tick(*TICKS["up", part])

    for number in range(tiles):

        def mid_back(tile, carry):
            at = tile_rows(tile)
            dh = nt(eu[0, at, :], up_w[:, :width])
            for part in range(1, parts):
                dh = dh + nt(eu[part, at, :], up_w[:, part * width : (part + 1) * width])
            hat, scale = norm_stats(x1[at, :])
            dx1 = nt(pool[0, at, :], proj_w[...]) + norm_back(dh, hat, scale, gain_two)
            x1[at, :] = dx1
            e1 = dx1.astype(BF16)
            pool[2, at, :] = e1
            pool[0, at, :] = nt(e1, out_w[...]).astype(BF16)
            add_to(6, dh * hat)
            add_to(8, dh)
            add_to(2, dx1)
            return carry

        lax.fori_loop(number, number + 1, mid_back, 0)
        tick(*TICKS["mid", number])
    qkv_w_again.start()

    weight_grad(9, 6, lambda at: pool[2, :, at])
    tick(*TICKS["out", 0])

    for item in qkv_copies:
        item.wait()
    per_loop = 2
    for turn in range(pairs * BLOCKS // per_loop):

        def attend_back_one(step):
            pair, block = step // BLOCKS, step % BLOCKS
            at = pl.ds(pl.multiple_of(pair * seq, seq), seq)
            lanes = pl.ds(pl.multiple_of(block * LANES, LANES), LANES)
            valid = lax.broadcasted_iota(jnp.int32, (seq, 1), 0) < length(pair)
            q, k, v = (
                down_w[pl.ds(pl.multiple_of(number * count + pair * seq, seq), seq), lanes] for number in range(3)
            )
            d = pool[0, at, lanes]
            log_rows = logs[pair, block]
            k_t = k.T
            d_t = d.T
            prod_t = d_t.astype(F32) * pool[3, at, lanes].T.astype(F32)
            dq_rows = []
            dk = None
            dv = None
            for head in range(2):
                span = slice(head * HEAD_DIM, (head + 1) * HEAD_DIM)
                row_dot = jnp.sum(prod_t[span], 0, keepdims=True)
                v_here = head_lanes(head, v)
                dq_parts = []
                for start in range(0, seq, QUERIES):
                    some = slice(start, start + QUERIES)
                    q_here = head_lanes(head, q[some])
                    scores = jnp.where(valid, nt(k, q_here), masked_score)
                    probs = jnp.exp(scores - log_rows[head : head + 1, some])
                    d_probs = nn(v_here, d_t[:, some])
                    d_scores = (probs * (d_probs - row_dot[:, some])).astype(BF16)
                    dv_here = nn(probs.astype(BF16), head_lanes(head, d[some]))
                    dk_here = nn(d_scores, q_here)
                    dq_parts.append(nn(k_t[span], d_scores))
                    dk = dk_here if dk is None else dk + dk_here
                    dv = dv_here if dv is None else dv + dv_here
                dq_rows.append(jnp.concatenate(dq_parts, 1))
            dq = jnp.concatenate(dq_rows, 0).T * HEAD_DIM**-0.5
            for number, value in ((0, dq), (1, dk), (2, dv)):
                eu[number, at, lanes] = value.astype(BF16)
            add_to(0, dq, lanes)
            add_to(1, dv, lanes)

        def attend_back(step, carry):
            for number in range(per_loop):
                attend_back_one(step * per_loop + number)
            return carry

        lax.fori_loop(turn, turn + 1, attend_back, 0)
        tick(*TICKS["attend", turn])

    h1_copy.wait()
    for part in range(3):
        weight_grad(10 + part, 0, lambda at, part=part: eu[part, :, at])
        tick(*TICKS["qkv", part])

    qkv_w_again.wait()
    for number in range(tiles):

        def first_back(tile, carry):
            at = tile_rows(tile)
            dh = nt(eu[0, at, :], up_w[:, :width])
            for part in (1, 2):
                dh = dh + nt(eu[part, at, :], up_w[:, part * width : (part + 1) * width])
            hat, scale = norm_stats(pool[1, at, :].astype(F32))
            pool[0, at, :] = (x1[at, :] + norm_back(dh, hat, scale, gain_one)).astype(BF16)
            add_to(5, dh * hat)
            add_to(7, dh)
            return carry

        lax.fori_loop(number, number + 1, first_back, 0)
        tick(*TICKS["first", number])
    tokens_copy.start()

    def vec_swap(level):
        return pltpu.make_async_remote_copy(
            vec.at[level],
            vec_got.at[level],
            vec_send.at[level],
            vec_recv.at[level],
            device_id=(by_core, by_y, by_lo, by_hi, by_x)[level],
            device_id_type=MESH,
        )

    vec_swap(0).start()

    y_swap.wait()

    def projected(side, start, size):
        own = merged[0, start : start + size, :].astype(F32)
        got = y_got[start : start + size, :].astype(F32)
        return jnp.where(tower == side, own, got)

    merged[0, 2 * seq : 2 * seq + 1, :] = projected(1, seq - 16, 16)[15:16].astype(BF16)
    for side in (1, 0):
        for start in range(seq - strip, -1, -strip):
            value = projected(side, start, strip)
            if start > 0:
                before = projected(side, start - 16, 16)[15:16]
            elif side == 1:
                before = projected(0, seq - 16, 16)[15:16]
            else:
                before = cls_row_ref[...].reshape(1, width).astype(F32)
            moved = jnp.where(row == 0, before, pltpu.roll(value, 1, 0))
            merged[0, side * seq + start : side * seq + start + strip, :] = moved.astype(BF16)
    merged_copy.start()

    for number, work in enumerate(TICKS["tail", 0]):
        tick(work)
        if number < 4:
            vec_swap(number).wait_recv()
            vec[number + 1] = vec[number] + vec_got[number]
            vec_swap(number + 1).start()
    vec_swap(4).wait_recv()
    vec_ref[0:13] = vec[4, 0:13]
    vec_ref[13:16] = vec[4, 13:16] + vec_got[4, 13:16]
    for level in range(5):
        vec_swap(level).wait_send()
    for number in range(BLOCK_COUNT - 3, BLOCK_COUNT):
        sum_copy(finished[number], number % 3).wait()
    tokens_copy.wait()
    merged_copy.wait()
    assert len(done) == 4 * BLOCK_COUNT


TICKS = {
    ('proj', 0): [],
    ('e2', 0): [],
    ('down', 0): [],
    ('down', 1): [(0, 1)],
    ('down', 2): [],
    ('down', 3): [(1, 1)],
    ('du', 0): [(2, 1)],
    ('du', 1): [(3, 1), (4, 1)],
    ('du', 2): [(0, 2)],
    ('du', 3): [],
    ('up', 0): [(1, 2)],
    ('up', 1): [],
    ('up', 2): [(2, 2)],
    ('up', 3): [(5, 1)],
    ('mid', 0): [(0, 3), (3, 2), (6, 1), (7, 1)],
    ('mid', 1): [(1, 3), (8, 1)],
    ('mid', 2): [(4, 2)],
    ('mid', 3): [(2, 3), (5, 2)],
    ('out', 0): [(0, 4)],
    ('attend', 0): [(1, 4), (3, 3)],
    ('attend', 1): [(6, 2), (9, 1)],
    ('attend', 2): [(8, 2)],
    ('attend', 3): [(2, 4), (4, 3), (5, 3), (3, 4), (7, 2)],
    ('attend', 4): [(6, 3)],
    ('attend', 5): [(4, 4), (9, 2)],
    ('qkv', 0): [(5, 4)],
    ('qkv', 1): [(7, 3), (8, 3)],
    ('qkv', 2): [(6, 4)],
    ('first', 0): [(10, 1), (9, 3), (11, 1)],
    ('first', 1): [(7, 4), (12, 1)],
    ('first', 2): [],
    ('first', 3): [(8, 4)],
    ('tail', 0): [(9, 4), (10, 2), (11, 2), (10, 3), (12, 2), (11, 3), (10, 4), (12, 3), (11, 4), (12, 4)],
}


def run_one(group_id, caption_len, gains, shifts, biases, hidden, cls_row, x, g, qkv_w, out_w, up_w, down_w, proj_w):
    count, width = x.shape
    ff = up_w.shape[1]
    pairs = group_id.shape[0]
    seq = count // pairs
    shard = jax.ShapeDtypeStruct
    vmem = pl.BlockSpec(memory_space=pltpu.VMEM)
    hbm = pl.BlockSpec(memory_space=pl.ANY)
    return pl.pallas_call(
        one_kernel,
        in_specs=[pl.BlockSpec(memory_space=pltpu.SMEM)] * 2 + [vmem] * 5 + [hbm] * 7,
        out_specs=[hbm] * 5 + [vmem] + [hbm] * 4,
        out_shape=[
            shard((SHARD, width), F32),
            shard((4 * SHARD, width), F32),
            shard((SHARD, ff), F32),
            shard((SHARD, width), F32),
            shard((SHARD, 3 * width), F32),
            shard((VECTORS, width), F32),
            shard((count, width), BF16),
            shard(g.shape, BF16),
            shard((3, count, width), BF16),
            shard((16, SHARD, count), BF16),
        ],
        scratch_shapes=[
            pltpu.VMEM((RING, 16, SHARD, width), BF16),
            pltpu.VMEM((CORE_RING, 8, SHARD, width), BF16),
            pltpu.VMEM((SECOND_RING, 4, SHARD, width), BF16),
            pltpu.VMEM((BLOCK_COUNT, 2, SHARD, width), BF16),
            pltpu.VMEM((BLOCK_COUNT, 1, SHARD, width), BF16),
            pltpu.VMEM((7, 16, SHARD, count), BF16),
            pltpu.VMEM((4, count, width), BF16),
            pltpu.VMEM((ff // width, count, width), BF16),
            pltpu.VMEM((ff, width), BF16),
            pltpu.VMEM((width, ff), BF16),
            pltpu.VMEM((width, width), BF16),
            pltpu.VMEM((width, width), BF16),
            pltpu.VMEM((count, width), F32),
            pltpu.VMEM((pairs, BLOCKS, 2, seq), F32),
            pltpu.VMEM((5, VECTORS, width), F32),
            pltpu.VMEM((5, VECTORS, width), F32),
            pltpu.VMEM((seq, width), BF16),
            pltpu.VMEM((seq, width), BF16),
            pltpu.VMEM(g.shape, BF16),
            pltpu.VMEM((3, SHARD, width), F32),
            pltpu.SemaphoreType.DMA((4, BLOCK_COUNT)),
            pltpu.SemaphoreType.DMA((4, BLOCK_COUNT)),
            pltpu.SemaphoreType.DMA((20,)),
            pltpu.SemaphoreType.DMA((3,)),
            pltpu.SemaphoreType.DMA((5,)),
            pltpu.SemaphoreType.DMA((5,)),
            pltpu.SemaphoreType.DMA((4,)),
            pltpu.SemaphoreType.REGULAR((2, BLOCK_COUNT)),
        ],
        compiler_params=pltpu.CompilerParams(
            collective_id=0, has_side_effects=True, vmem_limit_bytes=63 * MIB
        ),
        cost_estimate=cost(60e9, 60 * MIB),
        name="one",
    )(group_id, caption_len, gains, shifts, biases, hidden, cls_row, x, g, qkv_w, out_w, up_w, down_w, proj_w)


def full_grad_kernel(left_ref, *refs):
    start = 0
    for right_ref in refs[:-1]:
        stop = start + right_ref.shape[1]
        refs[-1][:, start:stop] = nn(left_ref[...], right_ref[...])
        start = stop


def run_full_grad(left, *rights):
    height, count = left.shape
    width = sum(right.shape[1] for right in rights)
    tile = 384
    return pl.pallas_call(
        full_grad_kernel,
        grid=(height // tile,),
        in_specs=[rows(tile, count)] + [whole(right.shape) for right in rights],
        out_specs=rows(tile, width),
        out_shape=jax.ShapeDtypeStruct((height, width), F32),
        compiler_params=params(),
        name="full_grad",
    )(left, *rights)


def in_order(slabs):
    return jnp.stack([slabs[..., slot_of(chunk), :, :] for chunk in range(16)], -3)


def plain_back(lengths, logs, gains, feed_sums, cls_sum, left, h1, slope, g, e2, dx2, x1, a, qkv, x, y, down_w, up_w, out_w, qkv_w):
    count, width = x.shape
    seq = y.shape[2]
    eu, dx1, e1, da, hidden_sum, mid_sums = run_feed_back(e2, dx2, slope, x1, gains, out_w, up_w, down_w)
    dq, dk, dv, sum_q, sum_v = run_attend_back(lengths, qkv, a, da, logs, seq)
    tokens_grad, first_sums = run_qkv_back(dq, dk, dv, dx1, x, gains, qkv_w)
    turned = in_order(left)
    z = turned[1:5].transpose(1, 0, 2, 3).reshape(4 * width, count)
    x2, h2, a_t = (turned[i].reshape(width, count) for i in (0, 5, 6))
    h1 = in_order(h1).reshape(width, count)
    grads = (run_full_grad(x2, g), run_full_grad(z, e2), run_full_grad(h2, eu), run_full_grad(a_t, e1), run_full_grad(h1, dq, dk, dv))
    grads = [lax.psum_scatter(grad, "dp", scatter_dimension=0, tiled=True) for grad in grads]
    vectors = jnp.concatenate(
        [
            jnp.sum(sum_q, 0), jnp.sum(sum_v, 0), mid_sums[2:3], feed_sums, first_sums[0:1], mid_sums[0:1],
            first_sums[1:2], mid_sums[1:2], hidden_sum.reshape(-1, width),
        ],
        axis=0,
    )
    vectors = lax.psum(vectors, "dp")
    cls = lax.psum(cls_sum, ("tower", "dp"))
    y_got = lax.ppermute(take(y, 1 - lax.axis_index("tower")), "tower", [(0, 1), (1, 0)])
    return grads, vectors, cls, tokens_grad, y_got


def take(value, index):
    return lax.dynamic_index_in_dim(value, index, 0, keepdims=False)


PIECE = 256


def spread_kernel(index_ref, vec_ref, *refs):
    sources, (gain_ref, shift_ref, bias_ref, hidden_ref, cls_ref), targets, held = refs[:7], refs[7:12], refs[12:19], refs[19:26]
    sem_in, sem_out = refs[26:]
    ins, outs = [], []
    for source, there, target in zip(sources, held, targets):
        size = source.shape[0]
        step = PIECE if size % PIECE == 0 else size
        for start in range(0, size, step):
            number, at = len(ins), pl.ds(start, step)
            ins.append(pltpu.make_async_copy(source.at[at], there.at[at], sem_in.at[number]))
            outs.append(pltpu.make_async_copy(there.at[at], target.at[at], sem_out.at[number]))
    for item in ins:
        item.start()
    index = index_ref[0]
    width = vec_ref.shape[1]
    piece = gain_ref.shape[1]
    mine = pltpu.roll(vec_ref[...], width - piece * index, 1)[:, :piece]
    for number in range(5):
        bias_ref[number] = mine[number : number + 1]
    gain_ref[...] = mine[5:7]
    shift_ref[...] = mine[7:9]
    share = hidden_ref.shape[1]
    per_row = width // share
    row = vec_ref[pl.ds(9 + index // per_row, 1), :]
    hidden_ref[...] = pltpu.roll(row, width - share * (index % per_row), 1)[:, :share]
    cls_ref[...] = vec_ref[13]
    for before, after in zip(ins, outs):
        before.wait()
        after.start()
    for item in outs:
        item.wait()


def run_spread(index, vectors, *arrays):
    width = vectors.shape[1]
    small = [jax.ShapeDtypeStruct(shape, F32) for shape in ((2, width // 16), (2, width // 16), (5, 1, width // 16), (1, width // 4), (width,))]
    vmem = pl.BlockSpec(memory_space=pltpu.VMEM)
    hbm = pl.BlockSpec(memory_space=pl.ANY)
    return pl.pallas_call(
        spread_kernel,
        in_specs=[pl.BlockSpec(memory_space=pltpu.SMEM), vmem] + [hbm] * len(arrays),
        out_specs=[vmem] * 5 + [hbm] * len(arrays),
        out_shape=small + [jax.ShapeDtypeStruct(array.shape, array.dtype) for array in arrays],
        scratch_shapes=[pltpu.VMEM(array.shape, array.dtype) for array in arrays]
        + [pltpu.SemaphoreType.DMA((16,))] * 2,
        compiler_params=params(62),
        name="spread",
    )(index, vectors, *arrays)


def local(
    dp, tokens, group_id, caption_len, cls_row, norm_gains, shifts, bias_model, bias_hidden,
    w_qkv, w_out, w_up, w_down, w_proj, merged_grad,
):
    tower = lax.axis_index("tower")
    index = lax.axis_index("dp")
    pairs, seq, width = tokens.shape[1:]
    half = pairs // 2
    count = pairs * seq
    image_len = jnp.where(group_id == 1, IMG_LARGE, IMG_SMALL)
    lengths = jnp.where(tower == 0, image_len, caption_len).astype(jnp.int32)
    gains, shift_rows, biases, hidden = norm_gains[0], shifts[0], bias_model[0], bias_hidden
    qkv_w, out_w, up_w, down_w, proj_w = w_qkv[0], w_out[0], w_up[0], w_down[0], w_proj[0]
    x = tokens[0].reshape(count, width)

    if dp == 16 and pairs == 2:
        *grads, vectors, tokens_grad, merged_input, _, _ = run_one(
            group_id, caption_len, gains, shift_rows, biases, hidden, cls_row, x, merged_grad[0], qkv_w, out_w, up_w, down_w, proj_w
        )
        gain_sum, shift_sum, bias_sum, hidden_sum, cls, *arrays = run_spread(
            index.astype(jnp.int32)[None], vectors, merged_input, tokens_grad, *grads
        )
        bias_sum = bias_sum.transpose(1, 0, 2)[0]
        merged_input, tokens_grad, proj, down, up, out, qkv_grad = arrays
    else:
        positions = lax.broadcasted_iota(jnp.int32, (pairs, seq), 1)
        valid = (positions < lengths[:, None]).reshape(count, 1).astype(F32)
        image_grad = merged_grad[0, :, 1 : 1 + seq]
        text_grad = merged_grad[0, :, 1 + seq :]
        g_keep = jnp.where(tower == 0, image_grad, text_grad)
        g_send = jnp.where(tower == 0, text_grad, image_grad)
        g_got = lax.ppermute(g_send, "tower", [(0, 1), (1, 0)])
        cls_sum = jnp.sum(merged_grad[0, :, 0].astype(F32), 0)[None]
        h1, qkv = run_qkv(x, gains, shift_rows, biases, qkv_w)
        mixed, logs = run_attend(lengths, qkv, seq)
        g = jnp.where(tower == 0, jnp.stack([g_keep, g_got]), jnp.stack([g_got, g_keep])).reshape(count, width)
        x1, left, slope, y, g_low, dx2, e2, feed_sums = run_feed(
            valid, x, mixed, g, gains, shift_rows, biases, hidden, out_w, up_w, down_w, proj_w
        )
        y = y.reshape(2, half, seq, width)
        grads, vectors, cls, tokens_grad, y_got = plain_back(
            lengths, logs, gains, feed_sums, cls_sum, left, h1, slope, g_low, e2, dx2, x1, mixed, qkv, x, y,
            down_w, up_w, out_w, qkv_w,
        )
        proj, down, up, out, qkv_grad = grads
        y_own = take(y, tower)
        cls_block = jnp.broadcast_to(cls_row.reshape(1, 1, width), (half, 1, width))
        image_rows = jnp.where(tower == 0, y_own, y_got)
        text_rows = jnp.where(tower == 0, y_got, y_own)
        merged_input = jnp.concatenate([cls_block, image_rows, text_rows], axis=1)
        mine = lax.dynamic_slice_in_dim(vectors[:9], index * (width // dp), width // dp, 1)
        bias_sum, gain_sum, shift_sum = mine[0:5], mine[5:7], mine[7:9]
        ff = up_w.shape[1]
        hidden_sum = lax.dynamic_slice_in_dim(vectors[9:13].reshape(1, ff), index * (ff // dp), ff // dp, 1)
    return (
        merged_input[None], tokens_grad.reshape(tokens.shape), cls.reshape(width), gain_sum[None], shift_sum[None],
        bias_sum[None], hidden_sum, qkv_grad[None], out[None], up[None], down[None], proj[None],
    )


def solution(mesh):
    tower = P("tower", None, None)
    in_specs = (
        P("tower", "dp", None, None), P("dp"), P("dp"), P(), tower, tower, tower, P("tower", None),
        tower, tower, tower, tower, tower, P("tower", "dp", None, None),
    )
    spread = P("tower", None, "dp")
    weight = P("tower", "dp", None)
    out_specs = (
        P("tower", "dp", None, None), P("tower", "dp", None, None), P(), spread, spread, spread, P("tower", "dp"),
        weight, weight, weight, weight, weight,
    )
    return jax.shard_map(
        partial(local, mesh.shape["dp"]), mesh=mesh, in_specs=in_specs, out_specs=out_specs, check_vma=False
    )
```

```python
from functools import partial

import jax
import jax.numpy as jnp
from jax import lax
from jax.experimental import pallas as pl
from jax.experimental.pallas import tpu as pltpu
from jax.sharding import PartitionSpec as P

HEADS = 12
HEAD_DIM = 64
IMG_SMALL = 197
IMG_LARGE = 325
LANES = 128
BLOCKS = HEADS * HEAD_DIM // LANES

norm_eps = 1e-06
masked_score = -1e30
F32 = jnp.float32
BF16 = jnp.bfloat16
MIB = 1 << 20
SHARD = 48

ERF_P = 0.39
ERF_C = (0.2344334842, 0.09695712066, 0.6357617632, -0.6184387086, 0.8763152235, -0.225028871)


def nn(left, right):
    return jnp.dot(left, right, preferred_element_type=F32)


def nt(left, right):
    return lax.dot_general(left, right, (((1,), (1,)), ((), ())), preferred_element_type=F32)


def tn(left, right):
    return lax.dot_general(left, right, (((0,), (0,)), ((), ())), preferred_element_type=F32)


def params(vmem=48, semantics=None):
    return pltpu.CompilerParams(vmem_limit_bytes=vmem * MIB, dimension_semantics=semantics)


def cost(flops, nbytes, trans=0):
    return pl.CostEstimate(flops=int(flops), bytes_accessed=int(nbytes), transcendentals=int(trans))


def whole(shape):
    return pl.BlockSpec(shape, lambda *_: (0,) * len(shape), pipeline_mode=pl.Buffered(1))


def rows(tile, width):
    return pl.BlockSpec((tile, width), lambda i, *_: (i, 0))


def norm_stats(x):
    mean = jnp.mean(x, -1, keepdims=True)
    centred = x - mean
    spread = jnp.mean(centred * centred, -1, keepdims=True)
    scale = lax.rsqrt(spread + norm_eps)
    return centred * scale, scale


def norm_back(grad, hat, scale, gain):
    d_hat = grad * gain
    first = jnp.mean(d_hat, -1, keepdims=True)
    second = jnp.mean(d_hat * hat, -1, keepdims=True)
    return scale * (d_hat - first - hat * second)


def gelu_and_slope(u):
    bell = jnp.exp2(u * u * (-0.5 * 1.4426950408889634))
    t = 1.0 / (1.0 + (ERF_P * 0.5**0.5) * jnp.abs(u))
    poly = jnp.full_like(u, 0.5 * ERF_C[-1])
    for c in ERF_C[-2::-1]:
        poly = poly * t + 0.5 * c
    tail = poly * t * bell
    phi = jnp.where(u >= 0, 1.0 - tail, tail)
    slope = phi + u * bell * 0.3989422804014327
    return u * phi, slope


def slot_of(chunk):
    z_hi, z_lo, y, core = chunk // 8, chunk // 4 % 2, chunk // 2 % 2, chunk % 2
    return ((core * 2 + y) * 2 + z_lo) * 2 + z_hi


def put_slabs(ref, lead, value):
    turned = value.T
    for chunk in range(16):
        ref[(*lead, slot_of(chunk))] = turned[chunk * SHARD : (chunk + 1) * SHARD]


def add_sum(ref, index, value, first):
    ref[index : index + 1, :] = jnp.where(first, 0.0, ref[index : index + 1, :]) + jnp.sum(value, 0, keepdims=True)


def qkv_kernel(x_ref, gain_ref, shift_ref, bias_ref, w_ref, h_ref, out_ref):
    width = x_ref.shape[1]
    hat, _ = norm_stats(x_ref[...].astype(F32))
    h = (hat * gain_ref[0:1].astype(F32) + shift_ref[0:1].astype(F32)).astype(BF16)
    put_slabs(h_ref, (), h)
    q = nn(h, w_ref[:, :width]) + bias_ref[0:1].astype(F32)
    out_ref[:, :width] = q.astype(BF16) * BF16(HEAD_DIM**-0.5)
    out_ref[:, width : 2 * width] = nn(h, w_ref[:, width : 2 * width]).astype(BF16)
    v = nn(h, w_ref[:, 2 * width :]) + bias_ref[1:2].astype(F32)
    out_ref[:, 2 * width :] = v.astype(BF16)


def run_qkv(x, gains, shifts, biases, w, tile=256):
    count, width = x.shape
    return pl.pallas_call(
        qkv_kernel,
        grid=(count // tile,),
        in_specs=[rows(tile, width), whole(gains.shape), whole(shifts.shape), whole(biases.shape), whole(w.shape)],
        out_specs=[pl.BlockSpec((16, SHARD, tile), lambda i: (0, 0, i)), rows(tile, 3 * width)],
        out_shape=[
            jax.ShapeDtypeStruct((16, SHARD, count), BF16),
            jax.ShapeDtypeStruct((count, 3 * width), BF16),
        ],
        compiler_params=params(),
        cost_estimate=cost(6 * count * width * width, 2 * (count * width * 5 + 3 * width * width)),
        name="qkv",
    )(x, gains, shifts, biases, w)


def head_lanes(head, block):
    lane = lax.broadcasted_iota(jnp.int32, (1, LANES), 1)
    keep = (lane < HEAD_DIM) if head == 0 else (lane >= HEAD_DIM)
    return jnp.where(keep, block, jnp.zeros_like(block))


def attend_kernel(len_ref, q_ref, k_ref, v_ref, a_ref, l_ref):
    seq = q_ref.shape[0]
    valid = lax.broadcasted_iota(jnp.int32, (seq, 1), 0) < len_ref[pl.program_id(0)]
    q = q_ref[...]
    k = k_ref[...]
    v_t = v_ref[...].T
    parts = []
    for head in range(2):
        scores = jnp.where(valid, nt(k, head_lanes(head, q)), masked_score)
        largest = jnp.max(scores, 0, keepdims=True)
        weights = jnp.exp(scores - largest)
        total = jnp.sum(weights, 0, keepdims=True)
        mixed = nn(v_t[head * HEAD_DIM : (head + 1) * HEAD_DIM], weights.astype(BF16))
        parts.append((mixed * (1.0 / total)).astype(BF16))
        l_ref[0, 0, head : head + 1, :] = largest + jnp.log(total)
    a_ref[...] = jnp.concatenate(parts, 0).T


def column(seq, shift):
    return pl.BlockSpec((seq, LANES), lambda p, b, *_: (p, b + shift))


def run_attend(lengths, qkv, seq):
    count = qkv.shape[0]
    width = qkv.shape[1] // 3
    pairs = count // seq
    return pl.pallas_call(
        attend_kernel,
        grid_spec=pltpu.PrefetchScalarGridSpec(
            num_scalar_prefetch=1,
            grid=(pairs, BLOCKS),
            in_specs=[column(seq, 0), column(seq, BLOCKS), column(seq, 2 * BLOCKS)],
            out_specs=[column(seq, 0), pl.BlockSpec((1, 1, 2, seq), lambda p, b, *_: (p, b, 0, 0))],
        ),
        out_shape=[
            jax.ShapeDtypeStruct((count, width), BF16),
            jax.ShapeDtypeStruct((pairs, BLOCKS, 2, seq), F32),
        ],
        compiler_params=params(),
        cost_estimate=cost(16 * pairs * HEADS * seq * seq * HEAD_DIM, 8 * count * width, pairs * HEADS * seq * seq),
        name="attend",
    )(lengths, qkv, qkv, qkv)


def attend_back_kernel(len_ref, q_ref, k_ref, v_ref, a_ref, d_ref, l_ref, dq_ref, dk_ref, dv_ref, sq_ref, sv_ref):
    seq = q_ref.shape[0]
    valid = lax.broadcasted_iota(jnp.int32, (seq, 1), 0) < len_ref[pl.program_id(0)]
    q = q_ref[...]
    k = k_ref[...]
    v = v_ref[...]
    d = d_ref[...]
    k_t = k.T
    d_t = d.T
    prod_t = d_t.astype(F32) * a_ref[...].T.astype(F32)
    dq_parts = []
    dk = None
    dv = None
    for head in range(2):
        span = slice(head * HEAD_DIM, (head + 1) * HEAD_DIM)
        q_here = head_lanes(head, q)
        scores = jnp.where(valid, nt(k, q_here), masked_score)
        probs = jnp.exp(scores - l_ref[0, 0, head : head + 1, :])
        row_dot = jnp.sum(prod_t[span], 0, keepdims=True)
        d_probs = nn(head_lanes(head, v), d_t)
        d_scores = (probs * (d_probs - row_dot)).astype(BF16)
        dv_here = nn(probs.astype(BF16), head_lanes(head, d))
        dk_here = nn(d_scores, q_here)
        dq_parts.append(nn(k_t[span], d_scores))
        dk = dk_here if dk is None else dk + dk_here
        dv = dv_here if dv is None else dv + dv_here
    dq = jnp.concatenate(dq_parts, 0).T * HEAD_DIM**-0.5
    dq_ref[...] = dq.astype(BF16)
    dk_ref[...] = dk.astype(BF16)
    dv_ref[...] = dv.astype(BF16)
    sq_ref[0] = jnp.sum(dq, 0, keepdims=True)
    sv_ref[0] = jnp.sum(dv, 0, keepdims=True)


def run_attend_back(lengths, qkv, mixed, d_mixed, log_total, seq):
    count = qkv.shape[0]
    width = qkv.shape[1] // 3
    pairs = count // seq
    sums = pl.BlockSpec((1, 1, LANES), lambda p, b, *_: (p, 0, b))
    return pl.pallas_call(
        attend_back_kernel,
        grid_spec=pltpu.PrefetchScalarGridSpec(
            num_scalar_prefetch=1,
            grid=(pairs, BLOCKS),
            in_specs=[
                column(seq, 0),
                column(seq, BLOCKS),
                column(seq, 2 * BLOCKS),
                column(seq, 0),
                column(seq, 0),
                pl.BlockSpec((1, 1, 2, seq), lambda p, b, *_: (p, b, 0, 0)),
            ],
            out_specs=[column(seq, 0)] * 3 + [sums] * 2,
        ),
        out_shape=[jax.ShapeDtypeStruct((count, width), BF16)] * 3
        + [jax.ShapeDtypeStruct((pairs, 1, width), F32)] * 2,
        compiler_params=params(),
        cost_estimate=cost(40 * pairs * HEADS * seq * seq * HEAD_DIM, 16 * count * width, pairs * HEADS * seq * seq),
        name="attend_back",
    )(lengths, qkv, qkv, qkv, mixed, d_mixed, log_total)


def feed_kernel(
    valid_ref, x_ref, a_ref, g_ref, gain_ref, shift_ref, bias_ref, hidden_ref, out_w, up_w, down_w, proj_w,
    x1_ref, left_ref, slope_ref, y_ref, gm_ref, dx2_ref, e2_ref, sum_ref,
):
    width = x_ref.shape[1]
    first = pl.program_id(0) == 0
    valid = valid_ref[...]
    a = a_ref[...]
    put_slabs(left_ref, (6,), a)
    x1 = x_ref[...].astype(F32) + nn(a, out_w[...]) + bias_ref[2:3].astype(F32)
    x1_ref[...] = x1
    hat, _ = norm_stats(x1)
    h = (hat * gain_ref[1:2].astype(F32) + shift_ref[1:2].astype(F32)).astype(BF16)
    put_slabs(left_ref, (5,), h)
    x2 = x1 + bias_ref[3:4].astype(F32)
    for part in range(up_w.shape[1] // width):
        span = slice(part * width, (part + 1) * width)
        u = nn(h, up_w[:, span]) + hidden_ref[:, span].astype(F32)
        acted, slope = gelu_and_slope(u)
        z = acted.astype(BF16)
        slope_ref[:, span] = slope.astype(BF16)
        turned = z.T
        for piece in range(16):
            chunk, block = part * 4 + piece // 4, piece % 4
            left_ref[1 + block, slot_of(chunk)] = turned[piece * SHARD : (piece + 1) * SHARD]
        x2 = x2 + nn(z, down_w[span, :])
    x2_low = x2.astype(BF16)
    put_slabs(left_ref, (0,), x2_low)
    y_ref[...] = ((nn(x2_low, proj_w[...]) + bias_ref[4:5].astype(F32)) * valid).astype(BF16)
    g = g_ref[...].astype(F32) * valid
    g_low = g.astype(BF16)
    gm_ref[...] = g_low
    dx2 = nt(g_low, proj_w[...])
    dx2_ref[...] = dx2
    e2_ref[...] = dx2.astype(BF16)
    add_sum(sum_ref, 0, dx2, first)
    add_sum(sum_ref, 1, g, first)


def run_feed(valid, x, a, g, gains, shifts, biases, hidden, out_w, up_w, down_w, proj_w, tile=256):
    count, width = x.shape
    ff = up_w.shape[1]
    low = jax.ShapeDtypeStruct((count, width), BF16)
    full = jax.ShapeDtypeStruct((count, width), F32)
    weights = (gains, shifts, biases, hidden, out_w, up_w, down_w, proj_w)
    return pl.pallas_call(
        feed_kernel,
        grid=(count // tile,),
        in_specs=[rows(tile, 1)] + [rows(tile, width)] * 3 + [whole(w.shape) for w in weights],
        out_specs=[
            rows(tile, width), pl.BlockSpec((7, 16, SHARD, tile), lambda i: (0, 0, 0, i)), rows(tile, ff),
            rows(tile, width), rows(tile, width), rows(tile, width), rows(tile, width), whole((2, width)),
        ],
        out_shape=[
            full, jax.ShapeDtypeStruct((7, 16, SHARD, count), BF16), jax.ShapeDtypeStruct((count, ff), BF16),
            low, low, full, low, jax.ShapeDtypeStruct((2, width), F32),
        ],
        compiler_params=params(60),
        cost_estimate=cost(2 * count * width * (3 * width + 2 * ff), count * (width * 24 + ff * 6) + 11 * MIB),
        name="feed",
    )(valid, x, a, g, *weights)


def feed_back_kernel(
    e2_ref, dx2_ref, slope_ref, x1_ref, gain_ref, out_w, up_w, down_w,
    eu_ref, dx1_ref, e1_ref, da_ref, hid_ref, sum_ref,
):
    width = e2_ref.shape[1]
    first = pl.program_id(0) == 0
    e2 = e2_ref[...]
    dh = None
    for start in range(0, up_w.shape[1], width):
        span = slice(start, start + width)
        du = nt(e2, down_w[span, :]) * slope_ref[:, span].astype(F32)
        eu = du.astype(BF16)
        eu_ref[:, span] = eu
        hid_ref[:, span] = jnp.where(first, 0.0, hid_ref[:, span]) + jnp.sum(du, 0, keepdims=True)
        part = nt(eu, up_w[:, span])
        dh = part if dh is None else dh + part
    hat, scale = norm_stats(x1_ref[...])
    dx1 = dx2_ref[...] + norm_back(dh, hat, scale, gain_ref[1:2].astype(F32))
    dx1_ref[...] = dx1
    e1 = dx1.astype(BF16)
    e1_ref[...] = e1
    da_ref[...] = nt(e1, out_w[...]).astype(BF16)
    add_sum(sum_ref, 0, dh * hat, first)
    add_sum(sum_ref, 1, dh, first)
    add_sum(sum_ref, 2, dx1, first)


def run_feed_back(e2, dx2, slope, x1, gains, out_w, up_w, down_w, tile=256):
    count, width = x1.shape
    ff = up_w.shape[1]
    low = jax.ShapeDtypeStruct((count, width), BF16)
    return pl.pallas_call(
        feed_back_kernel,
        grid=(count // tile,),
        in_specs=[rows(tile, width), rows(tile, width), rows(tile, ff), rows(tile, width)]
        + [whole(w.shape) for w in (gains, out_w, up_w, down_w)],
        out_specs=[rows(tile, ff), rows(tile, width), rows(tile, width), rows(tile, width), whole((1, ff)), whole((3, width))],
        out_shape=[
            jax.ShapeDtypeStruct((count, ff), BF16),
            jax.ShapeDtypeStruct((count, width), F32),
            low,
            low,
            jax.ShapeDtypeStruct((1, ff), F32),
            jax.ShapeDtypeStruct((3, width), F32),
        ],
        compiler_params=params(60),
        cost_estimate=cost(2 * count * width * (width + 2 * ff), count * (width * 18 + ff * 6) + 10 * MIB),
        name="feed_back",
    )(e2, dx2, slope, x1, gains, out_w, up_w, down_w)


def qkv_back_kernel(dq_ref, dk_ref, dv_ref, dx1_ref, x_ref, gain_ref, w_ref, out_ref, sum_ref):
    width = x_ref.shape[1]
    first = pl.program_id(0) == 0
    dh = nt(dq_ref[...], w_ref[:, :width])
    dh = dh + nt(dk_ref[...], w_ref[:, width : 2 * width])
    dh = dh + nt(dv_ref[...], w_ref[:, 2 * width :])
    hat, scale = norm_stats(x_ref[...].astype(F32))
    out_ref[...] = (dx1_ref[...] + norm_back(dh, hat, scale, gain_ref[0:1].astype(F32))).astype(BF16)
    add_sum(sum_ref, 0, dh * hat, first)
    add_sum(sum_ref, 1, dh, first)


def run_qkv_back(dq, dk, dv, dx1, x, gains, w, tile=256):
    count, width = x.shape
    return pl.pallas_call(
        qkv_back_kernel,
        grid=(count // tile,),
        in_specs=[rows(tile, width)] * 5 + [whole(gains.shape), whole(w.shape)],
        out_specs=[rows(tile, width), whole((2, width))],
        out_shape=[jax.ShapeDtypeStruct((count, width), BF16), jax.ShapeDtypeStruct((2, width), F32)],
        compiler_params=params(),
        cost_estimate=cost(6 * count * width * width, count * width * 14 + 6 * width * width),
        name="qkv_back",
    )(dq, dk, dv, dx1, x, gains, w)


BLOCK_COUNT = 13
RING = 6
CORE_RING = 4
SECOND_RING = 7
MODES = ('lyh', 'ylh', 'lyh', 'ylh', 'lyh', 'lyh', 'ylh', 'ylh', 'lyh', 'ylh', 'ylh', 'ylh', 'ylh')
QUERIES = 256
ABREAST = 3
VECTORS = 16
TILE = 256
MESH = pl.DeviceIdType.MESH


def one_kernel(
    group_ref, caption_ref, gain_ref, shift_ref, bias_ref, hidden_ref, cls_row_ref,
    x_hbm, g_hbm, qkv_w_hbm, out_hbm, up_hbm, down_hbm, proj_hbm,
    proj_ref, down_ref, up_ref, out_ref, qkv_ref, vec_ref, tokens_hbm, merged_hbm, qkv_hbm, h1_hbm,
    grads, got_1, got_2, got_3, got_4, lefts, pool, eu, down_w, up_w, out_w, proj_w, x1, logs, vec, vec_got,
    y_send, y_got, merged, sums,
    send_sem, recv_sem, load_sem, sum_sem, vec_send, vec_recv, tower_sem, free_sem,
):
    count, width = x1.shape
    pairs, _, _, seq = logs.shape
    half = pairs // 2
    parts = eu.shape[0]
    tiles = count // TILE
    index = lax.axis_index("dp")
    tower = lax.axis_index("tower")
    core, y, z_lo, z_hi = index % 2, index // 2 % 2, index // 4 % 2, index // 8
    by_core = {"dp": index + 1 - 2 * core}
    by_y = {"dp": index + 2 - 4 * y}
    by_lo = {"dp": index + 4 - 8 * z_lo}
    by_hi = {"dp": index + 8 - 16 * z_hi}
    by_x = {"tower": 1 - tower}

    def length(pair):
        image = jnp.where(group_ref[pair] == 1, IMG_LARGE, IMG_SMALL)
        return jnp.where(tower == 0, image, caption_ref[pair])

    barrier = pltpu.get_barrier_semaphore()
    for partner in (by_core, by_y, by_lo, by_hi, by_x):
        pl.semaphore_signal(barrier, inc=1, device_id=partner, device_id_type=MESH)

    def copy(number, source, target):
        return pltpu.make_async_copy(source, target, load_sem.at[number])

    x_copy = copy(0, x_hbm, pool.at[1])
    qkv_w_copies = [
        copy(1 + i, qkv_w_hbm.at[:, pl.ds(i * width, width)], down_w.at[pl.ds(i * width, width)]) for i in range(3)
    ]
    g_copy = copy(4, g_hbm, merged)
    out_copy = copy(5, out_hbm, out_w)
    up_copy = copy(6, up_hbm, up_w)
    proj_copy = copy(7, proj_hbm, proj_w)
    down_copy = copy(8, down_hbm, down_w)
    qkv_saves = [copy(9 + i, eu.at[i], qkv_hbm.at[i]) for i in range(3)]
    h1_save = copy(12, lefts.at[0], h1_hbm)
    h1_copy = copy(13, h1_hbm, lefts.at[0])
    qkv_copies = [copy(14 + i, qkv_hbm.at[i], down_w.at[pl.ds(i * count, count)]) for i in range(3)]
    qkv_w_again = copy(17, qkv_w_hbm, up_w.at[:, pl.ds(0, 3 * width)])
    tokens_copy = copy(18, pool.at[0], tokens_hbm)
    merged_copy = copy(19, merged, merged_hbm)

    for item in (x_copy, *qkv_w_copies, g_copy):
        item.start()
    vec[0] = jnp.zeros((VECTORS, width), F32)

    def add_to(row, value, lanes=slice(None)):
        vec[0, row : row + 1, lanes] = vec[0, row : row + 1, lanes] + jnp.sum(value, 0, keepdims=True)

    def tile_rows(tile):
        return pl.ds(pl.multiple_of(tile * TILE, TILE), TILE)

    def tile_valid(tile):
        per_pair = seq // TILE
        row = lax.broadcasted_iota(jnp.int32, (TILE, 1), 0) + tile % per_pair * TILE
        return row < length(tile // per_pair)

    def put(slot, value, at):
        turned = value.T
        for chunk in range(16):
            lefts[slot, slot_of(chunk), :, at] = turned[chunk * SHARD : (chunk + 1) * SHARD]

    gain_one, gain_two = gain_ref[0:1].astype(F32), gain_ref[1:2].astype(F32)
    shift_one, shift_two = shift_ref[0:1].astype(F32), shift_ref[1:2].astype(F32)
    biases = bias_ref[...].astype(F32)
    x_copy.wait()

    def first_norm(tile, carry):
        at = tile_rows(tile)
        hat, _ = norm_stats(pool[1, at, :].astype(F32))
        h = (hat * gain_one + shift_one).astype(BF16)
        pool[2, at, :] = h
        put(0, h, at)
        return carry

    def first_products(tile, carry):
        at = tile_rows(tile)
        h = pool[2, at, :]
        q = (nn(h, down_w[:width, :]) + biases[0:1]).astype(BF16)
        eu[0, at, :] = q * BF16(HEAD_DIM**-0.5)
        eu[1, at, :] = nn(h, down_w[width : 2 * width, :]).astype(BF16)
        eu[2, at, :] = (nn(h, down_w[2 * width : 3 * width, :]) + biases[1:2]).astype(BF16)
        return carry

    lax.fori_loop(0, tiles, first_norm, 0)
    h1_save.start()
    for item in qkv_w_copies:
        item.wait()
    lax.fori_loop(0, tiles, first_products, 0)
    for item in (*qkv_saves, down_copy, out_copy, up_copy, proj_copy):
        item.start()

    g_copy.wait()
    pl.semaphore_wait(barrier, 5)
    strip = 128
    row = lax.broadcasted_iota(jnp.int32, (strip, 1), 0)

    def cotangent(side, put_strip):
        for start in range(0, seq, strip):
            first = pl.multiple_of(side * seq + start, strip)
            value = merged[0, pl.ds(first, strip), :].astype(F32)
            after = merged[0, pl.ds(first + strip, 1), :].astype(F32)
            put_strip(start, jnp.where(row == strip - 1, after, pltpu.roll(value, strip - 1, 0)).astype(BF16))

    def put_send(start, value):
        pool[2, start : start + strip, :] = value

    def put_own(start, value):
        pool[0, pl.ds(pl.multiple_of(tower * seq + start, strip), strip), :] = value

    cotangent(1 - tower, put_send)
    own_rows = pl.ds(pl.multiple_of(tower * seq, seq), seq)
    g_swap = pltpu.make_async_remote_copy(
        pool.at[2, pl.ds(0, seq)], pool.at[0, own_rows], tower_sem.at[0], tower_sem.at[1], device_id=by_x, device_id_type=MESH
    )
    g_swap.start()
    cotangent(tower, put_own)
    vec[0, 13:14, :] = merged[0, 0:1, :].astype(F32)

    def attend_one(pair, block):
        at = pl.ds(pl.multiple_of(pair * seq, seq), seq)
        lanes = pl.ds(pl.multiple_of(block * LANES, LANES), LANES)
        valid = lax.broadcasted_iota(jnp.int32, (1, seq), 1) < length(pair)
        q, k, v = (eu[number, at, lanes] for number in range(3))
        mixed = None
        for head in range(2):
            scores = jnp.where(valid, nt(head_lanes(head, q), k), masked_score)
            largest = jnp.max(scores, 1, keepdims=True)
            weights = jnp.exp(scores - largest)
            total = jnp.sum(weights, 1, keepdims=True)
            here = nn(weights.astype(BF16), head_lanes(head, v)) * (1.0 / total)
            mixed = here if mixed is None else mixed + here
            logs[pair, block, head : head + 1, :] = (largest + jnp.log(total)).reshape(1, seq)
        pool[3, at, lanes] = mixed.astype(BF16)

    def attend(step, carry):
        steps = BLOCKS // ABREAST
        for number in range(ABREAST):
            attend_one(step // steps, step % steps * ABREAST + number)
        return carry

    lax.fori_loop(0, pairs * BLOCKS // ABREAST, attend, 0)

    for item in (h1_save, *qkv_saves, out_copy, up_copy, down_copy, proj_copy):
        item.wait()

    def feed(tile, carry):
        at = tile_rows(tile)
        a = pool[3, at, :]
        put(6, a, at)
        mid = pool[1, at, :].astype(F32) + nn(a, out_w[...]) + biases[2:3]
        x1[at, :] = mid
        hat, _ = norm_stats(mid)
        h = (hat * gain_two + shift_two).astype(BF16)
        put(5, h, at)
        x2 = mid + biases[3:4]
        for part in range(parts):
            span = slice(part * width, (part + 1) * width)
            u = nn(h, up_w[:, span]) + hidden_ref[:, span].astype(F32)
            acted, slope = gelu_and_slope(u)
            z = acted.astype(BF16)
            eu[part, at, :] = slope.astype(BF16)
            turned = z.T
            for piece in range(16):
                chunk, block = part * 4 + piece // 4, piece % 4
                lefts[1 + block, slot_of(chunk), :, at] = turned[piece * SHARD : (piece + 1) * SHARD]
            x2 = x2 + nn(z, down_w[span, :])
        x2_low = x2.astype(BF16)
        put(0, x2_low, at)
        rows_y = jnp.where(tile_valid(tile), nn(x2_low, proj_w[...]) + biases[4:5], 0.0).astype(BF16)
        per_pair = seq // TILE
        here = pl.ds(pl.multiple_of(tile % per_pair * TILE, TILE), TILE)

        @pl.when(tile // per_pair == tower)
        def _():
            merged[0, here, :] = rows_y

        @pl.when(tile // per_pair != tower)
        def _():
            y_send[here, :] = rows_y

        return carry

    lax.fori_loop(0, tiles, feed, 0)
    y_swap = pltpu.make_async_remote_copy(
        y_send, y_got, tower_sem.at[2], tower_sem.at[3], device_id=by_x, device_id_type=MESH
    )
    y_swap.start()

    g_swap.wait()

    def cotangent_rows(tile, carry):
        at = tile_rows(tile)
        g = jnp.where(tile_valid(tile), pool[0, at, :].astype(F32), 0.0)
        pool[0, at, :] = g.astype(BF16)
        add_to(4, g)
        return carry

    lax.fori_loop(0, tiles, cotangent_rows, 0)

    def project_back(tile, carry):
        at = tile_rows(tile)
        dx2 = nt(pool[0, at, :], proj_w[...])
        pool[2, at, :] = dx2.astype(BF16)
        add_to(3, dx2)
        return carry

    def bits(block):
        ways = {"y": (by_y, y), "l": (by_lo, z_lo), "h": (by_hi, z_hi)}
        partners, sides = zip(*(ways[letter] for letter in MODES[block]))
        return (by_core, *partners), sides

    def shelf(block):
        if 5 <= block < 9:
            return lefts, block - 4
        return grads, (block if block < 5 else block - 4) % RING

    def shards(block, of_core, first, size):
        buffer, slot = shelf(block)
        return buffer.at[slot, pl.ds(of_core * 8 + first, size), :, pl.ds(0, width)]

    gots = (got_1, got_2, got_3, got_4)

    def place(block, level):
        return block % (CORE_RING, SECOND_RING, BLOCK_COUNT, BLOCK_COUNT)[level]

    def swap_of(block, level):
        partners, (b1, b2, b3) = bits(block)
        if level == 0:
            source = shards(block, 1 - core, 0, 8)
        elif level == 1:
            source = shards(block, core, (1 - b1) * 4, 4)
        elif level == 2:
            source = shards(block, core, b1 * 4 + (1 - b2) * 2, 2)
        else:
            source = shards(block, core, b1 * 4 + b2 * 2 + 1 - b3, 1)
        return pltpu.make_async_remote_copy(
            source,
            gots[level].at[place(block, level)],
            send_sem.at[level, block],
            recv_sem.at[level, block],
            device_id=partners[level],
            device_id_type=MESH,
        )

    def advance(block, level):
        _, (b1, b2, b3) = bits(block)
        buffer, slot = shelf(block)
        swap_of(block, level - 1).wait_recv()
        got = gots[level - 1]
        size = 8 >> level
        bit = (b1, b2, b3)[level - 1]
        base = (0, b1 * 4, b1 * 4 + b2 * 2)[level - 1]
        for other in (1, 0):
            side = (1 - bit) if other else bit

            def add(i, carry, side=side):
                at = side * size + i
                here = core * 8 + base + at
                total = buffer[slot, here, :, :width].astype(F32) + got[place(block, level - 1), at].astype(F32)
                buffer[slot, here, :, :width] = total.astype(BF16)
                return carry

            lax.fori_loop(0, size, add, 0)
            if other:
                if level == 1 and block >= SECOND_RING:
                    assert (block - SECOND_RING, 2) in done
                    pl.semaphore_wait(free_sem.at[1, block], 1)
                swap_of(block, level).start()
        later = block + (CORE_RING, SECOND_RING, BLOCK_COUNT)[level - 1]
        if later < BLOCK_COUNT:
            pl.semaphore_signal(
                free_sem.at[level - 1, later], inc=1, device_id=bits(later)[0][level - 1], device_id_type=MESH
            )

    def sum_copies(block, slot):
        if block == 0:
            target = proj_ref
        elif block < 5:
            target = down_ref.at[pl.ds((block - 1) * SHARD, SHARD)]
        elif block < 9:
            target = up_ref.at[:, pl.ds((block - 5) * width, width)]
        elif block == 9:
            target = out_ref
        else:
            piece = 2 * LANES
            return [
                pltpu.make_async_copy(
                    sums.at[slot, :, pl.ds(i * piece, piece)],
                    qkv_ref.at[:, pl.ds(i * width + (block - 10) * piece, piece)],
                    sum_sem.at[slot, i],
                )
                for i in range(3)
            ]
        return [pltpu.make_async_copy(sums.at[slot], target, sum_sem.at[slot, 0])]

    finished = []

    def finish(block):
        _, (b1, b2, b3) = bits(block)
        swap_of(block, 3).wait_recv()
        buffer, slot = shelf(block)
        total = buffer[slot, core * 8 + b1 * 4 + b2 * 2 + b3, :, :width].astype(F32) + got_4[block, 0].astype(F32)
        if len(finished) >= 3:
            for item in sum_copies(finished[-3], (len(finished) - 3) % 3):
                item.wait()
        place_now = len(finished) % 3
        sums[place_now] = total
        for item in sum_copies(block, place_now):
            item.start()
        finished.append(block)
        for level in range(4):
            swap_of(block, level).wait_send()

    done = set()

    def tick(*work):
        for block, level in work:
            assert (block, level) not in done and (level == 1 or (block, level - 1) in done)
            done.add((block, level))
            if level == 4:
                finish(block)
            else:
                advance(block, level)

    def weight_grad(block, number, right):
        assert block < 10 or (block - 10, 4) in done
        assert block < CORE_RING or (block - CORE_RING, 1) in done
        left = lefts[number].reshape(16 * SHARD, count)
        buffer, slot = shelf(block)
        step = 256

        def columns(i, carry):
            at = pl.ds(pl.multiple_of(i * step, step), step)
            product = nn(left, right(i, at)).astype(BF16).reshape(16, SHARD, step)
            if MODES[block] == "ylh":
                buffer[slot, :, :, at] = product
            else:
                for number in range(16):
                    side = {"y": number // 4 % 2, "l": number // 2 % 2, "h": number % 2}
                    a, b, c = (side[letter] for letter in MODES[block])
                    buffer[slot, number // 8 * 8 + a * 4 + b * 2 + c, :, at] = product[number]
            return carry

        lax.fori_loop(0, width // step, columns, 0)
        if block >= CORE_RING:
            pl.semaphore_wait(free_sem.at[0, block], 1)
        swap_of(block, 0).start()

    weight_grad(0, 0, lambda i, at: pool[0, :, at])
    h1_copy.start()
    lax.fori_loop(0, tiles, project_back, 0)
    tick(*TICKS["e2", 0])
    for part in range(parts):
        weight_grad(1 + part, 1 + part, lambda i, at: pool[2, :, at])
        tick(*TICKS["down", part])

    for part in range(parts):

        def tile_du(tile, carry, part=part):
            at = tile_rows(tile)
            du = nt(pool[2, at, :], down_w[part * width : (part + 1) * width, :])
            du = du * eu[part, at, :].astype(F32)
            eu[part, at, :] = du.astype(BF16)
            add_to(9 + part, du)
            return carry

        lax.fori_loop(0, tiles, tile_du, 0)
        tick(*TICKS["du", part])
    for item in qkv_copies:
        item.start()

    for part in range(parts):
        weight_grad(5 + part, 5, lambda i, at, part=part: eu[part, :, at])
        tick(*TICKS["up", part])

    for number in range(tiles):

        def mid_back(tile, carry):
            at = tile_rows(tile)
            dh = nt(eu[0, at, :], up_w[:, :width])
            for part in range(1, parts):
                dh = dh + nt(eu[part, at, :], up_w[:, part * width : (part + 1) * width])
            hat, scale = norm_stats(x1[at, :])
            dx1 = nt(pool[0, at, :], proj_w[...]) + norm_back(dh, hat, scale, gain_two)
            x1[at, :] = dx1
            e1 = dx1.astype(BF16)
            pool[2, at, :] = e1
            pool[0, at, :] = nt(e1, out_w[...]).astype(BF16)
            add_to(6, dh * hat)
            add_to(8, dh)
            add_to(2, dx1)
            return carry

        lax.fori_loop(number, number + 1, mid_back, 0)
        tick(*TICKS["mid", number])
    qkv_w_again.start()

    weight_grad(9, 6, lambda i, at: pool[2, :, at])
    tick(*TICKS["out", 0])

    for item in (*qkv_copies, h1_copy):
        item.wait()
    per_loop = 2
    for turn in range(pairs * BLOCKS // per_loop):

        def attend_back_one(step):
            pair, block = step // 2 % pairs, step // (2 * pairs) * 2 + step % 2
            at = pl.ds(pl.multiple_of(pair * seq, seq), seq)
            lanes = pl.ds(pl.multiple_of(block * LANES, LANES), LANES)
            valid = lax.broadcasted_iota(jnp.int32, (seq, 1), 0) < length(pair)
            q, k, v = (
                down_w[pl.ds(pl.multiple_of(number * count + pair * seq, seq), seq), lanes] for number in range(3)
            )
            d = pool[0, at, lanes]
            log_rows = logs[pair, block]
            k_t = k.T
            d_t = d.T
            prod_t = d_t.astype(F32) * pool[3, at, lanes].T.astype(F32)
            dq_rows = []
            dk = None
            dv = None
            for head in range(2):
                span = slice(head * HEAD_DIM, (head + 1) * HEAD_DIM)
                row_dot = jnp.sum(prod_t[span], 0, keepdims=True)
                v_here = head_lanes(head, v)
                dq_parts = []
                for start in range(0, seq, QUERIES):
                    some = slice(start, start + QUERIES)
                    q_here = head_lanes(head, q[some])
                    scores = jnp.where(valid, nt(k, q_here), masked_score)
                    probs = jnp.exp(scores - log_rows[head : head + 1, some])
                    d_probs = nn(v_here, d_t[:, some])
                    d_scores = (probs * (d_probs - row_dot[:, some])).astype(BF16)
                    dv_here = nn(probs.astype(BF16), head_lanes(head, d[some]))
                    dk_here = nn(d_scores, q_here)
                    dq_parts.append(nn(k_t[span], d_scores))
                    dk = dk_here if dk is None else dk + dk_here
                    dv = dv_here if dv is None else dv + dv_here
                dq_rows.append(jnp.concatenate(dq_parts, 1))
            dq = jnp.concatenate(dq_rows, 0).T * HEAD_DIM**-0.5
            for number, value in ((0, dq), (1, dk), (2, dv)):
                eu[number, at, lanes] = value.astype(BF16)
            add_to(0, dq, lanes)
            add_to(1, dv, lanes)

        def attend_back(step, carry):
            for number in range(per_loop):
                attend_back_one(step * per_loop + number)
            return carry

        lax.fori_loop(turn, turn + 1, attend_back, 0)
        tick(*TICKS["attend", turn])
        if turn % 2 == 1:
            third = turn // 2
            some = pl.ds(third * 2 * LANES, 2 * LANES)
            weight_grad(10 + third, 0, lambda i, at, some=some: eu[i, :, some])
            tick(*TICKS["qkv", third])

    qkv_w_again.wait()
    for number in range(tiles):

        def first_back(tile, carry):
            at = tile_rows(tile)
            dh = nt(eu[0, at, :], up_w[:, :width])
            for part in (1, 2):
                dh = dh + nt(eu[part, at, :], up_w[:, part * width : (part + 1) * width])
            hat, scale = norm_stats(pool[1, at, :].astype(F32))
            pool[0, at, :] = (x1[at, :] + norm_back(dh, hat, scale, gain_one)).astype(BF16)
            add_to(5, dh * hat)
            add_to(7, dh)
            return carry

        lax.fori_loop(number, number + 1, first_back, 0)
        tick(*TICKS["first", number])
    tokens_copy.start()

    def vec_swap(level):
        return pltpu.make_async_remote_copy(
            vec.at[level],
            vec_got.at[level],
            vec_send.at[level],
            vec_recv.at[level],
            device_id=(by_core, by_y, by_lo, by_hi, by_x)[level],
            device_id_type=MESH,
        )

    vec_swap(0).start()

    y_swap.wait()

    def projected(side, start, size):
        own = merged[0, start : start + size, :].astype(F32)
        got = y_got[start : start + size, :].astype(F32)
        return jnp.where(tower == side, own, got)

    merged[0, 2 * seq : 2 * seq + 1, :] = projected(1, seq - 16, 16)[15:16].astype(BF16)
    for side in (1, 0):
        for start in range(seq - strip, -1, -strip):
            value = projected(side, start, strip)
            if start > 0:
                before = projected(side, start - 16, 16)[15:16]
            elif side == 1:
                before = projected(0, seq - 16, 16)[15:16]
            else:
                before = cls_row_ref[...].reshape(1, width).astype(F32)
            moved = jnp.where(row == 0, before, pltpu.roll(value, 1, 0))
            merged[0, side * seq + start : side * seq + start + strip, :] = moved.astype(BF16)
    merged_copy.start()

    for number, work in enumerate(TICKS["tail", 0]):
        tick(work)
        if number < 4:
            vec_swap(number).wait_recv()
            vec[number + 1] = vec[number] + vec_got[number]
            vec_swap(number + 1).start()
    vec_swap(4).wait_recv()
    vec_ref[0:13] = vec[4, 0:13]
    vec_ref[13:16] = vec[4, 13:16] + vec_got[4, 13:16]
    for level in range(5):
        vec_swap(level).wait_send()
    for number in range(BLOCK_COUNT - 3, BLOCK_COUNT):
        for item in sum_copies(finished[number], number % 3):
            item.wait()
    tokens_copy.wait()
    merged_copy.wait()
    assert len(done) == 4 * BLOCK_COUNT


TICKS = {
    ('proj', 0): [],
    ('e2', 0): [],
    ('down', 0): [],
    ('down', 1): [(0, 1)],
    ('down', 2): [],
    ('down', 3): [(1, 1)],
    ('du', 0): [(2, 1)],
    ('du', 1): [(3, 1), (4, 1)],
    ('du', 2): [(0, 2)],
    ('du', 3): [],
    ('up', 0): [(1, 2)],
    ('up', 1): [],
    ('up', 2): [(2, 2)],
    ('up', 3): [(5, 1)],
    ('mid', 0): [(3, 2), (6, 1), (7, 1)],
    ('mid', 1): [(0, 3), (4, 2), (8, 1)],
    ('mid', 2): [(1, 3), (2, 3)],
    ('mid', 3): [],
    ('out', 0): [],
    ('attend', 0): [(5, 2), (6, 2)],
    ('attend', 1): [(0, 4), (3, 3), (7, 2), (9, 1)],
    ('qkv', 0): [],
    ('attend', 2): [(4, 3), (8, 2)],
    ('attend', 3): [(1, 4), (2, 4), (5, 3), (10, 1)],
    ('qkv', 1): [(6, 3)],
    ('attend', 4): [(3, 4), (9, 2), (11, 1)],
    ('attend', 5): [(4, 4), (5, 4), (7, 3), (8, 3)],
    ('qkv', 2): [(6, 4)],
    ('first', 0): [(10, 2)],
    ('first', 1): [(9, 3), (12, 1), (7, 4)],
    ('first', 2): [],
    ('first', 3): [(8, 4), (11, 2)],
    ('tail', 0): [(10, 3), (9, 4), (12, 2), (11, 3), (10, 4), (12, 3), (11, 4), (12, 4)],
}


def run_one(group_id, caption_len, gains, shifts, biases, hidden, cls_row, x, g, qkv_w, out_w, up_w, down_w, proj_w):
    count, width = x.shape
    ff = up_w.shape[1]
    pairs = group_id.shape[0]
    seq = count // pairs
    shard = jax.ShapeDtypeStruct
    vmem = pl.BlockSpec(memory_space=pltpu.VMEM)
    hbm = pl.BlockSpec(memory_space=pl.ANY)
    return pl.pallas_call(
        one_kernel,
        in_specs=[pl.BlockSpec(memory_space=pltpu.SMEM)] * 2 + [vmem] * 5 + [hbm] * 7,
        out_specs=[hbm] * 5 + [vmem] + [hbm] * 4,
        out_shape=[
            shard((SHARD, width), F32),
            shard((4 * SHARD, width), F32),
            shard((SHARD, ff), F32),
            shard((SHARD, width), F32),
            shard((SHARD, 3 * width), F32),
            shard((VECTORS, width), F32),
            shard((count, width), BF16),
            shard(g.shape, BF16),
            shard((3, count, width), BF16),
            shard((16, SHARD, count), BF16),
        ],
        scratch_shapes=[
            pltpu.VMEM((RING, 16, SHARD, width), BF16),
            pltpu.VMEM((CORE_RING, 8, SHARD, width), BF16),
            pltpu.VMEM((SECOND_RING, 4, SHARD, width), BF16),
            pltpu.VMEM((BLOCK_COUNT, 2, SHARD, width), BF16),
            pltpu.VMEM((BLOCK_COUNT, 1, SHARD, width), BF16),
            pltpu.VMEM((7, 16, SHARD, count), BF16),
            pltpu.VMEM((4, count, width), BF16),
            pltpu.VMEM((ff // width, count, width), BF16),
            pltpu.VMEM((ff, width), BF16),
            pltpu.VMEM((width, ff), BF16),
            pltpu.VMEM((width, width), BF16),
            pltpu.VMEM((width, width), BF16),
            pltpu.VMEM((count, width), F32),
            pltpu.VMEM((pairs, BLOCKS, 2, seq), F32),
            pltpu.VMEM((5, VECTORS, width), F32),
            pltpu.VMEM((5, VECTORS, width), F32),
            pltpu.VMEM((seq, width), BF16),
            pltpu.VMEM((seq, width), BF16),
            pltpu.VMEM(g.shape, BF16),
            pltpu.VMEM((3, SHARD, width), F32),
            pltpu.SemaphoreType.DMA((4, BLOCK_COUNT)),
            pltpu.SemaphoreType.DMA((4, BLOCK_COUNT)),
            pltpu.SemaphoreType.DMA((20,)),
            pltpu.SemaphoreType.DMA((3, 3)),
            pltpu.SemaphoreType.DMA((5,)),
            pltpu.SemaphoreType.DMA((5,)),
            pltpu.SemaphoreType.DMA((4,)),
            pltpu.SemaphoreType.REGULAR((2, BLOCK_COUNT)),
        ],
        compiler_params=pltpu.CompilerParams(
            collective_id=0, has_side_effects=True, vmem_limit_bytes=63 * MIB
        ),
        cost_estimate=cost(60e9, 60 * MIB),
        name="one",
    )(group_id, caption_len, gains, shifts, biases, hidden, cls_row, x, g, qkv_w, out_w, up_w, down_w, proj_w)


def full_grad_kernel(left_ref, *refs):
    start = 0
    for right_ref in refs[:-1]:
        stop = start + right_ref.shape[1]
        refs[-1][:, start:stop] = nn(left_ref[...], right_ref[...])
        start = stop


def run_full_grad(left, *rights):
    height, count = left.shape
    width = sum(right.shape[1] for right in rights)
    tile = 384
    return pl.pallas_call(
        full_grad_kernel,
        grid=(height // tile,),
        in_specs=[rows(tile, count)] + [whole(right.shape) for right in rights],
        out_specs=rows(tile, width),
        out_shape=jax.ShapeDtypeStruct((height, width), F32),
        compiler_params=params(),
        name="full_grad",
    )(left, *rights)


def in_order(slabs):
    return jnp.stack([slabs[..., slot_of(chunk), :, :] for chunk in range(16)], -3)


def plain_back(lengths, logs, gains, feed_sums, cls_sum, left, h1, slope, g, e2, dx2, x1, a, qkv, x, y, down_w, up_w, out_w, qkv_w):
    count, width = x.shape
    seq = y.shape[2]
    eu, dx1, e1, da, hidden_sum, mid_sums = run_feed_back(e2, dx2, slope, x1, gains, out_w, up_w, down_w)
    dq, dk, dv, sum_q, sum_v = run_attend_back(lengths, qkv, a, da, logs, seq)
    tokens_grad, first_sums = run_qkv_back(dq, dk, dv, dx1, x, gains, qkv_w)
    turned = in_order(left)
    z = turned[1:5].transpose(1, 0, 2, 3).reshape(4 * width, count)
    x2, h2, a_t = (turned[i].reshape(width, count) for i in (0, 5, 6))
    h1 = in_order(h1).reshape(width, count)
    grads = (run_full_grad(x2, g), run_full_grad(z, e2), run_full_grad(h2, eu), run_full_grad(a_t, e1), run_full_grad(h1, dq, dk, dv))
    grads = [lax.psum_scatter(grad, "dp", scatter_dimension=0, tiled=True) for grad in grads]
    vectors = jnp.concatenate(
        [
            jnp.sum(sum_q, 0), jnp.sum(sum_v, 0), mid_sums[2:3], feed_sums, first_sums[0:1], mid_sums[0:1],
            first_sums[1:2], mid_sums[1:2], hidden_sum.reshape(-1, width),
        ],
        axis=0,
    )
    vectors = lax.psum(vectors, "dp")
    cls = lax.psum(cls_sum, ("tower", "dp"))
    y_got = lax.ppermute(take(y, 1 - lax.axis_index("tower")), "tower", [(0, 1), (1, 0)])
    return grads, vectors, cls, tokens_grad, y_got


def take(value, index):
    return lax.dynamic_index_in_dim(value, index, 0, keepdims=False)


PIECE = 256


def spread_kernel(index_ref, vec_ref, *refs):
    sources, (gain_ref, shift_ref, bias_ref, hidden_ref, cls_ref), targets, held = refs[:7], refs[7:12], refs[12:19], refs[19:26]
    sem_in, sem_out = refs[26:]
    ins, outs = [], []
    for source, there, target in zip(sources, held, targets):
        size = source.shape[0]
        step = PIECE if size % PIECE == 0 else size
        for start in range(0, size, step):
            number, at = len(ins), pl.ds(start, step)
            ins.append(pltpu.make_async_copy(source.at[at], there.at[at], sem_in.at[number]))
            outs.append(pltpu.make_async_copy(there.at[at], target.at[at], sem_out.at[number]))
    for item in ins:
        item.start()
    index = index_ref[0]
    width = vec_ref.shape[1]
    piece = gain_ref.shape[1]
    mine = pltpu.roll(vec_ref[...], width - piece * index, 1)[:, :piece]
    for number in range(5):
        bias_ref[number] = mine[number : number + 1]
    gain_ref[...] = mine[5:7]
    shift_ref[...] = mine[7:9]
    share = hidden_ref.shape[1]
    per_row = width // share
    row = vec_ref[pl.ds(9 + index // per_row, 1), :]
    hidden_ref[...] = pltpu.roll(row, width - share * (index % per_row), 1)[:, :share]
    cls_ref[...] = vec_ref[13]
    for before, after in zip(ins, outs):
        before.wait()
        after.start()
    for item in outs:
        item.wait()


def run_spread(index, vectors, *arrays):
    width = vectors.shape[1]
    small = [jax.ShapeDtypeStruct(shape, F32) for shape in ((2, width // 16), (2, width // 16), (5, 1, width // 16), (1, width // 4), (width,))]
    vmem = pl.BlockSpec(memory_space=pltpu.VMEM)
    hbm = pl.BlockSpec(memory_space=pl.ANY)
    return pl.pallas_call(
        spread_kernel,
        in_specs=[pl.BlockSpec(memory_space=pltpu.SMEM), vmem] + [hbm] * len(arrays),
        out_specs=[vmem] * 5 + [hbm] * len(arrays),
        out_shape=small + [jax.ShapeDtypeStruct(array.shape, array.dtype) for array in arrays],
        scratch_shapes=[pltpu.VMEM(array.shape, array.dtype) for array in arrays]
        + [pltpu.SemaphoreType.DMA((16,))] * 2,
        compiler_params=params(62),
        name="spread",
    )(index, vectors, *arrays)


def local(
    dp, tokens, group_id, caption_len, cls_row, norm_gains, shifts, bias_model, bias_hidden,
    w_qkv, w_out, w_up, w_down, w_proj, merged_grad,
):
    tower = lax.axis_index("tower")
    index = lax.axis_index("dp")
    pairs, seq, width = tokens.shape[1:]
    half = pairs // 2
    count = pairs * seq
    image_len = jnp.where(group_id == 1, IMG_LARGE, IMG_SMALL)
    lengths = jnp.where(tower == 0, image_len, caption_len).astype(jnp.int32)
    gains, shift_rows, biases, hidden = norm_gains[0], shifts[0], bias_model[0], bias_hidden
    qkv_w, out_w, up_w, down_w, proj_w = w_qkv[0], w_out[0], w_up[0], w_down[0], w_proj[0]
    x = tokens[0].reshape(count, width)

    if dp == 16 and pairs == 2:
        *grads, vectors, tokens_grad, merged_input, _, _ = run_one(
            group_id, caption_len, gains, shift_rows, biases, hidden, cls_row, x, merged_grad[0], qkv_w, out_w, up_w, down_w, proj_w
        )
        gain_sum, shift_sum, bias_sum, hidden_sum, cls, *arrays = run_spread(
            index.astype(jnp.int32)[None], vectors, merged_input, tokens_grad, *grads
        )
        bias_sum = bias_sum.transpose(1, 0, 2)[0]
        merged_input, tokens_grad, proj, down, up, out, qkv_grad = arrays
    else:
        positions = lax.broadcasted_iota(jnp.int32, (pairs, seq), 1)
        valid = (positions < lengths[:, None]).reshape(count, 1).astype(F32)
        image_grad = merged_grad[0, :, 1 : 1 + seq]
        text_grad = merged_grad[0, :, 1 + seq :]
        g_keep = jnp.where(tower == 0, image_grad, text_grad)
        g_send = jnp.where(tower == 0, text_grad, image_grad)
        g_got = lax.ppermute(g_send, "tower", [(0, 1), (1, 0)])
        cls_sum = jnp.sum(merged_grad[0, :, 0].astype(F32), 0)[None]
        h1, qkv = run_qkv(x, gains, shift_rows, biases, qkv_w)
        mixed, logs = run_attend(lengths, qkv, seq)
        g = jnp.where(tower == 0, jnp.stack([g_keep, g_got]), jnp.stack([g_got, g_keep])).reshape(count, width)
        x1, left, slope, y, g_low, dx2, e2, feed_sums = run_feed(
            valid, x, mixed, g, gains, shift_rows, biases, hidden, out_w, up_w, down_w, proj_w
        )
        y = y.reshape(2, half, seq, width)
        grads, vectors, cls, tokens_grad, y_got = plain_back(
            lengths, logs, gains, feed_sums, cls_sum, left, h1, slope, g_low, e2, dx2, x1, mixed, qkv, x, y,
            down_w, up_w, out_w, qkv_w,
        )
        proj, down, up, out, qkv_grad = grads
        y_own = take(y, tower)
        cls_block = jnp.broadcast_to(cls_row.reshape(1, 1, width), (half, 1, width))
        image_rows = jnp.where(tower == 0, y_own, y_got)
        text_rows = jnp.where(tower == 0, y_got, y_own)
        merged_input = jnp.concatenate([cls_block, image_rows, text_rows], axis=1)
        mine = lax.dynamic_slice_in_dim(vectors[:9], index * (width // dp), width // dp, 1)
        bias_sum, gain_sum, shift_sum = mine[0:5], mine[5:7], mine[7:9]
        ff = up_w.shape[1]
        hidden_sum = lax.dynamic_slice_in_dim(vectors[9:13].reshape(1, ff), index * (ff // dp), ff // dp, 1)
    return (
        merged_input[None], tokens_grad.reshape(tokens.shape), cls.reshape(width), gain_sum[None], shift_sum[None],
        bias_sum[None], hidden_sum, qkv_grad[None], out[None], up[None], down[None], proj[None],
    )


def solution(mesh):
    tower = P("tower", None, None)
    in_specs = (
        P("tower", "dp", None, None), P("dp"), P("dp"), P(), tower, tower, tower, P("tower", None),
        tower, tower, tower, tower, tower, P("tower", "dp", None, None),
    )
    spread = P("tower", None, "dp")
    weight = P("tower", "dp", None)
    out_specs = (
        P("tower", "dp", None, None), P("tower", "dp", None, None), P(), spread, spread, spread, P("tower", "dp"),
        weight, weight, weight, weight, weight,
    )
    return jax.shard_map(
        partial(local, mesh.shape["dp"]), mesh=mesh, in_specs=in_specs, out_specs=out_specs, check_vma=False
    )
```

```python
from functools import partial

import jax
import jax.numpy as jnp
from jax import lax
from jax.experimental import pallas as pl
from jax.experimental.pallas import tpu as pltpu
from jax.sharding import PartitionSpec as P

HEADS = 12
HEAD_DIM = 64
IMG_SMALL = 197
IMG_LARGE = 325
LANES = 128
BLOCKS = HEADS * HEAD_DIM // LANES

norm_eps = 1e-06
masked_score = -1e30
F32 = jnp.float32
BF16 = jnp.bfloat16
MIB = 1 << 20
SHARD = 48

ERF_P = 0.39
ERF_C = (0.2344334842, 0.09695712066, 0.6357617632, -0.6184387086, 0.8763152235, -0.225028871)


def nn(left, right):
    return jnp.dot(left, right, preferred_element_type=F32)


def nt(left, right):
    return lax.dot_general(left, right, (((1,), (1,)), ((), ())), preferred_element_type=F32)


def tn(left, right):
    return lax.dot_general(left, right, (((0,), (0,)), ((), ())), preferred_element_type=F32)


def params(vmem=48, semantics=None):
    return pltpu.CompilerParams(vmem_limit_bytes=vmem * MIB, dimension_semantics=semantics)


def cost(flops, nbytes, trans=0):
    return pl.CostEstimate(flops=int(flops), bytes_accessed=int(nbytes), transcendentals=int(trans))


def whole(shape):
    return pl.BlockSpec(shape, lambda *_: (0,) * len(shape), pipeline_mode=pl.Buffered(1))


def rows(tile, width):
    return pl.BlockSpec((tile, width), lambda i, *_: (i, 0))


def norm_stats(x):
    mean = jnp.mean(x, -1, keepdims=True)
    centred = x - mean
    spread = jnp.mean(centred * centred, -1, keepdims=True)
    scale = lax.rsqrt(spread + norm_eps)
    return centred * scale, scale


def norm_back(grad, hat, scale, gain):
    d_hat = grad * gain
    first = jnp.mean(d_hat, -1, keepdims=True)
    second = jnp.mean(d_hat * hat, -1, keepdims=True)
    return scale * (d_hat - first - hat * second)


def gelu_and_slope(u):
    bell = jnp.exp2(u * u * (-0.5 * 1.4426950408889634))
    t = 1.0 / (1.0 + (ERF_P * 0.5**0.5) * jnp.abs(u))
    poly = jnp.full_like(u, 0.5 * ERF_C[-1])
    for c in ERF_C[-2::-1]:
        poly = poly * t + 0.5 * c
    tail = poly * t * bell
    phi = jnp.where(u >= 0, 1.0 - tail, tail)
    slope = phi + u * bell * 0.3989422804014327
    return u * phi, slope


def slot_of(chunk):
    z_hi, z_lo, y, core = chunk // 8, chunk // 4 % 2, chunk // 2 % 2, chunk % 2
    return ((core * 2 + y) * 2 + z_lo) * 2 + z_hi


def put_slabs(ref, lead, value):
    turned = value.T
    for chunk in range(16):
        ref[(*lead, slot_of(chunk))] = turned[chunk * SHARD : (chunk + 1) * SHARD]


def add_sum(ref, index, value, first):
    ref[index : index + 1, :] = jnp.where(first, 0.0, ref[index : index + 1, :]) + jnp.sum(value, 0, keepdims=True)


def qkv_kernel(x_ref, gain_ref, shift_ref, bias_ref, w_ref, h_ref, out_ref):
    width = x_ref.shape[1]
    hat, _ = norm_stats(x_ref[...].astype(F32))
    h = (hat * gain_ref[0:1].astype(F32) + shift_ref[0:1].astype(F32)).astype(BF16)
    put_slabs(h_ref, (), h)
    q = nn(h, w_ref[:, :width]) + bias_ref[0:1].astype(F32)
    out_ref[:, :width] = q.astype(BF16) * BF16(HEAD_DIM**-0.5)
    out_ref[:, width : 2 * width] = nn(h, w_ref[:, width : 2 * width]).astype(BF16)
    v = nn(h, w_ref[:, 2 * width :]) + bias_ref[1:2].astype(F32)
    out_ref[:, 2 * width :] = v.astype(BF16)


def run_qkv(x, gains, shifts, biases, w, tile=256):
    count, width = x.shape
    return pl.pallas_call(
        qkv_kernel,
        grid=(count // tile,),
        in_specs=[rows(tile, width), whole(gains.shape), whole(shifts.shape), whole(biases.shape), whole(w.shape)],
        out_specs=[pl.BlockSpec((16, SHARD, tile), lambda i: (0, 0, i)), rows(tile, 3 * width)],
        out_shape=[
            jax.ShapeDtypeStruct((16, SHARD, count), BF16),
            jax.ShapeDtypeStruct((count, 3 * width), BF16),
        ],
        compiler_params=params(),
        cost_estimate=cost(6 * count * width * width, 2 * (count * width * 5 + 3 * width * width)),
        name="qkv",
    )(x, gains, shifts, biases, w)


def head_lanes(head, block):
    lane = lax.broadcasted_iota(jnp.int32, (1, LANES), 1)
    keep = (lane < HEAD_DIM) if head == 0 else (lane >= HEAD_DIM)
    return jnp.where(keep, block, jnp.zeros_like(block))


def attend_kernel(len_ref, q_ref, k_ref, v_ref, a_ref, l_ref):
    seq = q_ref.shape[0]
    valid = lax.broadcasted_iota(jnp.int32, (seq, 1), 0) < len_ref[pl.program_id(0)]
    q = q_ref[...]
    k = k_ref[...]
    v_t = v_ref[...].T
    parts = []
    for head in range(2):
        scores = jnp.where(valid, nt(k, head_lanes(head, q)), masked_score)
        largest = jnp.max(scores, 0, keepdims=True)
        weights = jnp.exp(scores - largest)
        total = jnp.sum(weights, 0, keepdims=True)
        mixed = nn(v_t[head * HEAD_DIM : (head + 1) * HEAD_DIM], weights.astype(BF16))
        parts.append((mixed * (1.0 / total)).astype(BF16))
        l_ref[0, 0, head : head + 1, :] = largest + jnp.log(total)
    a_ref[...] = jnp.concatenate(parts, 0).T


def column(seq, shift):
    return pl.BlockSpec((seq, LANES), lambda p, b, *_: (p, b + shift))


def run_attend(lengths, qkv, seq):
    count = qkv.shape[0]
    width = qkv.shape[1] // 3
    pairs = count // seq
    return pl.pallas_call(
        attend_kernel,
        grid_spec=pltpu.PrefetchScalarGridSpec(
            num_scalar_prefetch=1,
            grid=(pairs, BLOCKS),
            in_specs=[column(seq, 0), column(seq, BLOCKS), column(seq, 2 * BLOCKS)],
            out_specs=[column(seq, 0), pl.BlockSpec((1, 1, 2, seq), lambda p, b, *_: (p, b, 0, 0))],
        ),
        out_shape=[
            jax.ShapeDtypeStruct((count, width), BF16),
            jax.ShapeDtypeStruct((pairs, BLOCKS, 2, seq), F32),
        ],
        compiler_params=params(),
        cost_estimate=cost(16 * pairs * HEADS * seq * seq * HEAD_DIM, 8 * count * width, pairs * HEADS * seq * seq),
        name="attend",
    )(lengths, qkv, qkv, qkv)


def attend_back_kernel(len_ref, q_ref, k_ref, v_ref, a_ref, d_ref, l_ref, dq_ref, dk_ref, dv_ref, sq_ref, sv_ref):
    seq = q_ref.shape[0]
    valid = lax.broadcasted_iota(jnp.int32, (seq, 1), 0) < len_ref[pl.program_id(0)]
    q = q_ref[...]
    k = k_ref[...]
    v = v_ref[...]
    d = d_ref[...]
    k_t = k.T
    d_t = d.T
    prod_t = d_t.astype(F32) * a_ref[...].T.astype(F32)
    dq_parts = []
    dk = None
    dv = None
    for head in range(2):
        span = slice(head * HEAD_DIM, (head + 1) * HEAD_DIM)
        q_here = head_lanes(head, q)
        scores = jnp.where(valid, nt(k, q_here), masked_score)
        probs = jnp.exp(scores - l_ref[0, 0, head : head + 1, :])
        row_dot = jnp.sum(prod_t[span], 0, keepdims=True)
        d_probs = nn(head_lanes(head, v), d_t)
        d_scores = (probs * (d_probs - row_dot)).astype(BF16)
        dv_here = nn(probs.astype(BF16), head_lanes(head, d))
        dk_here = nn(d_scores, q_here)
        dq_parts.append(nn(k_t[span], d_scores))
        dk = dk_here if dk is None else dk + dk_here
        dv = dv_here if dv is None else dv + dv_here
    dq = jnp.concatenate(dq_parts, 0).T * HEAD_DIM**-0.5
    dq_ref[...] = dq.astype(BF16)
    dk_ref[...] = dk.astype(BF16)
    dv_ref[...] = dv.astype(BF16)
    sq_ref[0] = jnp.sum(dq, 0, keepdims=True)
    sv_ref[0] = jnp.sum(dv, 0, keepdims=True)


def run_attend_back(lengths, qkv, mixed, d_mixed, log_total, seq):
    count = qkv.shape[0]
    width = qkv.shape[1] // 3
    pairs = count // seq
    sums = pl.BlockSpec((1, 1, LANES), lambda p, b, *_: (p, 0, b))
    return pl.pallas_call(
        attend_back_kernel,
        grid_spec=pltpu.PrefetchScalarGridSpec(
            num_scalar_prefetch=1,
            grid=(pairs, BLOCKS),
            in_specs=[
                column(seq, 0),
                column(seq, BLOCKS),
                column(seq, 2 * BLOCKS),
                column(seq, 0),
                column(seq, 0),
                pl.BlockSpec((1, 1, 2, seq), lambda p, b, *_: (p, b, 0, 0)),
            ],
            out_specs=[column(seq, 0)] * 3 + [sums] * 2,
        ),
        out_shape=[jax.ShapeDtypeStruct((count, width), BF16)] * 3
        + [jax.ShapeDtypeStruct((pairs, 1, width), F32)] * 2,
        compiler_params=params(),
        cost_estimate=cost(40 * pairs * HEADS * seq * seq * HEAD_DIM, 16 * count * width, pairs * HEADS * seq * seq),
        name="attend_back",
    )(lengths, qkv, qkv, qkv, mixed, d_mixed, log_total)


def feed_kernel(
    valid_ref, x_ref, a_ref, g_ref, gain_ref, shift_ref, bias_ref, hidden_ref, out_w, up_w, down_w, proj_w,
    x1_ref, left_ref, slope_ref, y_ref, gm_ref, dx2_ref, e2_ref, sum_ref,
):
    width = x_ref.shape[1]
    first = pl.program_id(0) == 0
    valid = valid_ref[...]
    a = a_ref[...]
    put_slabs(left_ref, (6,), a)
    x1 = x_ref[...].astype(F32) + nn(a, out_w[...]) + bias_ref[2:3].astype(F32)
    x1_ref[...] = x1
    hat, _ = norm_stats(x1)
    h = (hat * gain_ref[1:2].astype(F32) + shift_ref[1:2].astype(F32)).astype(BF16)
    put_slabs(left_ref, (5,), h)
    x2 = x1 + bias_ref[3:4].astype(F32)
    for part in range(up_w.shape[1] // width):
        span = slice(part * width, (part + 1) * width)
        u = nn(h, up_w[:, span]) + hidden_ref[:, span].astype(F32)
        acted, slope = gelu_and_slope(u)
        z = acted.astype(BF16)
        slope_ref[:, span] = slope.astype(BF16)
        turned = z.T
        for piece in range(16):
            chunk, block = part * 4 + piece // 4, piece % 4
            left_ref[1 + block, slot_of(chunk)] = turned[piece * SHARD : (piece + 1) * SHARD]
        x2 = x2 + nn(z, down_w[span, :])
    x2_low = x2.astype(BF16)
    put_slabs(left_ref, (0,), x2_low)
    y_ref[...] = ((nn(x2_low, proj_w[...]) + bias_ref[4:5].astype(F32)) * valid).astype(BF16)
    g = g_ref[...].astype(F32) * valid
    g_low = g.astype(BF16)
    gm_ref[...] = g_low
    dx2 = nt(g_low, proj_w[...])
    dx2_ref[...] = dx2
    e2_ref[...] = dx2.astype(BF16)
    add_sum(sum_ref, 0, dx2, first)
    add_sum(sum_ref, 1, g, first)


def run_feed(valid, x, a, g, gains, shifts, biases, hidden, out_w, up_w, down_w, proj_w, tile=256):
    count, width = x.shape
    ff = up_w.shape[1]
    low = jax.ShapeDtypeStruct((count, width), BF16)
    full = jax.ShapeDtypeStruct((count, width), F32)
    weights = (gains, shifts, biases, hidden, out_w, up_w, down_w, proj_w)
    return pl.pallas_call(
        feed_kernel,
        grid=(count // tile,),
        in_specs=[rows(tile, 1)] + [rows(tile, width)] * 3 + [whole(w.shape) for w in weights],
        out_specs=[
            rows(tile, width), pl.BlockSpec((7, 16, SHARD, tile), lambda i: (0, 0, 0, i)), rows(tile, ff),
            rows(tile, width), rows(tile, width), rows(tile, width), rows(tile, width), whole((2, width)),
        ],
        out_shape=[
            full, jax.ShapeDtypeStruct((7, 16, SHARD, count), BF16), jax.ShapeDtypeStruct((count, ff), BF16),
            low, low, full, low, jax.ShapeDtypeStruct((2, width), F32),
        ],
        compiler_params=params(60),
        cost_estimate=cost(2 * count * width * (3 * width + 2 * ff), count * (width * 24 + ff * 6) + 11 * MIB),
        name="feed",
    )(valid, x, a, g, *weights)


def feed_back_kernel(
    e2_ref, dx2_ref, slope_ref, x1_ref, gain_ref, out_w, up_w, down_w,
    eu_ref, dx1_ref, e1_ref, da_ref, hid_ref, sum_ref,
):
    width = e2_ref.shape[1]
    first = pl.program_id(0) == 0
    e2 = e2_ref[...]
    dh = None
    for start in range(0, up_w.shape[1], width):
        span = slice(start, start + width)
        du = nt(e2, down_w[span, :]) * slope_ref[:, span].astype(F32)
        eu = du.astype(BF16)
        eu_ref[:, span] = eu
        hid_ref[:, span] = jnp.where(first, 0.0, hid_ref[:, span]) + jnp.sum(du, 0, keepdims=True)
        part = nt(eu, up_w[:, span])
        dh = part if dh is None else dh + part
    hat, scale = norm_stats(x1_ref[...])
    dx1 = dx2_ref[...] + norm_back(dh, hat, scale, gain_ref[1:2].astype(F32))
    dx1_ref[...] = dx1
    e1 = dx1.astype(BF16)
    e1_ref[...] = e1
    da_ref[...] = nt(e1, out_w[...]).astype(BF16)
    add_sum(sum_ref, 0, dh * hat, first)
    add_sum(sum_ref, 1, dh, first)
    add_sum(sum_ref, 2, dx1, first)


def run_feed_back(e2, dx2, slope, x1, gains, out_w, up_w, down_w, tile=256):
    count, width = x1.shape
    ff = up_w.shape[1]
    low = jax.ShapeDtypeStruct((count, width), BF16)
    return pl.pallas_call(
        feed_back_kernel,
        grid=(count // tile,),
        in_specs=[rows(tile, width), rows(tile, width), rows(tile, ff), rows(tile, width)]
        + [whole(w.shape) for w in (gains, out_w, up_w, down_w)],
        out_specs=[rows(tile, ff), rows(tile, width), rows(tile, width), rows(tile, width), whole((1, ff)), whole((3, width))],
        out_shape=[
            jax.ShapeDtypeStruct((count, ff), BF16),
            jax.ShapeDtypeStruct((count, width), F32),
            low,
            low,
            jax.ShapeDtypeStruct((1, ff), F32),
            jax.ShapeDtypeStruct((3, width), F32),
        ],
        compiler_params=params(60),
        cost_estimate=cost(2 * count * width * (width + 2 * ff), count * (width * 18 + ff * 6) + 10 * MIB),
        name="feed_back",
    )(e2, dx2, slope, x1, gains, out_w, up_w, down_w)


def qkv_back_kernel(dq_ref, dk_ref, dv_ref, dx1_ref, x_ref, gain_ref, w_ref, out_ref, sum_ref):
    width = x_ref.shape[1]
    first = pl.program_id(0) == 0
    dh = nt(dq_ref[...], w_ref[:, :width])
    dh = dh + nt(dk_ref[...], w_ref[:, width : 2 * width])
    dh = dh + nt(dv_ref[...], w_ref[:, 2 * width :])
    hat, scale = norm_stats(x_ref[...].astype(F32))
    out_ref[...] = (dx1_ref[...] + norm_back(dh, hat, scale, gain_ref[0:1].astype(F32))).astype(BF16)
    add_sum(sum_ref, 0, dh * hat, first)
    add_sum(sum_ref, 1, dh, first)


def run_qkv_back(dq, dk, dv, dx1, x, gains, w, tile=256):
    count, width = x.shape
    return pl.pallas_call(
        qkv_back_kernel,
        grid=(count // tile,),
        in_specs=[rows(tile, width)] * 5 + [whole(gains.shape), whole(w.shape)],
        out_specs=[rows(tile, width), whole((2, width))],
        out_shape=[jax.ShapeDtypeStruct((count, width), BF16), jax.ShapeDtypeStruct((2, width), F32)],
        compiler_params=params(),
        cost_estimate=cost(6 * count * width * width, count * width * 14 + 6 * width * width),
        name="qkv_back",
    )(dq, dk, dv, dx1, x, gains, w)


BLOCK_COUNT = 13
RING = 6
CORE_RING = 4
SECOND_RING = 7
MODES = ('lyh', 'ylh', 'lyh', 'ylh', 'lyh', 'lyh', 'ylh', 'ylh', 'lyh', 'ylh', 'ylh', 'ylh', 'ylh')
QUERIES = 256
ABREAST = 3
VECTORS = 16
TILE = 256
MESH = pl.DeviceIdType.MESH


def one_kernel(
    group_ref, caption_ref, gain_ref, shift_ref, bias_ref, hidden_ref, cls_row_ref,
    x_hbm, g_hbm, qkv_w_hbm, out_hbm, up_hbm, down_hbm, proj_hbm,
    proj_ref, down_ref, up_ref, out_ref, qkv_ref, vec_ref, tokens_hbm, merged_hbm, qkv_hbm, h1_hbm,
    grads, got_1, got_2, got_3, got_4, lefts, pool, eu, down_w, up_w, out_w, proj_w, x1, logs, vec, vec_got,
    y_send, y_got, merged, sums,
    send_sem, recv_sem, load_sem, sum_sem, vec_send, vec_recv, tower_sem, free_sem,
):
    count, width = x1.shape
    pairs, _, _, seq = logs.shape
    half = pairs // 2
    parts = eu.shape[0]
    tiles = count // TILE
    index = lax.axis_index("dp")
    tower = lax.axis_index("tower")
    core, y, z_lo, z_hi = index % 2, index // 2 % 2, index // 4 % 2, index // 8
    by_core = {"dp": index + 1 - 2 * core}
    by_y = {"dp": index + 2 - 4 * y}
    by_lo = {"dp": index + 4 - 8 * z_lo}
    by_hi = {"dp": index + 8 - 16 * z_hi}
    by_x = {"tower": 1 - tower}

    def length(pair):
        image = jnp.where(group_ref[pair] == 1, IMG_LARGE, IMG_SMALL)
        return jnp.where(tower == 0, image, caption_ref[pair])

    barrier = pltpu.get_barrier_semaphore()
    for partner in (by_core, by_y, by_lo, by_hi, by_x):
        pl.semaphore_signal(barrier, inc=1, device_id=partner, device_id_type=MESH)

    def copy(number, source, target):
        return pltpu.make_async_copy(source, target, load_sem.at[number])

    x_copy = copy(0, x_hbm, pool.at[1])
    qkv_w_copies = [
        copy(1 + i, qkv_w_hbm.at[:, pl.ds(i * width, width)], down_w.at[pl.ds(i * width, width)]) for i in range(3)
    ]
    g_copy = copy(4, g_hbm, merged)
    out_copy = copy(5, out_hbm, out_w)
    up_copy = copy(6, up_hbm, up_w)
    proj_copy = copy(7, proj_hbm, proj_w)
    down_copy = copy(8, down_hbm, down_w)
    qkv_saves = [copy(9 + i, eu.at[i], qkv_hbm.at[i]) for i in range(3)]
    h1_save = copy(12, lefts.at[0], h1_hbm)
    h1_copy = copy(13, h1_hbm, lefts.at[0])
    qkv_copies = [copy(14 + i, qkv_hbm.at[i], down_w.at[pl.ds(i * count, count)]) for i in range(3)]
    qkv_w_again = copy(17, qkv_w_hbm, up_w.at[:, pl.ds(0, 3 * width)])
    tokens_copy = copy(18, pool.at[0], tokens_hbm)
    merged_copy = copy(19, merged, merged_hbm)

    for item in (x_copy, *qkv_w_copies, g_copy):
        item.start()
    vec[0] = jnp.zeros((VECTORS, width), F32)

    def add_to(row, value, lanes=slice(None)):
        vec[0, row : row + 1, lanes] = vec[0, row : row + 1, lanes] + jnp.sum(value, 0, keepdims=True)

    def tile_rows(tile):
        return pl.ds(pl.multiple_of(tile * TILE, TILE), TILE)

    def tile_valid(tile):
        per_pair = seq // TILE
        row = lax.broadcasted_iota(jnp.int32, (TILE, 1), 0) + tile % per_pair * TILE
        return row < length(tile // per_pair)

    def put(slot, value, at):
        turned = value.T
        for chunk in range(16):
            lefts[slot, slot_of(chunk), :, at] = turned[chunk * SHARD : (chunk + 1) * SHARD]

    gain_one, gain_two = gain_ref[0:1].astype(F32), gain_ref[1:2].astype(F32)
    shift_one, shift_two = shift_ref[0:1].astype(F32), shift_ref[1:2].astype(F32)
    biases = bias_ref[...].astype(F32)
    x_copy.wait()

    def first_norm(tile, carry):
        at = tile_rows(tile)
        hat, _ = norm_stats(pool[1, at, :].astype(F32))
        h = (hat * gain_one + shift_one).astype(BF16)
        pool[2, at, :] = h
        put(0, h, at)
        return carry

    def first_products(tile, carry):
        at = tile_rows(tile)
        h = pool[2, at, :]
        q = (nn(h, down_w[:width, :]) + biases[0:1]).astype(BF16)
        eu[0, at, :] = q * BF16(HEAD_DIM**-0.5)
        eu[1, at, :] = nn(h, down_w[width : 2 * width, :]).astype(BF16)
        eu[2, at, :] = (nn(h, down_w[2 * width : 3 * width, :]) + biases[1:2]).astype(BF16)
        return carry

    lax.fori_loop(0, tiles, first_norm, 0)
    h1_save.start()
    for item in qkv_w_copies:
        item.wait()
    lax.fori_loop(0, tiles, first_products, 0)
    for item in (*qkv_saves, down_copy, out_copy, up_copy, proj_copy):
        item.start()

    g_copy.wait()
    pl.semaphore_wait(barrier, 5)
    strip = 128
    row = lax.broadcasted_iota(jnp.int32, (strip, 1), 0)

    def cotangent(side, put_strip):
        for start in range(0, seq, strip):
            first = pl.multiple_of(side * seq + start, strip)
            value = merged[0, pl.ds(first, strip), :].astype(F32)
            after = merged[0, pl.ds(first + strip, 1), :].astype(F32)
            put_strip(start, jnp.where(row == strip - 1, after, pltpu.roll(value, strip - 1, 0)).astype(BF16))

    def put_send(start, value):
        pool[2, start : start + strip, :] = value

    def put_own(start, value):
        pool[0, pl.ds(pl.multiple_of(tower * seq + start, strip), strip), :] = value

    cotangent(1 - tower, put_send)
    own_rows = pl.ds(pl.multiple_of(tower * seq, seq), seq)
    g_swap = pltpu.make_async_remote_copy(
        pool.at[2, pl.ds(0, seq)], pool.at[0, own_rows], tower_sem.at[0], tower_sem.at[1], device_id=by_x, device_id_type=MESH
    )
    g_swap.start()
    cotangent(tower, put_own)
    vec[0, 13:14, :] = merged[0, 0:1, :].astype(F32)

    def attend_one(pair, block):
        at = pl.ds(pl.multiple_of(pair * seq, seq), seq)
        lanes = pl.ds(pl.multiple_of(block * LANES, LANES), LANES)
        valid = lax.broadcasted_iota(jnp.int32, (1, seq), 1) < length(pair)
        q, k, v = (eu[number, at, lanes] for number in range(3))
        mixed = None
        for head in range(2):
            scores = jnp.where(valid, nt(head_lanes(head, q), k), masked_score)
            largest = jnp.max(scores, 1, keepdims=True)
            weights = jnp.exp(scores - largest)
            total = jnp.sum(weights, 1, keepdims=True)
            here = nn(weights.astype(BF16), head_lanes(head, v)) * (1.0 / total)
            mixed = here if mixed is None else mixed + here
            logs[pair, block, head : head + 1, :] = (largest + jnp.log(total)).reshape(1, seq)
        pool[3, at, lanes] = mixed.astype(BF16)

    def attend(step, carry):
        steps = BLOCKS // ABREAST
        for number in range(ABREAST):
            attend_one(step // steps, step % steps * ABREAST + number)
        return carry

    lax.fori_loop(0, pairs * BLOCKS // ABREAST, attend, 0)

    for item in (h1_save, *qkv_saves, out_copy, up_copy, down_copy, proj_copy):
        item.wait()

    def feed(tile, carry):
        at = tile_rows(tile)
        a = pool[3, at, :]
        put(6, a, at)
        mid = pool[1, at, :].astype(F32) + nn(a, out_w[...]) + biases[2:3]
        x1[at, :] = mid
        hat, _ = norm_stats(mid)
        h = (hat * gain_two + shift_two).astype(BF16)
        put(5, h, at)
        x2 = mid + biases[3:4]
        for part in range(parts):
            span = slice(part * width, (part + 1) * width)
            u = nn(h, up_w[:, span]) + hidden_ref[:, span].astype(F32)
            acted, slope = gelu_and_slope(u)
            z = acted.astype(BF16)
            eu[part, at, :] = slope.astype(BF16)
            turned = z.T
            for piece in range(16):
                chunk, block = part * 4 + piece // 4, piece % 4
                lefts[1 + block, slot_of(chunk), :, at] = turned[piece * SHARD : (piece + 1) * SHARD]
            x2 = x2 + nn(z, down_w[span, :])
        x2_low = x2.astype(BF16)
        put(0, x2_low, at)
        rows_y = jnp.where(tile_valid(tile), nn(x2_low, proj_w[...]) + biases[4:5], 0.0).astype(BF16)
        per_pair = seq // TILE
        here = pl.ds(pl.multiple_of(tile % per_pair * TILE, TILE), TILE)

        @pl.when(tile // per_pair == tower)
        def _():
            merged[0, here, :] = rows_y

        @pl.when(tile // per_pair != tower)
        def _():
            y_send[here, :] = rows_y

        return carry

    lax.fori_loop(0, tiles, feed, 0)
    y_swap = pltpu.make_async_remote_copy(
        y_send, y_got, tower_sem.at[2], tower_sem.at[3], device_id=by_x, device_id_type=MESH
    )
    y_swap.start()

    g_swap.wait()

    def cotangent_rows(tile, carry):
        at = tile_rows(tile)
        g = jnp.where(tile_valid(tile), pool[0, at, :].astype(F32), 0.0)
        pool[0, at, :] = g.astype(BF16)
        add_to(4, g)
        return carry

    lax.fori_loop(0, tiles, cotangent_rows, 0)

    def project_back(tile, carry):
        at = tile_rows(tile)
        dx2 = nt(pool[0, at, :], proj_w[...])
        pool[2, at, :] = dx2.astype(BF16)
        add_to(3, dx2)
        return carry

    def bits(block):
        ways = {"y": (by_y, y), "l": (by_lo, z_lo), "h": (by_hi, z_hi)}
        partners, sides = zip(*(ways[letter] for letter in MODES[block]))
        return (by_core, *partners), sides

    def shelf(block):
        if 5 <= block < 9:
            return lefts, block - 4
        return grads, (block if block < 5 else block - 4) % RING

    def shards(block, of_core, first, size):
        buffer, slot = shelf(block)
        return buffer.at[slot, pl.ds(of_core * 8 + first, size), :, pl.ds(0, width)]

    gots = (got_1, got_2, got_3, got_4)

    def place(block, level):
        return block % (CORE_RING, SECOND_RING, BLOCK_COUNT, BLOCK_COUNT)[level]

    def swap_of(block, level):
        partners, (b1, b2, b3) = bits(block)
        if level == 0:
            source = shards(block, 1 - core, 0, 8)
        elif level == 1:
            source = shards(block, core, (1 - b1) * 4, 4)
        elif level == 2:
            source = shards(block, core, b1 * 4 + (1 - b2) * 2, 2)
        else:
            source = shards(block, core, b1 * 4 + b2 * 2 + 1 - b3, 1)
        return pltpu.make_async_remote_copy(
            source,
            gots[level].at[place(block, level)],
            send_sem.at[level, block],
            recv_sem.at[level, block],
            device_id=partners[level],
            device_id_type=MESH,
        )

    def advance(block, level):
        _, (b1, b2, b3) = bits(block)
        buffer, slot = shelf(block)
        swap_of(block, level - 1).wait_recv()
        got = gots[level - 1]
        size = 8 >> level
        bit = (b1, b2, b3)[level - 1]
        base = (0, b1 * 4, b1 * 4 + b2 * 2)[level - 1]
        for other in (1, 0):
            side = (1 - bit) if other else bit

            def add(i, carry, side=side):
                at = side * size + i
                here = core * 8 + base + at
                total = buffer[slot, here, :, :width].astype(F32) + got[place(block, level - 1), at].astype(F32)
                buffer[slot, here, :, :width] = total.astype(BF16)
                return carry

            lax.fori_loop(0, size, add, 0, unroll=True)
            if other:
                if level == 1 and block >= SECOND_RING:
                    assert (block - SECOND_RING, 2) in done
                    pl.semaphore_wait(free_sem.at[1, block], 1)
                swap_of(block, level).start()
        later = block + (CORE_RING, SECOND_RING, BLOCK_COUNT)[level - 1]
        if later < BLOCK_COUNT:
            pl.semaphore_signal(
                free_sem.at[level - 1, later], inc=1, device_id=bits(later)[0][level - 1], device_id_type=MESH
            )

    def sum_copies(block, slot):
        if block == 0:
            target = proj_ref
        elif block < 5:
            target = down_ref.at[pl.ds((block - 1) * SHARD, SHARD)]
        elif block < 9:
            target = up_ref.at[:, pl.ds((block - 5) * width, width)]
        elif block == 9:
            target = out_ref
        else:
            piece = 2 * LANES
            return [
                pltpu.make_async_copy(
                    sums.at[slot, :, pl.ds(i * piece, piece)],
                    qkv_ref.at[:, pl.ds(i * width + (block - 10) * piece, piece)],
                    sum_sem.at[slot, i],
                )
                for i in range(3)
            ]
        return [pltpu.make_async_copy(sums.at[slot], target, sum_sem.at[slot, 0])]

    finished = []

    def finish(block):
        _, (b1, b2, b3) = bits(block)
        swap_of(block, 3).wait_recv()
        buffer, slot = shelf(block)
        total = buffer[slot, core * 8 + b1 * 4 + b2 * 2 + b3, :, :width].astype(F32) + got_4[block, 0].astype(F32)
        if len(finished) >= 3:
            for item in sum_copies(finished[-3], (len(finished) - 3) % 3):
                item.wait()
        place_now = len(finished) % 3
        sums[place_now] = total
        for item in sum_copies(block, place_now):
            item.start()
        finished.append(block)
        for level in range(4):
            swap_of(block, level).wait_send()

    done = set()

    def tick(*work):
        for block, level in work:
            assert (block, level) not in done and (level == 1 or (block, level - 1) in done)
            done.add((block, level))
            if level == 4:
                finish(block)
            else:
                advance(block, level)

    def weight_grad(block, number, right):
        assert block < 10 or (block - 10, 4) in done
        assert block < CORE_RING or (block - CORE_RING, 1) in done
        left = lefts[number].reshape(16 * SHARD, count)
        buffer, slot = shelf(block)
        step = 256

        def columns(i, carry):
            at = pl.ds(pl.multiple_of(i * step, step), step)
            product = nn(left, right(i, at)).astype(BF16).reshape(16, SHARD, step)
            if MODES[block] == "ylh":
                buffer[slot, :, :, at] = product
            else:
                for number in range(16):
                    side = {"y": number // 4 % 2, "l": number // 2 % 2, "h": number % 2}
                    a, b, c = (side[letter] for letter in MODES[block])
                    buffer[slot, number // 8 * 8 + a * 4 + b * 2 + c, :, at] = product[number]
            return carry

        lax.fori_loop(0, width // step, columns, 0)
        if block >= CORE_RING:
            pl.semaphore_wait(free_sem.at[0, block], 1)
        swap_of(block, 0).start()

    weight_grad(0, 0, lambda i, at: pool[0, :, at])
    h1_copy.start()
    lax.fori_loop(0, tiles, project_back, 0)
    tick(*TICKS["e2", 0])
    for part in range(parts):
        weight_grad(1 + part, 1 + part, lambda i, at: pool[2, :, at])
        tick(*TICKS["down", part])

    for part in range(parts):

        def tile_du(tile, carry, part=part):
            at = tile_rows(tile)
            du = nt(pool[2, at, :], down_w[part * width : (part + 1) * width, :])
            du = du * eu[part, at, :].astype(F32)
            eu[part, at, :] = du.astype(BF16)
            add_to(9 + part, du)
            return carry

        lax.fori_loop(0, tiles, tile_du, 0)
        tick(*TICKS["du", part])
    for item in qkv_copies:
        item.start()

    for part in range(parts):
        weight_grad(5 + part, 5, lambda i, at, part=part: eu[part, :, at])
        tick(*TICKS["up", part])

    for number in range(tiles):

        def mid_back(tile, carry):
            at = tile_rows(tile)
            dh = nt(eu[0, at, :], up_w[:, :width])
            for part in range(1, parts):
                dh = dh + nt(eu[part, at, :], up_w[:, part * width : (part + 1) * width])
            hat, scale = norm_stats(x1[at, :])
            dx1 = nt(pool[0, at, :], proj_w[...]) + norm_back(dh, hat, scale, gain_two)
            x1[at, :] = dx1
            e1 = dx1.astype(BF16)
            pool[2, at, :] = e1
            pool[0, at, :] = nt(e1, out_w[...]).astype(BF16)
            add_to(6, dh * hat)
            add_to(8, dh)
            add_to(2, dx1)
            return carry

        lax.fori_loop(number, number + 1, mid_back, 0)
        tick(*TICKS["mid", number])
    qkv_w_again.start()

    weight_grad(9, 6, lambda i, at: pool[2, :, at])
    tick(*TICKS["out", 0])

    for item in (*qkv_copies, h1_copy):
        item.wait()
    per_loop = 2
    for turn in range(pairs * BLOCKS // per_loop):

        def attend_back_one(step):
            pair, block = step // 2 % pairs, step // (2 * pairs) * 2 + step % 2
            at = pl.ds(pl.multiple_of(pair * seq, seq), seq)
            lanes = pl.ds(pl.multiple_of(block * LANES, LANES), LANES)
            valid = lax.broadcasted_iota(jnp.int32, (seq, 1), 0) < length(pair)
            q, k, v = (
                down_w[pl.ds(pl.multiple_of(number * count + pair * seq, seq), seq), lanes] for number in range(3)
            )
            d = pool[0, at, lanes]
            log_rows = logs[pair, block]
            k_t = k.T
            d_t = d.T
            prod_t = d_t.astype(F32) * pool[3, at, lanes].T.astype(F32)
            dq_rows = []
            dk = None
            dv = None
            for head in range(2):
                span = slice(head * HEAD_DIM, (head + 1) * HEAD_DIM)
                row_dot = jnp.sum(prod_t[span], 0, keepdims=True)
                v_here = head_lanes(head, v)
                dq_parts = []
                for start in range(0, seq, QUERIES):
                    some = slice(start, start + QUERIES)
                    q_here = head_lanes(head, q[some])
                    scores = jnp.where(valid, nt(k, q_here), masked_score)
                    probs = jnp.exp(scores - log_rows[head : head + 1, some])
                    d_probs = nn(v_here, d_t[:, some])
                    d_scores = (probs * (d_probs - row_dot[:, some])).astype(BF16)
                    dv_here = nn(probs.astype(BF16), head_lanes(head, d[some]))
                    dk_here = nn(d_scores, q_here)
                    dq_parts.append(nn(k_t[span], d_scores))
                    dk = dk_here if dk is None else dk + dk_here
                    dv = dv_here if dv is None else dv + dv_here
                dq_rows.append(jnp.concatenate(dq_parts, 1))
            dq = jnp.concatenate(dq_rows, 0).T * HEAD_DIM**-0.5
            for number, value in ((0, dq), (1, dk), (2, dv)):
                eu[number, at, lanes] = value.astype(BF16)
            add_to(0, dq, lanes)
            add_to(1, dv, lanes)

        def attend_back(step, carry):
            for number in range(per_loop):
                attend_back_one(step * per_loop + number)
            return carry

        lax.fori_loop(turn, turn + 1, attend_back, 0)
        tick(*TICKS["attend", turn])
        if turn % 2 == 1:
            third = turn // 2
            some = pl.ds(third * 2 * LANES, 2 * LANES)
            weight_grad(10 + third, 0, lambda i, at, some=some: eu[i, :, some])
            tick(*TICKS["qkv", third])

    qkv_w_again.wait()
    for number in range(tiles):

        def first_back(tile, carry):
            at = tile_rows(tile)
            dh = nt(eu[0, at, :], up_w[:, :width])
            for part in (1, 2):
                dh = dh + nt(eu[part, at, :], up_w[:, part * width : (part + 1) * width])
            hat, scale = norm_stats(pool[1, at, :].astype(F32))
            pool[0, at, :] = (x1[at, :] + norm_back(dh, hat, scale, gain_one)).astype(BF16)
            add_to(5, dh * hat)
            add_to(7, dh)
            return carry

        lax.fori_loop(number, number + 1, first_back, 0)
        tick(*TICKS["first", number])
    tokens_copy.start()

    def vec_swap(level):
        return pltpu.make_async_remote_copy(
            vec.at[level],
            vec_got.at[level],
            vec_send.at[level],
            vec_recv.at[level],
            device_id=(by_core, by_y, by_lo, by_hi, by_x)[level],
            device_id_type=MESH,
        )

    vec_swap(0).start()

    y_swap.wait()

    def projected(side, start, size):
        own = merged[0, start : start + size, :].astype(F32)
        got = y_got[start : start + size, :].astype(F32)
        return jnp.where(tower == side, own, got)

    merged[0, 2 * seq : 2 * seq + 1, :] = projected(1, seq - 16, 16)[15:16].astype(BF16)
    for side in (1, 0):
        for start in range(seq - strip, -1, -strip):
            value = projected(side, start, strip)
            if start > 0:
                before = projected(side, start - 16, 16)[15:16]
            elif side == 1:
                before = projected(0, seq - 16, 16)[15:16]
            else:
                before = cls_row_ref[...].reshape(1, width).astype(F32)
            moved = jnp.where(row == 0, before, pltpu.roll(value, 1, 0))
            merged[0, side * seq + start : side * seq + start + strip, :] = moved.astype(BF16)
    merged_copy.start()

    for number, work in enumerate(TICKS["tail", 0]):
        tick(work)
        if number < 4:
            vec_swap(number).wait_recv()
            vec[number + 1] = vec[number] + vec_got[number]
            vec_swap(number + 1).start()
    vec_swap(4).wait_recv()
    vec_ref[0:13] = vec[4, 0:13]
    vec_ref[13:16] = vec[4, 13:16] + vec_got[4, 13:16]
    for level in range(5):
        vec_swap(level).wait_send()
    for number in range(BLOCK_COUNT - 3, BLOCK_COUNT):
        for item in sum_copies(finished[number], number % 3):
            item.wait()
    tokens_copy.wait()
    merged_copy.wait()
    assert len(done) == 4 * BLOCK_COUNT


TICKS = {
    ('proj', 0): [],
    ('e2', 0): [],
    ('down', 0): [],
    ('down', 1): [(0, 1)],
    ('down', 2): [],
    ('down', 3): [(1, 1)],
    ('du', 0): [(2, 1)],
    ('du', 1): [(3, 1), (4, 1)],
    ('du', 2): [(0, 2)],
    ('du', 3): [],
    ('up', 0): [(1, 2)],
    ('up', 1): [],
    ('up', 2): [(2, 2)],
    ('up', 3): [(5, 1)],
    ('mid', 0): [(3, 2), (6, 1), (7, 1)],
    ('mid', 1): [(0, 3), (4, 2), (8, 1)],
    ('mid', 2): [(1, 3), (2, 3)],
    ('mid', 3): [],
    ('out', 0): [],
    ('attend', 0): [(5, 2), (6, 2)],
    ('attend', 1): [(0, 4), (3, 3), (7, 2), (9, 1)],
    ('qkv', 0): [],
    ('attend', 2): [(4, 3), (8, 2)],
    ('attend', 3): [(1, 4), (2, 4), (5, 3), (10, 1)],
    ('qkv', 1): [(6, 3)],
    ('attend', 4): [(3, 4), (9, 2), (11, 1)],
    ('attend', 5): [(4, 4), (5, 4), (7, 3), (8, 3)],
    ('qkv', 2): [(6, 4)],
    ('first', 0): [(10, 2)],
    ('first', 1): [(9, 3), (12, 1), (7, 4)],
    ('first', 2): [],
    ('first', 3): [(8, 4), (11, 2)],
    ('tail', 0): [(10, 3), (9, 4), (12, 2), (11, 3), (10, 4), (12, 3), (11, 4), (12, 4)],
}


def run_one(group_id, caption_len, gains, shifts, biases, hidden, cls_row, x, g, qkv_w, out_w, up_w, down_w, proj_w):
    count, width = x.shape
    ff = up_w.shape[1]
    pairs = group_id.shape[0]
    seq = count // pairs
    shard = jax.ShapeDtypeStruct
    vmem = pl.BlockSpec(memory_space=pltpu.VMEM)
    hbm = pl.BlockSpec(memory_space=pl.ANY)
    return pl.pallas_call(
        one_kernel,
        in_specs=[pl.BlockSpec(memory_space=pltpu.SMEM)] * 2 + [vmem] * 5 + [hbm] * 7,
        out_specs=[hbm] * 5 + [vmem] + [hbm] * 4,
        out_shape=[
            shard((SHARD, width), F32),
            shard((4 * SHARD, width), F32),
            shard((SHARD, ff), F32),
            shard((SHARD, width), F32),
            shard((SHARD, 3 * width), F32),
            shard((VECTORS, width), F32),
            shard((count, width), BF16),
            shard(g.shape, BF16),
            shard((3, count, width), BF16),
            shard((16, SHARD, count), BF16),
        ],
        scratch_shapes=[
            pltpu.VMEM((RING, 16, SHARD, width), BF16),
            pltpu.VMEM((CORE_RING, 8, SHARD, width), BF16),
            pltpu.VMEM((SECOND_RING, 4, SHARD, width), BF16),
            pltpu.VMEM((BLOCK_COUNT, 2, SHARD, width), BF16),
            pltpu.VMEM((BLOCK_COUNT, 1, SHARD, width), BF16),
            pltpu.VMEM((7, 16, SHARD, count), BF16),
            pltpu.VMEM((4, count, width), BF16),
            pltpu.VMEM((ff // width, count, width), BF16),
            pltpu.VMEM((ff, width), BF16),
            pltpu.VMEM((width, ff), BF16),
            pltpu.VMEM((width, width), BF16),
            pltpu.VMEM((width, width), BF16),
            pltpu.VMEM((count, width), F32),
            pltpu.VMEM((pairs, BLOCKS, 2, seq), F32),
            pltpu.VMEM((5, VECTORS, width), F32),
            pltpu.VMEM((5, VECTORS, width), F32),
            pltpu.VMEM((seq, width), BF16),
            pltpu.VMEM((seq, width), BF16),
            pltpu.VMEM(g.shape, BF16),
            pltpu.VMEM((3, SHARD, width), F32),
            pltpu.SemaphoreType.DMA((4, BLOCK_COUNT)),
            pltpu.SemaphoreType.DMA((4, BLOCK_COUNT)),
            pltpu.SemaphoreType.DMA((20,)),
            pltpu.SemaphoreType.DMA((3, 3)),
            pltpu.SemaphoreType.DMA((5,)),
            pltpu.SemaphoreType.DMA((5,)),
            pltpu.SemaphoreType.DMA((4,)),
            pltpu.SemaphoreType.REGULAR((2, BLOCK_COUNT)),
        ],
        compiler_params=pltpu.CompilerParams(
            collective_id=0, has_side_effects=True, vmem_limit_bytes=63 * MIB
        ),
        cost_estimate=cost(60e9, 60 * MIB),
        name="one",
    )(group_id, caption_len, gains, shifts, biases, hidden, cls_row, x, g, qkv_w, out_w, up_w, down_w, proj_w)


def full_grad_kernel(left_ref, *refs):
    start = 0
    for right_ref in refs[:-1]:
        stop = start + right_ref.shape[1]
        refs[-1][:, start:stop] = nn(left_ref[...], right_ref[...])
        start = stop


def run_full_grad(left, *rights):
    height, count = left.shape
    width = sum(right.shape[1] for right in rights)
    tile = 384
    return pl.pallas_call(
        full_grad_kernel,
        grid=(height // tile,),
        in_specs=[rows(tile, count)] + [whole(right.shape) for right in rights],
        out_specs=rows(tile, width),
        out_shape=jax.ShapeDtypeStruct((height, width), F32),
        compiler_params=params(),
        name="full_grad",
    )(left, *rights)


def in_order(slabs):
    return jnp.stack([slabs[..., slot_of(chunk), :, :] for chunk in range(16)], -3)


def plain_back(lengths, logs, gains, feed_sums, cls_sum, left, h1, slope, g, e2, dx2, x1, a, qkv, x, y, down_w, up_w, out_w, qkv_w):
    count, width = x.shape
    seq = y.shape[2]
    eu, dx1, e1, da, hidden_sum, mid_sums = run_feed_back(e2, dx2, slope, x1, gains, out_w, up_w, down_w)
    dq, dk, dv, sum_q, sum_v = run_attend_back(lengths, qkv, a, da, logs, seq)
    tokens_grad, first_sums = run_qkv_back(dq, dk, dv, dx1, x, gains, qkv_w)
    turned = in_order(left)
    z = turned[1:5].transpose(1, 0, 2, 3).reshape(4 * width, count)
    x2, h2, a_t = (turned[i].reshape(width, count) for i in (0, 5, 6))
    h1 = in_order(h1).reshape(width, count)
    grads = (run_full_grad(x2, g), run_full_grad(z, e2), run_full_grad(h2, eu), run_full_grad(a_t, e1), run_full_grad(h1, dq, dk, dv))
    grads = [lax.psum_scatter(grad, "dp", scatter_dimension=0, tiled=True) for grad in grads]
    vectors = jnp.concatenate(
        [
            jnp.sum(sum_q, 0), jnp.sum(sum_v, 0), mid_sums[2:3], feed_sums, first_sums[0:1], mid_sums[0:1],
            first_sums[1:2], mid_sums[1:2], hidden_sum.reshape(-1, width),
        ],
        axis=0,
    )
    vectors = lax.psum(vectors, "dp")
    cls = lax.psum(cls_sum, ("tower", "dp"))
    y_got = lax.ppermute(take(y, 1 - lax.axis_index("tower")), "tower", [(0, 1), (1, 0)])
    return grads, vectors, cls, tokens_grad, y_got


def take(value, index):
    return lax.dynamic_index_in_dim(value, index, 0, keepdims=False)


PIECE = 256


def spread_kernel(index_ref, vec_ref, *refs):
    sources, (gain_ref, shift_ref, bias_ref, hidden_ref, cls_ref), targets, held = refs[:7], refs[7:12], refs[12:19], refs[19:26]
    sem_in, sem_out = refs[26:]
    ins, outs = [], []
    for source, there, target in zip(sources, held, targets):
        size = source.shape[0]
        step = PIECE if size % PIECE == 0 else size
        for start in range(0, size, step):
            number, at = len(ins), pl.ds(start, step)
            ins.append(pltpu.make_async_copy(source.at[at], there.at[at], sem_in.at[number]))
            outs.append(pltpu.make_async_copy(there.at[at], target.at[at], sem_out.at[number]))
    for item in ins:
        item.start()
    index = index_ref[0]
    width = vec_ref.shape[1]
    piece = gain_ref.shape[1]
    mine = pltpu.roll(vec_ref[...], width - piece * index, 1)[:, :piece]
    for number in range(5):
        bias_ref[number] = mine[number : number + 1]
    gain_ref[...] = mine[5:7]
    shift_ref[...] = mine[7:9]
    share = hidden_ref.shape[1]
    per_row = width // share
    row = vec_ref[pl.ds(9 + index // per_row, 1), :]
    hidden_ref[...] = pltpu.roll(row, width - share * (index % per_row), 1)[:, :share]
    cls_ref[...] = vec_ref[13]
    for before, after in zip(ins, outs):
        before.wait()
        after.start()
    for item in outs:
        item.wait()


def run_spread(index, vectors, *arrays):
    width = vectors.shape[1]
    small = [jax.ShapeDtypeStruct(shape, F32) for shape in ((2, width // 16), (2, width // 16), (5, 1, width // 16), (1, width // 4), (width,))]
    vmem = pl.BlockSpec(memory_space=pltpu.VMEM)
    hbm = pl.BlockSpec(memory_space=pl.ANY)
    return pl.pallas_call(
        spread_kernel,
        in_specs=[pl.BlockSpec(memory_space=pltpu.SMEM), vmem] + [hbm] * len(arrays),
        out_specs=[vmem] * 5 + [hbm] * len(arrays),
        out_shape=small + [jax.ShapeDtypeStruct(array.shape, array.dtype) for array in arrays],
        scratch_shapes=[pltpu.VMEM(array.shape, array.dtype) for array in arrays]
        + [pltpu.SemaphoreType.DMA((16,))] * 2,
        compiler_params=params(62),
        name="spread",
    )(index, vectors, *arrays)


def local(
    dp, tokens, group_id, caption_len, cls_row, norm_gains, shifts, bias_model, bias_hidden,
    w_qkv, w_out, w_up, w_down, w_proj, merged_grad,
):
    tower = lax.axis_index("tower")
    index = lax.axis_index("dp")
    pairs, seq, width = tokens.shape[1:]
    half = pairs // 2
    count = pairs * seq
    image_len = jnp.where(group_id == 1, IMG_LARGE, IMG_SMALL)
    lengths = jnp.where(tower == 0, image_len, caption_len).astype(jnp.int32)
    gains, shift_rows, biases, hidden = norm_gains[0], shifts[0], bias_model[0], bias_hidden
    qkv_w, out_w, up_w, down_w, proj_w = w_qkv[0], w_out[0], w_up[0], w_down[0], w_proj[0]
    x = tokens[0].reshape(count, width)

    if dp == 16 and pairs == 2:
        *grads, vectors, tokens_grad, merged_input, _, _ = run_one(
            group_id, caption_len, gains, shift_rows, biases, hidden, cls_row, x, merged_grad[0], qkv_w, out_w, up_w, down_w, proj_w
        )
        gain_sum, shift_sum, bias_sum, hidden_sum, cls, *arrays = run_spread(
            index.astype(jnp.int32)[None], vectors, merged_input, tokens_grad, *grads
        )
        bias_sum = bias_sum.transpose(1, 0, 2)[0]
        merged_input, tokens_grad, proj, down, up, out, qkv_grad = arrays
    else:
        positions = lax.broadcasted_iota(jnp.int32, (pairs, seq), 1)
        valid = (positions < lengths[:, None]).reshape(count, 1).astype(F32)
        image_grad = merged_grad[0, :, 1 : 1 + seq]
        text_grad = merged_grad[0, :, 1 + seq :]
        g_keep = jnp.where(tower == 0, image_grad, text_grad)
        g_send = jnp.where(tower == 0, text_grad, image_grad)
        g_got = lax.ppermute(g_send, "tower", [(0, 1), (1, 0)])
        cls_sum = jnp.sum(merged_grad[0, :, 0].astype(F32), 0)[None]
        h1, qkv = run_qkv(x, gains, shift_rows, biases, qkv_w)
        mixed, logs = run_attend(lengths, qkv, seq)
        g = jnp.where(tower == 0, jnp.stack([g_keep, g_got]), jnp.stack([g_got, g_keep])).reshape(count, width)
        x1, left, slope, y, g_low, dx2, e2, feed_sums = run_feed(
            valid, x, mixed, g, gains, shift_rows, biases, hidden, out_w, up_w, down_w, proj_w
        )
        y = y.reshape(2, half, seq, width)
        grads, vectors, cls, tokens_grad, y_got = plain_back(
            lengths, logs, gains, feed_sums, cls_sum, left, h1, slope, g_low, e2, dx2, x1, mixed, qkv, x, y,
            down_w, up_w, out_w, qkv_w,
        )
        proj, down, up, out, qkv_grad = grads
        y_own = take(y, tower)
        cls_block = jnp.broadcast_to(cls_row.reshape(1, 1, width), (half, 1, width))
        image_rows = jnp.where(tower == 0, y_own, y_got)
        text_rows = jnp.where(tower == 0, y_got, y_own)
        merged_input = jnp.concatenate([cls_block, image_rows, text_rows], axis=1)
        mine = lax.dynamic_slice_in_dim(vectors[:9], index * (width // dp), width // dp, 1)
        bias_sum, gain_sum, shift_sum = mine[0:5], mine[5:7], mine[7:9]
        ff = up_w.shape[1]
        hidden_sum = lax.dynamic_slice_in_dim(vectors[9:13].reshape(1, ff), index * (ff // dp), ff // dp, 1)
    return (
        merged_input[None], tokens_grad.reshape(tokens.shape), cls.reshape(width), gain_sum[None], shift_sum[None],
        bias_sum[None], hidden_sum, qkv_grad[None], out[None], up[None], down[None], proj[None],
    )


def solution(mesh):
    tower = P("tower", None, None)
    in_specs = (
        P("tower", "dp", None, None), P("dp"), P("dp"), P(), tower, tower, tower, P("tower", None),
        tower, tower, tower, tower, tower, P("tower", "dp", None, None),
    )
    spread = P("tower", None, "dp")
    weight = P("tower", "dp", None)
    out_specs = (
        P("tower", "dp", None, None), P("tower", "dp", None, None), P(), spread, spread, spread, P("tower", "dp"),
        weight, weight, weight, weight, weight,
    )
    return jax.shard_map(
        partial(local, mesh.shape["dp"]), mesh=mesh, in_specs=in_specs, out_specs=out_specs, check_vma=False
    )
```
